32 devices in a mesh: seq: 8 (over z, x), rows: 4 (over y, core).
Axes of the slice: x: 2, y: 2, z: 4, core: 2. Of those that a mesh axis runs over, the one named last changes fastest.
Arguments:
- tokens: bfloat16 [32, 1024, 512], P('rows', 'seq'), may hold values from -6 to 6
- segments: int32 [32, 1024], P('rows'), may hold values from 0 to 7, as said below
- gain_attn: float32 [512], replicated, may hold values from 0.5 to 1.5
- gain_ffn: float32 [512], replicated, may hold values from 0.5 to 1.5
- w_query: bfloat16 [512, 512], replicated, may hold values from -0.25 to 0.25
- w_key: bfloat16 [512, 512], replicated, may hold values from -0.25 to 0.25
- w_value: bfloat16 [512, 512], replicated, may hold values from -0.25 to 0.25
- w_out: bfloat16 [512, 512], replicated, may hold values from -0.75 to 0.75
- w_up: bfloat16 [512, 2048], replicated, may hold values from -0.25 to 0.25
- w_down: bfloat16 [2048, 512], replicated, may hold values from -0.1875 to 0.1875
- cotangent: bfloat16 [32, 1024, 512], P('rows', 'seq'), may hold values from -6 to 6
Outputs:
- output: bfloat16 [32, 1024, 512], P('rows', 'seq')
- d_tokens: bfloat16 [32, 1024, 512], P('rows', 'seq')
- d_gain_attn: float32 [512], replicated
- d_gain_ffn: float32 [512], replicated
- d_w_query: float32 [512, 512], replicated
- d_w_key: float32 [512, 512], replicated
- d_w_value: float32 [512, 512], replicated
- d_w_out: float32 [512, 512], replicated
- d_w_up: float32 [512, 2048], replicated
- d_w_down: float32 [2048, 512], replicated
The draws below stay inside these ranges and needn't reach their ends.
Inputs may be any that keep to these rules, and one draw needn't show every extreme that they name: `segments`: along each row the document numbers start at 0, never fall and rise by at most one from a token to the next; in every aligned group of 8 rows one row is a single document.
All inputs are finite; a program needn't handle non-finite values.
Results may differ from the reference program's by a relative error of at most 0.014.
Values may be sent and summed in bfloat16 or wider, within the bound.
No kernel may reach another device: no remote copies, remote signals or barrier semaphores. Data moves between devices by JAX's collectives and lax.ppermute only.
A program may use at most 256 MiB of HBM per device.

```python
import jax
import jax.numpy as jnp
from jax import lax

HEADS = 8
HEAD = 64
D = 512
FF = 2048
BAND = 30
SEG_TOK = 128
ROWS_DEV = 8
LEN = 1024
ROWS = 32


def draw_segments(key, part):
    key = jax.random.fold_in(key, 7)
    key_hits, key_pick = jax.random.split(key)
    top_doc = LEN // SEG_TOK - 1
    starts = jax.random.randint(key_hits, (ROWS, LEN), 0, 2 * SEG_TOK) == 0
    position = jnp.arange(LEN)[None, :]
    starts = (starts | (position >= LEN - top_doc)) & (position > 0)
    chosen = jax.random.randint(key_pick, (ROWS // ROWS_DEV, 1), 0, ROWS_DEV)
    row_slot = (jnp.arange(ROWS) % ROWS_DEV).reshape(ROWS // ROWS_DEV, ROWS_DEV)
    single = (row_slot == chosen).reshape(ROWS, 1)
    starts = starts & jnp.logical_not(single)
    counted = jnp.cumsum(starts.astype(jnp.int32), axis=1)
    return jnp.minimum(counted, top_doc).astype(jnp.int32)


def level_of(own_key, dims, pieces, low, high):
    factor_of = 1.0
    for dim, shards_of in pieces:
        heights = jax.random.uniform(jax.random.fold_in(jax.random.fold_in(own_key, 6), dim), (shards_of,), jnp.float32, low / len(pieces), high / len(pieces))
        factor_of = factor_of * jnp.repeat(jnp.exp(heights), dims[dim] // shards_of).reshape((-1,) + (1,) * (len(dims) - 1 - dim))
    return factor_of


def bell_draw(rng, extent, width, bound, cuts=(), kind=jnp.bfloat16):
    values = jax.random.normal(rng, extent, jnp.float32) * width
    if len(cuts) > 0:
        values = level_of(rng, extent, cuts, -0.22, 0.18) * values
    return jnp.clip(values, min=-bound, max=bound).astype(kind)


def setup_inputs(seed: int = 0) -> dict:
    arg_keys = jax.random.split(jax.random.key(seed), 12)
    return {
        "tokens": bell_draw(arg_keys[0], (ROWS, LEN, D), 1.0, 6.0, ((0, 4), (1, 8))),
        "segments": draw_segments(jax.random.fold_in(arg_keys[11], 71), 0),
        "gain_attn": jnp.clip(1.0 + 0.1 * jax.random.normal(arg_keys[2], (D,), jnp.float32), 0.5, 1.5),
        "gain_ffn": jnp.clip(1.0 + 0.1 * jax.random.normal(arg_keys[3], (D,), jnp.float32), 0.5, 1.5),
        "w_query": bell_draw(arg_keys[4], (D, D), D ** -0.5, 0.25),
        "w_key": bell_draw(arg_keys[5], (D, D), D ** -0.5, 0.25),
        "w_value": bell_draw(arg_keys[6], (D, D), D ** -0.5, 0.25),
        "w_out": bell_draw(arg_keys[7], (D, D), (D // 8) ** -0.5, 0.75),
        "w_up": bell_draw(arg_keys[8], (D, FF), D ** -0.5, 0.25),
        "w_down": bell_draw(arg_keys[9], (FF, D), (FF // 2) ** -0.5, 0.1875),
        "cotangent": bell_draw(arg_keys[10], (ROWS, LEN, D), 1.0, 6.0, ((0, 4), (1, 8))),
    }


EPSILON = 1e-06
SCALE = 0.125
EXACT_MATMUL = lax.Precision.HIGHEST

@jax.custom_vjp
def low(v):
    return lax.optimization_barrier(v.astype(jnp.bfloat16)).astype(jnp.float32)

@jax.custom_vjp
def low_back(v):
    return v

def low_keep(v):
    return (low(v), None)

def low_pass(kept, grad):
    return (grad,)

def back_keep(v):
    return (v, None)

def back_low(kept, grad):
    return (low(grad),)
low.defvjp(low_keep, low_pass)
low_back.defvjp(back_keep, back_low)

def matmul(matrix_a, matrix_b):
    return jnp.dot(matrix_a, matrix_b, precision=EXACT_MATMUL)

def norm_rows(inputs, gain_vec):
    return inputs * lax.rsqrt(lax.optimization_barrier(jnp.mean(inputs * inputs, -1, keepdims=True)) + EPSILON) * gain_vec

def gelu_tanh(inputs):
    return 0.5 * inputs * (1.0 + jnp.tanh(0.7978845608028654 * (inputs + 0.044715 * inputs * inputs * inputs)))

def phi_elu(inputs):
    return jnp.where(inputs > 0, inputs + 1.0, jnp.exp(jnp.minimum(inputs, 0.0)))

def phi_tanh(inputs):
    return 1.0 + jnp.tanh(inputs)

def band_attention(query, key_pad, value_pad, seg_row, seg_pad):
    block_len = min(512, LEN)
    blocks = LEN // block_len
    offset = jnp.arange(block_len)[:, None] + BAND - jnp.arange(block_len + BAND)[None, :]
    inside = (offset >= 0) & (offset <= BAND)

    def block_fn(block_index):
        first = block_index * block_len
        query_block = lax.dynamic_slice_in_dim(query, first, block_len, 0)
        k_block = lax.dynamic_slice_in_dim(key_pad, first, block_len + BAND, 0)
        v_block = lax.dynamic_slice_in_dim(value_pad, first, block_len + BAND, 0)
        seg_q = lax.dynamic_slice_in_dim(seg_row, first, block_len, 0)
        seg_k = lax.dynamic_slice_in_dim(seg_pad, first, block_len + BAND, 0)
        allowed = inside & (seg_q[:, None] == seg_k[None, :])
        score = low_back(jnp.einsum('ihd,jhd->hij', query_block, k_block, precision=EXACT_MATMUL) * SCALE)
        score = jnp.where(allowed[None], score, -1e+30)
        score_max = lax.optimization_barrier(jnp.max(score, -1, keepdims=True))
        exponent = jnp.exp(score - score_max)
        attn_prob = low(exponent / lax.optimization_barrier(jnp.sum(exponent, -1, keepdims=True)))
        return jnp.einsum('hij,jhd->ihd', attn_prob, v_block, precision=EXACT_MATMUL)
    result = lax.map(jax.checkpoint(block_fn), jnp.arange(blocks, dtype=jnp.int32))
    return result.reshape(LEN, HEADS, HEAD)

def far_field(query, key, value, seg_row, seg_pad):
    block_len = min(512, LEN)
    blocks = LEN // block_len
    causal = jnp.arange(block_len)[:, None] >= jnp.arange(block_len)[None, :]
    feat_q = jnp.stack([phi_elu(query), phi_tanh(query)])
    feat_k = jnp.stack([phi_elu(key), phi_tanh(key)])

    def step_fn(carry, block_index):
        state, grand_total = carry
        first = block_index * block_len
        query_block = lax.dynamic_slice_in_dim(feat_q, first, block_len, 1)
        k_block = lax.dynamic_slice_in_dim(feat_k, first, block_len, 1)
        v_block = lax.dynamic_slice_in_dim(value, first, block_len, 0)
        seg_block = lax.dynamic_slice_in_dim(seg_row, first, block_len, 0)
        before = lax.dynamic_slice_in_dim(seg_pad, first + BAND - 1, 1, 0)[0]
        carry_applied_state = (seg_block == before).astype(query.dtype)
        same_doc = (causal & (seg_block[:, None] == seg_block[None, :])).astype(query.dtype)
        far_weight = jnp.einsum('mihd,mjhd->mhij', query_block, k_block, precision=EXACT_MATMUL) * same_doc
        numerator = jnp.einsum('mhij,jhe->mihe', far_weight, v_block, precision=EXACT_MATMUL)
        numerator = numerator + carry_applied_state[None, :, None, None] * jnp.einsum('mihd,mhde->mihe', query_block, state, precision=EXACT_MATMUL)
        normalizer_sum = jnp.transpose(lax.optimization_barrier(jnp.sum(far_weight, -1)), (0, 2, 1))
        normalizer_sum = normalizer_sum + carry_applied_state[None, :, None] * jnp.einsum('xzcv,xcv->xzc', query_block, grand_total, precision=EXACT_MATMUL)
        far_out = lax.optimization_barrier(jnp.sum(numerator / normalizer_sum[..., None], 0))
        last_seg = seg_block[block_len - 1]
        tail_mask = (seg_block == last_seg).astype(query.dtype)
        carry_on = (before == last_seg).astype(query.dtype)
        tail_k = k_block * tail_mask[None, :, None, None]
        state = jnp.einsum('mjhd,jhe->mhde', tail_k, v_block, precision=EXACT_MATMUL) + carry_on * state
        grand_total = lax.optimization_barrier(jnp.sum(tail_k, 1)) + carry_on * grand_total
        return ((state, grand_total), far_out)
    start_state = (jnp.zeros((2, HEADS, HEAD, HEAD), jnp.float32), jnp.zeros((2, HEADS, HEAD), jnp.float32))
    _, result = lax.scan(jax.checkpoint(step_fn), start_state, jnp.arange(blocks, dtype=jnp.int32))
    return result.reshape(LEN, HEADS, HEAD)

def layer(inputs, gain_attn, gain_ffn, w_query, w_key, w_value, w_out, w_up, w_down, seg_row):
    seg_pad = jnp.concatenate([jnp.full((BAND,), -1, jnp.int32), seg_row.astype(jnp.int32)])
    hidden = low(norm_rows(inputs, gain_attn))
    query = low_back(low(matmul(hidden, w_query))).reshape(LEN, HEADS, HEAD)
    key = low_back(low(matmul(hidden, w_key))).reshape(LEN, HEADS, HEAD)
    value = low_back(low(matmul(hidden, w_value))).reshape(LEN, HEADS, HEAD)
    zero_rim = jnp.zeros((BAND, HEADS, HEAD), inputs.dtype)
    key_pad = jnp.concatenate([zero_rim, key], 0)
    value_pad = jnp.concatenate([zero_rim, value], 0)
    near_out = band_attention(query, key_pad, value_pad, seg_row, seg_pad)
    far_out = far_field(query, key, value, seg_row, seg_pad)
    attended = low_back(low((near_out + far_out).reshape(LEN, D)))
    residual = inputs + low_back(matmul(attended, w_out))
    hidden_two = low(norm_rows(residual, gain_ffn))
    activated = low(gelu_tanh(low_back(matmul(hidden_two, w_up))))
    return residual + matmul(activated, w_down)

def reference(tokens, segments, gain_attn, gain_ffn, w_query, w_key, w_value, w_out, w_up, w_down, cotangent):
    params = (gain_attn.astype(jnp.float32), gain_ffn.astype(jnp.float32), w_query.astype(jnp.float32), w_key.astype(jnp.float32), w_value.astype(jnp.float32), w_out.astype(jnp.float32), w_up.astype(jnp.float32), w_down.astype(jnp.float32))

    def one_row(accum, row_data):
        row_in, seg_row, row_grad = row_data

        def row_layer(inputs, ga, gf, wq, wk, wv, wo, wu, wd):
            return layer(inputs, ga, gf, wq, wk, wv, wo, wu, wd, seg_row)
        result, pull = jax.vjp(row_layer, row_in.astype(jnp.float32), params[0], params[1], params[2], params[3], params[4], params[5], params[6], params[7])
        grads = pull(row_grad.astype(jnp.float32))
        new_accum = jax.tree.map(lambda left, right: left + right, accum, tuple(grads[1:]))
        return (new_accum, (result.astype(jnp.bfloat16), grads[0].astype(jnp.bfloat16)))
    start_accum = jax.tree.map(jnp.zeros_like, params)
    accum, (outputs, d_inputs) = lax.scan(one_row, start_accum, (tokens, segments, cotangent))
    return (outputs, d_inputs, accum[0], accum[1], accum[2], accum[3], accum[4], accum[5], accum[6], accum[7])
```

```python
import functools

import jax
import jax.numpy as jnp
from jax import lax
from jax.experimental import pallas as pl
from jax.experimental.pallas import tpu as pltpu
from jax.sharding import PartitionSpec as P

HEADS = 8
HEAD = 64
BAND = 30
EPSILON = 1e-06
SCALE = 0.125
CHUNK = 128
BLOCK = 256
PAIRS = HEADS // 2
NEG = -1e30
GELU_A = 0.7978845608028654
GELU_B = 0.044715
F32 = jnp.float32
BF16 = jnp.bfloat16
VMEM_LIMIT = 56 * 1024 * 1024


def nn(a, b):
    return lax.dot_general(a, b, (((1,), (0,)), ((), ())), preferred_element_type=F32)


def nt(a, b):
    return lax.dot_general(a, b, (((1,), (1,)), ((), ())), preferred_element_type=F32)


def tn(a, b):
    return lax.dot_general(a, b, (((0,), (0,)), ((), ())), preferred_element_type=F32)


def low_lanes(shape):
    return lax.broadcasted_iota(jnp.int32, shape, len(shape) - 1) < HEAD


def split_heads(pair):
    low = low_lanes(pair.shape)
    zero = jnp.zeros_like(pair)
    return jnp.concatenate([jnp.where(low, pair, zero), jnp.where(low, zero, pair)], 0)


def with_ones(pair):
    low = low_lanes(pair.shape)
    one = jnp.ones_like(pair)
    return jnp.where(low, pair, one), jnp.where(low, one, pair)


def pick(top, bottom):
    return jnp.where(low_lanes(top.shape), top, bottom)


def elu_one(t):
    return jnp.where(t > 0, t + 1.0, jnp.exp(jnp.minimum(t, 0.0)))


def chunk_masks(segc_ref, segr_ref, chunk):
    seg_q = segc_ref[chunk + 1]
    seg_prev = segr_ref[chunk]
    seg_own = segr_ref[chunk + 1]
    row = lax.broadcasted_iota(jnp.int32, (CHUNK, CHUNK), 0)
    col = lax.broadcasted_iota(jnp.int32, (CHUNK, CHUNK), 1)
    same_own = seg_q == seg_own
    same_prev = seg_q == seg_prev
    gap = row - col
    far = same_own & (gap >= 0)
    band_own = far & (gap <= BAND)
    band_prev = same_prev & (gap + CHUNK <= BAND)
    band = jnp.concatenate([band_prev, band_own], 1)
    before = seg_prev[:, CHUNK - 1 :]
    last = seg_own[:, CHUNK - 1 :]
    carry = seg_q == before
    tail = seg_q == last
    keep = (before == last).astype(F32)
    return (
        jnp.concatenate([band, band], 0),
        jnp.concatenate([far, far], 0),
        carry,
        tail,
        keep,
    )


def forward_kernel(
    x_ref, segc_ref, segr_ref, ga_ref, gf_ref, wq_ref, wk_ref, wv_ref, wo_ref, wu_ref, wd_ref,
    s0_ref, k0_ref, v0_ref,
    out_ref, x1_ref, a_ref, q_ref, k_ref, v_ref, lse_ref, far1_ref, far2_ref, iz1_ref, iz2_ref,
    states_ref, s_end_ref,
    s_ref, kp_ref, vp_ref,
):
    step = pl.program_id(0)

    @pl.when(step == 0)
    def _():
        s_ref[...] = s0_ref[...]
        kp_ref[...] = k0_ref[...]
        vp_ref[...] = v0_ref[...]

    x = x_ref[...].astype(F32)
    inv = lax.rsqrt(jnp.mean(x * x, -1, keepdims=True) + EPSILON)
    hidden = (x * inv * ga_ref[...]).astype(BF16)
    q_ref[...] = nn(hidden, wq_ref[...]).astype(BF16)
    k_ref[...] = nn(hidden, wk_ref[...]).astype(BF16)
    v_ref[...] = nn(hidden, wv_ref[...]).astype(BF16)
    far_refs = (far1_ref, far2_ref)
    iz_refs = (iz1_ref, iz2_ref)
    lane = lax.broadcasted_iota(jnp.int32, (CHUNK, CHUNK), 1)
    row_low = lax.broadcasted_iota(jnp.int32, (CHUNK, CHUNK), 0) < HEAD
    for sub in range(BLOCK // CHUNK):
        rows = slice(sub * CHUNK, (sub + 1) * CHUNK)
        chunk = step * (BLOCK // CHUNK) + sub
        band, far_mask, carry, tail, keep = chunk_masks(segc_ref, segr_ref, chunk)
        carry = carry.astype(BF16)
        tail = tail.astype(BF16)
        lse_all = jnp.zeros((CHUNK, CHUNK), F32)
        for p in range(PAIRS):
            lanes = slice(p * 128, (p + 1) * 128)
            qp = q_ref[rows, lanes]
            kp = k_ref[rows, lanes]
            vp = v_ref[rows, lanes]
            k_ext = jnp.concatenate([kp_ref[:, lanes], kp], 0)
            v_ext = jnp.concatenate([vp_ref[:, lanes], vp], 0)
            score = nt(split_heads(qp * SCALE), k_ext)
            score = jnp.where(band, score, NEG)
            top = jnp.max(score, -1, keepdims=True)
            expo = jnp.exp(score - top).astype(BF16)
            one0, one1 = with_ones(v_ext)
            acc0 = nn(expo[:CHUNK], one0)
            acc1 = nn(expo[CHUNK:], one1)
            total = pltpu.roll(pick(acc1, acc0), HEAD, 1)
            attended = pick(acc0, acc1) / total
            log_total = jnp.log(total)
            lse_all = jnp.where(lane == 2 * p, top[:CHUNK] + log_total[:, :1], lse_all)
            lse_all = jnp.where(
                lane == 2 * p + 1, top[CHUNK:] + log_total[:, HEAD : HEAD + 1], lse_all
            )
            qf = qp.astype(F32)
            kf = kp.astype(F32)
            own0, own1 = one0[CHUNK:], one1[CHUNK:]
            own01 = jnp.concatenate([own0, own1], 1)
            for m in range(2):
                if m == 0:
                    fq, fk = elu_one(qf).astype(BF16), elu_one(kf).astype(BF16)
                else:
                    fq, fk = (1.0 + jnp.tanh(qf)).astype(BF16), (1.0 + jnp.tanh(kf)).astype(BF16)
                state = s_ref[2 * p + m]
                state_low = state.astype(BF16)
                states_ref[sub, 2 * p + m] = state_low
                fq2 = split_heads(fq)
                weight = jnp.where(far_mask, nt(fq2, fk), 0.0).astype(BF16)
                fq2 = split_heads(fq * carry)
                acc0 = nn(weight[:CHUNK], own0) + nn(fq2[:CHUNK], state_low)
                acc1 = nn(weight[CHUNK:], own1) + nn(fq2[CHUNK:], state_low)
                inv_z = 1.0 / pltpu.roll(pick(acc1, acc0), HEAD, 1)
                far = pick(acc0, acc1) * inv_z
                attended = attended + far
                far_refs[m][rows, lanes] = far.astype(BF16)
                iz_refs[m][rows, lanes] = inv_z.astype(BF16)
                update = tn(fk * tail, own01)
                s_ref[2 * p + m] = keep * state + jnp.where(
                    row_low, update[:, :CHUNK], update[:, CHUNK:]
                )
            a_ref[rows, lanes] = attended.astype(BF16)
        lse_ref[rows] = lse_all
        kp_ref[...] = k_ref[rows]
        vp_ref[...] = v_ref[rows]
    s_end_ref[...] = s_ref[...]
    x1 = x + nn(a_ref[...], wo_ref[...])
    x1_ref[...] = x1
    inv = lax.rsqrt(jnp.mean(x1 * x1, -1, keepdims=True) + EPSILON)
    hidden = (x1 * inv * gf_ref[...]).astype(BF16)
    total = x1
    width = 512
    for f in range(wu_ref.shape[1] // width):
        cols = slice(f * width, (f + 1) * width)
        up = nn(hidden, wu_ref[:, cols])
        act = 0.5 * up * (1.0 + jnp.tanh(GELU_A * (up + GELU_B * up * up * up)))
        total = total + nn(act.astype(BF16), wd_ref[cols])
    out_ref[...] = total.astype(BF16)


def norm_backward(x, gain, grad):
    inv = lax.rsqrt(jnp.mean(x * x, -1, keepdims=True) + EPSILON)
    unit = x * inv
    scaled = grad * gain
    d_gain = jnp.sum(grad * unit, 0, keepdims=True)
    return inv * (scaled - unit * jnp.mean(unit * scaled, -1, keepdims=True)), d_gain


def ffn_backward_kernel(
    dy_ref, x1_ref, a_ref, gf_ref, wo_ref, wu_ref, wd_ref,
    dx1_ref, da_ref, dwd_ref, dwu_ref, dwo_ref, dg_ref,
    dwd_acc, dwu_acc, dwo_acc, dg_acc,
):
    step = pl.program_id(0)

    @pl.when(step == 0)
    def _():
        dwd_acc[...] = jnp.zeros_like(dwd_acc)
        dwu_acc[...] = jnp.zeros_like(dwu_acc)
        dwo_acc[...] = jnp.zeros_like(dwo_acc)
        dg_acc[...] = jnp.zeros_like(dg_acc)

    dy = dy_ref[...]
    x1 = x1_ref[...]
    gain = gf_ref[...]
    inv = lax.rsqrt(jnp.mean(x1 * x1, -1, keepdims=True) + EPSILON)
    hidden = (x1 * inv * gain).astype(BF16)
    d_hidden = jnp.zeros(x1.shape, F32)
    width = 512
    for f in range(wu_ref.shape[1] // width):
        cols = slice(f * width, (f + 1) * width)
        up = nn(hidden, wu_ref[:, cols])
        square = up * up
        tanh = jnp.tanh(GELU_A * up * (1.0 + GELU_B * square))
        half = 0.5 * (1.0 + tanh)
        act = (up * half).astype(BF16)
        slope = half + 0.5 * up * (1.0 - tanh * tanh) * (
            GELU_A + (3.0 * GELU_A * GELU_B) * square
        )
        d_up = (slope * nt(dy, wd_ref[cols])).astype(BF16)
        dwd_acc[cols] += tn(act, dy)
        dwu_acc[:, cols] += tn(hidden, d_up)
        d_hidden = d_hidden + nt(d_up, wu_ref[:, cols])
    d_norm, d_gain = norm_backward(x1, gain, d_hidden)
    dx1 = dy.astype(F32) + d_norm
    dg_acc[...] += jnp.broadcast_to(d_gain, dg_acc.shape)
    dx1_ref[...] = dx1
    d_branch = dx1.astype(BF16)
    dwo_acc[...] += tn(a_ref[...], d_branch)
    da_ref[...] = nt(d_branch, wo_ref[...]).astype(BF16)

    @pl.when(step == pl.num_programs(0) - 1)
    def _():
        dwd_ref[...] = dwd_acc[...].astype(BF16)
        dwu_ref[...] = dwu_acc[...].astype(BF16)
        dwo_ref[...] = dwo_acc[...].astype(BF16)
        dg_ref[...] = dg_acc[...]


def attention_backward_kernel(
    x_ref, dx1_ref, da_ref, q_ref, k_ref, v_ref, kprev_ref, vprev_ref,
    lse_ref, far1_ref, far2_ref, iz1_ref, iz2_ref,
    states_ref, segc_ref, segr_ref, ga_ref, wq_ref, wk_ref, wv_ref, r0_ref, dk0_ref, dv0_ref,
    dx_ref, dwq_ref, dwk_ref, dwv_ref, dg_ref, r_end_ref, dk_end_ref, dv_end_ref,
    r_ref, dkc_ref, dvc_ref, dq_ref, dk_ref, dv_ref, dwq_acc, dwk_acc, dwv_acc, dg_acc,
):
    step = pl.program_id(0)
    block = pl.num_programs(0) - 1 - step

    @pl.when(step == 0)
    def _():
        r_ref[...] = r0_ref[...]
        dkc_ref[...] = dk0_ref[...]
        dvc_ref[...] = dv0_ref[...]
        dwq_acc[...] = jnp.zeros_like(dwq_acc)
        dwk_acc[...] = jnp.zeros_like(dwk_acc)
        dwv_acc[...] = jnp.zeros_like(dwv_acc)
        dg_acc[...] = jnp.zeros_like(dg_acc)

    far_refs = (far1_ref, far2_ref)
    iz_refs = (iz1_ref, iz2_ref)
    row_low = lax.broadcasted_iota(jnp.int32, (CHUNK, CHUNK), 0) < HEAD
    lane_low = lax.broadcasted_iota(jnp.int32, (CHUNK, CHUNK), 1) < HEAD
    diagonal = row_low == lane_low
    swap = jnp.where(diagonal, 0.0, -1.0 / HEAD).astype(BF16)
    for sub in reversed(range(BLOCK // CHUNK)):
        rows = slice(sub * CHUNK, (sub + 1) * CHUNK)
        chunk = block * (BLOCK // CHUNK) + sub
        band, far_mask, carry, tail, keep = chunk_masks(segc_ref, segr_ref, chunk)
        carry = carry.astype(BF16)
        tail = tail.astype(BF16)
        lse_all = lse_ref[rows]
        for p in range(PAIRS):
            lanes = slice(p * 128, (p + 1) * 128)
            qp = q_ref[rows, lanes]
            kp = k_ref[rows, lanes]
            vp = v_ref[rows, lanes]
            da = da_ref[rows, lanes]
            if sub == 0:
                k_prev, v_prev = kprev_ref[:, lanes], vprev_ref[:, lanes]
            else:
                before = slice((sub - 1) * CHUNK, sub * CHUNK)
                k_prev, v_prev = k_ref[before, lanes], v_ref[before, lanes]
            k_ext = jnp.concatenate([k_prev, kp], 0)
            v_ext = jnp.concatenate([v_prev, vp], 0)
            q2 = split_heads(qp * SCALE)
            lse = jnp.concatenate(
                [lse_all[:, 2 * p : 2 * p + 1], lse_all[:, 2 * p + 1 : 2 * p + 2]], 0
            )
            prob = jnp.exp(jnp.where(band, nt(q2, k_ext) - lse, NEG))
            da2 = split_heads(da)
            d_prob = nt(da2, v_ext)
            delta = jnp.sum(prob * d_prob, -1, keepdims=True)
            d_score = (prob * (d_prob - delta)).astype(BF16)
            dq2 = nn(d_score, k_ext)
            dq = SCALE * pick(dq2[:CHUNK], dq2[CHUNK:])
            dk_ext = tn(d_score, q2)
            dv_ext = tn(prob.astype(BF16), da2)
            dk = dk_ext[CHUNK:] + dkc_ref[:, lanes]
            dv = dv_ext[CHUNK:] + dvc_ref[:, lanes]
            dkc_ref[:, lanes] = dk_ext[:CHUNK]
            dvc_ref[:, lanes] = dv_ext[:CHUNK]
            qf = qp.astype(F32)
            kf = kp.astype(F32)
            daf = da.astype(F32)
            one0, one1 = with_ones(vp)
            for m in range(2):
                if m == 0:
                    exp_q = jnp.exp(jnp.minimum(qf, 0.0))
                    exp_k = jnp.exp(jnp.minimum(kf, 0.0))
                    fq = jnp.where(qf > 0, qf + 1.0, exp_q).astype(BF16)
                    fk = jnp.where(kf > 0, kf + 1.0, exp_k).astype(BF16)
                    slope_q, slope_k = exp_q, exp_k
                else:
                    tanh_q, tanh_k = jnp.tanh(qf), jnp.tanh(kf)
                    fq, fk = (1.0 + tanh_q).astype(BF16), (1.0 + tanh_k).astype(BF16)
                    slope_q, slope_k = 1.0 - tanh_q * tanh_q, 1.0 - tanh_k * tanh_k
                state = states_ref[sub, 2 * p + m]
                back = r_ref[2 * p + m]
                back_low = back.astype(BF16)
                d_num = daf * iz_refs[m][rows, lanes].astype(F32)
                d_num_low = d_num.astype(BF16)
                d_den = nn((d_num * far_refs[m][rows, lanes].astype(F32)).astype(BF16), swap)
                d_den = d_den.astype(BF16)
                grad0 = pick(d_num_low, d_den)
                grad1 = pick(d_den, d_num_low)
                fq2 = split_heads(fq)
                weight = jnp.where(far_mask, nt(fq2, fk), 0.0).astype(BF16)
                d_weight = jnp.concatenate([nt(grad0, one0), nt(grad1, one1)], 0)
                d_weight = jnp.where(far_mask, d_weight, 0.0).astype(BF16)
                grad01 = jnp.concatenate([grad0, grad1], 0)
                carry2 = jnp.concatenate([carry, carry], 0)
                dfq2 = nn(d_weight, fk) + nt(grad01 * carry2, state)
                dfq = pick(dfq2[:CHUNK], dfq2[CHUNK:])
                dfk = tn(d_weight, fq2) + pick(
                    nt(one0 * tail, back_low), nt(one1 * tail, back_low)
                )
                dv = dv + tn(weight, split_heads(d_num_low))
                dv = dv + nn(fk * tail, jnp.where(diagonal, back_low, jnp.zeros_like(back_low)))
                dq = dq + slope_q * dfq
                dk = dk + slope_k * dfk
                update = tn(fq * carry, jnp.concatenate([grad0, grad1], 1))
                r_ref[2 * p + m] = keep * back + jnp.where(
                    row_low, update[:, :CHUNK], update[:, CHUNK:]
                )
            dq_ref[rows, lanes] = dq.astype(BF16)
            dk_ref[rows, lanes] = dk.astype(BF16)
            dv_ref[rows, lanes] = dv.astype(BF16)
    r_end_ref[...] = r_ref[...]
    dk_end_ref[...] = dkc_ref[...]
    dv_end_ref[...] = dvc_ref[...]
    x = x_ref[...].astype(F32)
    gain = ga_ref[...]
    inv = lax.rsqrt(jnp.mean(x * x, -1, keepdims=True) + EPSILON)
    hidden = (x * inv * gain).astype(BF16)
    dwq_acc[...] += tn(hidden, dq_ref[...])
    dwk_acc[...] += tn(hidden, dk_ref[...])
    dwv_acc[...] += tn(hidden, dv_ref[...])
    d_hidden = (
        nt(dq_ref[...], wq_ref[...])
        + nt(dk_ref[...], wk_ref[...])
        + nt(dv_ref[...], wv_ref[...])
    )
    d_norm, d_gain = norm_backward(x, gain, d_hidden)
    dg_acc[...] += jnp.broadcast_to(d_gain, dg_acc.shape)
    dx_ref[...] = (dx1_ref[...] + d_norm).astype(BF16)

    @pl.when(step == pl.num_programs(0) - 1)
    def _():
        dwq_ref[...] = dwq_acc[...].astype(BF16)
        dwk_ref[...] = dwk_acc[...].astype(BF16)
        dwv_ref[...] = dwv_acc[...].astype(BF16)
        dg_ref[...] = dg_acc[...]


def whole(shape):
    return pl.BlockSpec(shape, lambda i: (0,) * len(shape))


def tokens_of(width, index=lambda i: i):
    return pl.BlockSpec((BLOCK, width), lambda i: (index(i), 0))


def params():
    return pltpu.CompilerParams(
        vmem_limit_bytes=VMEM_LIMIT, dimension_semantics=("arbitrary",)
    )


def sds(shape, dtype):
    return jax.ShapeDtypeStruct(shape, dtype)


def run_forward(x, segc, segr, gain_attn, gain_ffn, wq, wk, wv, wo, wu, wd, s0, k0, v0):
    length, dim = x.shape
    ff = wu.shape[1]
    chunks = length // CHUNK
    steps = length // BLOCK
    per = BLOCK // CHUNK
    row = tokens_of(dim)
    state_shape = (HEADS, CHUNK, CHUNK)
    return pl.pallas_call(
        forward_kernel,
        grid=(steps,),
        in_specs=[
            row, whole(segc.shape), whole(segr.shape), whole((1, dim)), whole((1, dim)),
            whole((dim, dim)), whole((dim, dim)), whole((dim, dim)), whole((dim, dim)),
            whole((dim, ff)), whole((ff, dim)),
            whole(state_shape), whole((CHUNK, dim)), whole((CHUNK, dim)),
        ],
        out_specs=[
            row, row, row, row, row, row, tokens_of(CHUNK), row, row, row, row,
            pl.BlockSpec((per,) + state_shape, lambda i: (i, 0, 0, 0)),
            whole(state_shape),
        ],
        out_shape=[
            sds((length, dim), BF16), sds((length, dim), F32), sds((length, dim), BF16),
            sds((length, dim), BF16), sds((length, dim), BF16), sds((length, dim), BF16),
            sds((length, CHUNK), F32),
            sds((length, dim), BF16), sds((length, dim), BF16),
            sds((length, dim), BF16), sds((length, dim), BF16),
            sds((chunks,) + state_shape, BF16), sds(state_shape, F32),
        ],
        scratch_shapes=[
            pltpu.VMEM(state_shape, F32),
            pltpu.VMEM((CHUNK, dim), BF16),
            pltpu.VMEM((CHUNK, dim), BF16),
        ],
        compiler_params=params(),
        name="layer_forward",
    )(x, segc, segr, gain_attn, gain_ffn, wq, wk, wv, wo, wu, wd, s0, k0, v0)


def run_ffn_backward(dy, x1, a, gain_ffn, wo, wu, wd):
    length, dim = dy.shape
    ff = wu.shape[1]
    row = tokens_of(dim)
    return pl.pallas_call(
        ffn_backward_kernel,
        grid=(length // BLOCK,),
        in_specs=[
            row, row, row, whole((1, dim)), whole((dim, dim)), whole((dim, ff)), whole((ff, dim)),
        ],
        out_specs=[
            row, row, whole((ff, dim)), whole((dim, ff)), whole((dim, dim)), whole((8, dim)),
        ],
        out_shape=[
            sds((length, dim), F32), sds((length, dim), BF16),
            sds((ff, dim), BF16), sds((dim, ff), BF16), sds((dim, dim), BF16), sds((8, dim), F32),
        ],
        scratch_shapes=[
            pltpu.VMEM((ff, dim), F32), pltpu.VMEM((dim, ff), F32),
            pltpu.VMEM((dim, dim), F32), pltpu.VMEM((8, dim), F32),
        ],
        compiler_params=params(),
        name="ffn_backward",
    )(dy, x1, a, gain_ffn, wo, wu, wd)


def run_attention_backward(
    x, dx1, da, q, k, v, k0, v0, lse, far1, far2, iz1, iz2, states, segc, segr, gain_attn,
    wq, wk, wv, r0, dk0, dv0,
):
    length, dim = x.shape
    steps = length // BLOCK
    per = BLOCK // CHUNK
    state_shape = (HEADS, CHUNK, CHUNK)
    k_prev = jnp.concatenate([k0, k[: length - CHUNK]], 0)
    v_prev = jnp.concatenate([v0, v[: length - CHUNK]], 0)
    back = lambda i: steps - 1 - i
    row = tokens_of(dim, back)
    prev = pl.BlockSpec((CHUNK, dim), lambda i: (back(i) * per, 0))
    return pl.pallas_call(
        attention_backward_kernel,
        grid=(steps,),
        in_specs=[
            row, row, row, row, row, row, prev, prev, tokens_of(CHUNK, back),
            row, row, row, row,
            pl.BlockSpec((per,) + state_shape, lambda i: (back(i), 0, 0, 0)),
            whole(segc.shape), whole(segr.shape), whole((1, dim)),
            whole((dim, dim)), whole((dim, dim)), whole((dim, dim)),
            whole(state_shape), whole((CHUNK, dim)), whole((CHUNK, dim)),
        ],
        out_specs=[
            row, whole((dim, dim)), whole((dim, dim)), whole((dim, dim)), whole((8, dim)),
            whole(state_shape), whole((CHUNK, dim)), whole((CHUNK, dim)),
        ],
        out_shape=[
            sds((length, dim), BF16),
            sds((dim, dim), BF16), sds((dim, dim), BF16), sds((dim, dim), BF16), sds((8, dim), F32),
            sds(state_shape, F32), sds((CHUNK, dim), F32), sds((CHUNK, dim), F32),
        ],
        scratch_shapes=[
            pltpu.VMEM(state_shape, F32),
            pltpu.VMEM((CHUNK, dim), F32), pltpu.VMEM((CHUNK, dim), F32),
            pltpu.VMEM((BLOCK, dim), BF16), pltpu.VMEM((BLOCK, dim), BF16),
            pltpu.VMEM((BLOCK, dim), BF16),
            pltpu.VMEM((dim, dim), F32), pltpu.VMEM((dim, dim), F32), pltpu.VMEM((dim, dim), F32),
            pltpu.VMEM((8, dim), F32),
        ],
        compiler_params=params(),
        name="attention_backward",
    )(
        x, dx1, da, q, k, v, k_prev, v_prev, lse, far1, far2, iz1, iz2, states, segc, segr,
        gain_attn, wq, wk, wv, r0, dk0, dv0,
    )


def segment_views(seg_ext):
    chunks = seg_ext.shape[0] // CHUNK
    return seg_ext.reshape(chunks, CHUNK, 1), seg_ext.reshape(chunks, 1, CHUNK)


def local(
    tokens, segments, gain_attn, gain_ffn, w_query, w_key, w_value, w_out, w_up, w_down, cotangent
):
    row_count, shard_len, dim = tokens.shape
    seq_count = lax.axis_size("seq")
    parts = seq_count // row_count
    groups = [[g * row_count + r for r in range(row_count)] for g in range(parts)]
    length = row_count * shard_len
    index = lax.axis_index("seq")
    my_row = index % row_count
    my_part = index // row_count

    def trade(array):
        return lax.all_to_all(
            array.reshape(row_count, shard_len, dim), "seq", 0, 0, axis_index_groups=groups
        )

    def shifted(arrays, by):
        pairs = [
            (i, i + by * row_count)
            for i in range(seq_count)
            if 0 <= i + by * row_count < seq_count
        ]
        return lax.ppermute(arrays, "seq", pairs)

    seg_row = lax.dynamic_index_in_dim(segments, my_row, 0, False)
    seg_row = jnp.concatenate([jnp.full((CHUNK,), -1, jnp.int32), seg_row])
    seg_ext = lax.dynamic_slice_in_dim(seg_row, my_part * length, length + CHUNK, 0)
    segc, segr = segment_views(seg_ext)
    ga, gf = gain_attn.reshape(1, dim), gain_ffn.reshape(1, dim)

    x = trade(tokens).reshape(length, dim)
    dy = trade(cotangent).reshape(length, dim)
    state_zero = jnp.zeros((HEADS, CHUNK, CHUNK), F32)
    rim_zero = jnp.zeros((CHUNK, dim), BF16)
    entry = (state_zero, rim_zero, rim_zero)
    for turn in range(parts):
        (out, x1, a, q, k, v, lse, far1, far2, iz1, iz2, states, s_end) = run_forward(
            x, segc, segr, ga, gf, w_query, w_key, w_value, w_out, w_up, w_down, *entry
        )
        if turn < parts - 1:
            entry = shifted((s_end, k[length - CHUNK :], v[length - CHUNK :]), 1)
    output = trade(out)
    dx1, da, dwd, dwu, dwo, dgf = run_ffn_backward(dy, x1, a, gf, w_out, w_up, w_down)
    axes = ("seq", "rows")
    dwd, dwu, dwo = lax.psum((dwd, dwu, dwo), axes)
    grad_zero = jnp.zeros((CHUNK, dim), F32)
    back = (state_zero, grad_zero, grad_zero)
    for turn in range(parts):
        dx, dwq, dwk, dwv, dga, r_end, dk_end, dv_end = run_attention_backward(
            x, dx1, da, q, k, v, entry[1], entry[2], lse, far1, far2, iz1, iz2, states,
            segc, segr, ga, w_query, w_key, w_value, *back,
        )
        if turn < parts - 1:
            back = shifted((r_end, dk_end, dv_end), -1)
    d_tokens = trade(dx)
    dwq, dwk, dwv, dga, dgf = lax.psum((dwq, dwk, dwv, dga[0].astype(BF16), dgf[0].astype(BF16)), axes)
    wide = lambda array: array.astype(F32)
    return (
        output, d_tokens, wide(dga), wide(dgf),
        wide(dwq), wide(dwk), wide(dwv), wide(dwo), wide(dwu), wide(dwd),
    )


def solution(mesh):
    act = P("rows", "seq", None)
    return jax.shard_map(
        local,
        mesh=mesh,
        in_specs=(act, P("rows", None)) + (P(),) * 8 + (act,),
        out_specs=(act, act) + (P(),) * 8,
        check_vma=False,
    )
```

```python
import functools

import jax
import jax.numpy as jnp
from jax import lax
from jax.experimental import pallas as pl
from jax.experimental.pallas import tpu as pltpu
from jax.sharding import PartitionSpec as P

HEADS = 8
HEAD = 64
BAND = 30
EPSILON = 1e-06
SCALE = 0.125
CHUNK = 128
BLOCK = 256
PAIRS = HEADS // 2
NEG = -1e30
STEP_PAIRS = 2
GAIN_ROWS = 64
CALLS = ((0, 3), (3, 1))
STEPS_BEFORE = (1, 2)
GELU_A = 0.7978845608028654
GELU_B = 0.044715
F32 = jnp.float32
BF16 = jnp.bfloat16
VMEM_LIMIT = 56 * 1024 * 1024


def nn(a, b):
    return lax.dot_general(a, b, (((1,), (0,)), ((), ())), preferred_element_type=F32)


def nt(a, b):
    return lax.dot_general(a, b, (((1,), (1,)), ((), ())), preferred_element_type=F32)


def tn(a, b):
    return lax.dot_general(a, b, (((0,), (0,)), ((), ())), preferred_element_type=F32)


def low_lanes(shape):
    return lax.broadcasted_iota(jnp.int32, shape, len(shape) - 1) < HEAD


def split_heads(pair):
    low = low_lanes(pair.shape)
    zero = jnp.zeros_like(pair)
    return jnp.concatenate([jnp.where(low, pair, zero), jnp.where(low, zero, pair)], 0)


def pick(both):
    half = both.shape[0] // 2
    return jnp.where(low_lanes((half, both.shape[1])), both[:half], both[half:])


def over_lanes(column):
    half = column.shape[0] // 2
    return jnp.where(low_lanes((half, 2 * HEAD)), column[:half], column[half:])


def in_step(bodies):
    bodies = list(bodies)
    while bodies:
        bodies = [body for body in bodies if next(body, True) is None]


def features(t):
    expo = jnp.exp(jnp.minimum(t, 0.0))
    tanh = jnp.tanh(t)
    return (jnp.where(t > 0, t + 1.0, expo), 1.0 + tanh), (expo, 1.0 - tanh * tanh)


def head_mask(lanes):
    row = lax.broadcasted_iota(jnp.int32, (4 * HEAD, lanes), 0)
    lane = lax.broadcasted_iota(jnp.int32, (4 * HEAD, lanes), 1)
    head = (row // HEAD) % 2
    same = (lane < 2 * HEAD) & (lane // HEAD == head)
    return same | (lane == 2 * HEAD + row // HEAD)


def chunk_masks(seg_ref, place_ref, chunk):
    chunk = place_ref[1] + chunk

    def stretch(at):
        rows = seg_ref[:, pl.ds(pl.multiple_of(at * CHUNK, CHUNK), CHUNK)]
        mine = lax.broadcasted_iota(jnp.int32, rows.shape, 0) == place_ref[0]
        return jnp.max(jnp.where(mine, rows, -1), 0, keepdims=True).astype(F32)

    seg_own = stretch(chunk)
    seg_prev = jnp.where(chunk == 0, -1.0, stretch(jnp.maximum(chunk - 1, 0)))
    seg_q = jnp.broadcast_to(seg_own, (CHUNK, CHUNK)).T
    row = lax.broadcasted_iota(jnp.int32, (CHUNK, CHUNK), 0)
    col = lax.broadcasted_iota(jnp.int32, (CHUNK, CHUNK), 1)
    gap = row - col
    far = (seg_q == seg_own) & (gap >= 0)
    band_own = far & (gap <= BAND)
    band_prev = (seg_q == seg_prev) & (gap + CHUNK <= BAND)
    band = jnp.concatenate([band_prev, band_own], 1)
    before = seg_prev[:, CHUNK - 1 :]
    last = seg_own[:, CHUNK - 1 :]
    carry = (seg_q[:, :1] == before).astype(F32)
    tail = (seg_own == last).astype(BF16)
    keep = (before == last).astype(F32)
    return jnp.concatenate([band, band], 0), jnp.concatenate([far, far], 0), carry, tail, keep


def start_with(refs, entry_refs):
    for n, ref in enumerate(refs):
        ref[...] = entry_refs[n][...] if entry_refs else jnp.zeros_like(ref)


def forward_kernel(entries, *refs):
    (x_ref, seg_ref, place_ref, ga_ref, gf_ref, wq_ref, wk_ref, wv_ref, wo_ref, wu_ref, wd_ref,
     *refs) = refs
    entry_refs, refs = refs[:entries], refs[entries:]
    (out_ref, x1_ref, a_ref, h_ref, q_ref, k_ref, v_ref, stats_ref, states_ref, sums_ref,
     *refs) = refs
    end_refs, refs = refs[: min(entries, 2)], refs[min(entries, 2) :]
    s_ref, z_ref, kp_ref, vp_ref, wkt_ref, wvt_ref = refs
    step = pl.program_id(0)

    @pl.when(step == 0)
    def _():
        start_with((s_ref, z_ref, kp_ref, vp_ref), entry_refs)
        wkt_ref[...] = wk_ref[...].T
        wvt_ref[...] = wv_ref[...].T

    x = x_ref[...].astype(F32)
    inv = lax.rsqrt(jnp.mean(x * x, -1, keepdims=True) + EPSILON)
    hidden = (x * inv * ga_ref[...]).astype(BF16)
    h_ref[...] = hidden
    q_ref[...] = nn(hidden, wq_ref[...]).astype(BF16)
    k_ref[...] = nt(wkt_ref[...], hidden).astype(BF16)
    v_ref[...] = nt(wvt_ref[...], hidden).astype(BF16)
    same_head = head_mask(CHUNK)
    for sub in range(BLOCK // CHUNK):
        rows = slice(sub * CHUNK, (sub + 1) * CHUNK)
        chunk = step * (BLOCK // CHUNK) + sub
        band, far_mask, carry, tail, keep = chunk_masks(seg_ref, place_ref, chunk)
        tail_rows = jnp.broadcast_to(tail, (16, CHUNK))

        def body(p):
            lanes = slice(p * 128, (p + 1) * 128)
            qp = q_ref[rows, lanes]
            kt = k_ref[lanes, rows]
            vt = v_ref[lanes, rows]
            kt_ext = jnp.concatenate([kp_ref[lanes], kt], 1)
            vt_ext = jnp.concatenate([vp_ref[lanes], vt], 1)
            score = nn(split_heads(qp * SCALE), kt_ext)
            fq, _ = features(qp.astype(F32))
            fk, _ = features(kt.astype(F32))
            fk = [f.astype(BF16) for f in fk]
            fq = [f.astype(BF16) for f in fq]
            yield
            part = [
                jnp.where(far_mask, nn(split_heads(fq[m]), fk[m]), 0.0) for m in range(2)
            ]
            score = jnp.where(band, score, NEG)
            top = jnp.max(score, -1, keepdims=True)
            yield
            state = s_ref[p]
            state_low = state.astype(BF16)
            sums = z_ref[p]
            states_ref[sub, p] = state_low
            sums_ref[sub, p] = sums
            fk_both = jnp.concatenate(fk, 0)
            update = nt(fk_both * tail, vt)
            s_ref[p] = keep * state + jnp.where(same_head, update, 0.0)
            z_ref[p] = keep * sums + nt(tail_rows, fk_both)[:8]
            expo = jnp.exp(score - top)
            total = jnp.sum(expo, -1, keepdims=True)
            yield
            inv_total = 1.0 / total
            prob_prev = (expo[:, :CHUNK] * inv_total).astype(BF16)
            weight = expo[:, CHUNK:] * inv_total
            columns = [top + jnp.log(total)]
            scaled = []
            for m in range(2):
                fq_carry = fq[m].astype(F32) * carry
                entered = split_heads(fq_carry * sums[:1, m * 128 : (m + 1) * 128])
                inv_z = 1.0 / jnp.sum(part[m] + entered, -1, keepdims=True)
                columns.append(inv_z)
                weight = weight + part[m] * inv_z
                scaled.append((fq_carry * over_lanes(inv_z)).astype(BF16))
            both = jnp.concatenate([prob_prev, weight.astype(BF16)], 1)
            yield
            attended = pick(nt(both, vt_ext)) + nn(jnp.concatenate(scaled, 1), state_low)
            a_ref[rows, lanes] = attended.astype(BF16)
            for n, column in enumerate(columns):
                stats_ref[sub, p, n] = jnp.broadcast_to(column, (2 * CHUNK, CHUNK))

        for first in range(0, PAIRS, STEP_PAIRS):
            in_step(body(p) for p in range(first, first + STEP_PAIRS))
        kp_ref[...] = k_ref[:, rows]
        vp_ref[...] = v_ref[:, rows]
    for end_ref, ref in zip(end_refs, (s_ref, z_ref)):
        end_ref[...] = ref[...]
    x1 = x + nn(a_ref[...], wo_ref[...])
    x1_ref[...] = x1
    inv = lax.rsqrt(jnp.mean(x1 * x1, -1, keepdims=True) + EPSILON)
    hidden = (x1 * inv * gf_ref[...]).astype(BF16)
    total = x1
    width = 512
    for f in range(wu_ref.shape[1] // width):
        cols = slice(f * width, (f + 1) * width)
        up = nn(hidden, wu_ref[:, cols])
        act = 0.5 * up * (1.0 + jnp.tanh(GELU_A * (up + GELU_B * up * up * up)))
        total = total + nn(act.astype(BF16), wd_ref[cols])
    out_ref[...] = total.astype(BF16)


def norm_backward(x, gain, grad):
    inv = lax.rsqrt(jnp.mean(x * x, -1, keepdims=True) + EPSILON)
    unit = x * inv
    scaled = grad * gain
    d_gain = jnp.sum(grad * unit, 0, keepdims=True)
    return inv * (scaled - unit * jnp.mean(unit * scaled, -1, keepdims=True)), d_gain


def ffn_backward_kernel(first, last, *refs):
    dy_ref, x1_ref, gf_ref, wu_ref, wd_ref, core_ref, *refs = refs
    if not first:
        dh_in_ref, *refs = refs
    if last:
        a_ref, wo_ref, dx1_ref, da_ref, dg_ref, *refs = refs
    else:
        dh_out_ref, *refs = refs
    keep_ref, send_ref, dwd_acc, dwu_acc, *refs = refs
    if last:
        dwo_acc, dg_acc = refs
    step = pl.program_id(0)

    @pl.when(step == 0)
    def _():
        dwd_acc[...] = jnp.zeros_like(dwd_acc)
        dwu_acc[...] = jnp.zeros_like(dwu_acc)
        if last:
            dwo_acc[...] = jnp.zeros_like(dwo_acc)
            dg_acc[...] = jnp.zeros_like(dg_acc)

    dy = dy_ref[...]
    x1 = x1_ref[...]
    gain = gf_ref[...]
    inv = lax.rsqrt(jnp.mean(x1 * x1, -1, keepdims=True) + EPSILON)
    hidden = (x1 * inv * gain).astype(BF16)
    d_hidden = jnp.zeros(x1.shape, F32) if first else dh_in_ref[...]
    width = x1.shape[1]
    for f in range(wu_ref.shape[1] // width):
        cols = slice(f * width, (f + 1) * width)
        up = nn(hidden, wu_ref[:, cols])
        square = up * up
        tanh = jnp.tanh(GELU_A * up * (1.0 + GELU_B * square))
        half = 0.5 * (1.0 + tanh)
        act = (up * half).astype(BF16)
        slope = half + 0.5 * up * (1.0 - tanh * tanh) * (
            GELU_A + (3.0 * GELU_A * GELU_B) * square
        )
        d_up = (slope * nt(dy, wd_ref[cols])).astype(BF16)
        dwd_acc[cols] += tn(act, dy)
        dwu_acc[cols] += tn(hidden, d_up)
        d_hidden = d_hidden + nt(d_up, wu_ref[:, cols])
    if last:
        d_norm, d_gain = norm_backward(x1, gain, d_hidden)
        dx1 = dy.astype(F32) + d_norm
        dg_acc[...] += jnp.broadcast_to(d_gain, dg_acc.shape)
        dx1_ref[...] = dx1
        d_branch = dx1.astype(BF16)
        dwo_acc[...] += tn(a_ref[...], d_branch)
        da_ref[...] = nt(d_branch, wo_ref[...]).astype(BF16)
    else:
        dh_out_ref[...] = d_hidden

    @pl.when(step == pl.num_programs(0) - 1)
    def _():
        sums = (dwd_acc, dwu_acc) + ((dwo_acc,) if last else ())
        put_halves(sums, core_ref[0], keep_ref, send_ref)
        if last:
            dg_ref[...] = dg_acc[...]


def put_halves(sums, core, keep_ref, send_ref):
    at = 0
    for total in sums:
        half = total.shape[0] // 2
        for ref, which in ((keep_ref, core), (send_ref, 1 - core)):
            rows = total[pl.ds(pl.multiple_of(which * half, half), half)]
            ref[at : at + half] = rows.astype(BF16)
        at += half
    return at


def attention_backward_kernel(last, earlier, entries, *refs):
    (da_ref, q_ref, k_ref, v_ref, kprev_ref, vprev_ref, stats_ref, states_ref, sums_ref,
     seg_ref, h_ref, place_ref, *refs) = refs
    entry_refs, refs = refs[:entries], refs[entries:]
    if last:
        x_ref, dx1_ref, ga_ref, dgf_ref, wq_ref, wk_ref, wv_ref, *refs = refs
        earlier_refs, refs = refs[: 3 * earlier], refs[3 * earlier :]
        dx_ref, *refs = refs
    dq_ref, dk_ref, dv_ref, keep_ref, send_ref, *refs = refs
    end_refs, refs = refs[: min(entries, 3)], refs[min(entries, 3) :]
    r_ref, dkc_ref, dvc_ref, dwq_acc, dwk_acc, dwv_acc, *refs = refs
    if last:
        dg_acc, wkt_ref, wvt_ref = refs
    step = pl.program_id(0)
    block = pl.num_programs(0) - 1 - step

    @pl.when(step == 0)
    def _():
        start_with((r_ref, dkc_ref, dvc_ref), entry_refs)
        dwq_acc[...] = jnp.zeros_like(dwq_acc)
        dwk_acc[...] = jnp.zeros_like(dwk_acc)
        dwv_acc[...] = jnp.zeros_like(dwv_acc)
        if last:
            dg_acc[...] = jnp.zeros_like(dg_acc)
            wkt_ref[...] = wk_ref[...].T
            wvt_ref[...] = wv_ref[...].T

    lane = lax.broadcasted_iota(jnp.int32, (CHUNK, CHUNK), 1)
    same_head = head_mask(2 * CHUNK)
    for sub in reversed(range(BLOCK // CHUNK)):
        rows = slice(sub * CHUNK, (sub + 1) * CHUNK)
        chunk = block * (BLOCK // CHUNK) + sub
        band, far_mask, carry, tail, keep = chunk_masks(seg_ref, place_ref, chunk)
        tail_rows = jnp.broadcast_to(tail, (CHUNK, CHUNK))

        def body(p):
            lanes = slice(p * 128, (p + 1) * 128)
            qp = q_ref[rows, lanes]
            da = da_ref[rows, lanes]
            kt = k_ref[lanes, rows]
            vt = v_ref[lanes, rows]
            if sub == 0:
                kt_prev, vt_prev = kprev_ref[lanes], vprev_ref[lanes]
                if entry_refs:
                    kt_prev = jnp.where(block == 0, entry_refs[3][lanes], kt_prev)
                    vt_prev = jnp.where(block == 0, entry_refs[4][lanes], vt_prev)
            else:
                before = slice((sub - 1) * CHUNK, sub * CHUNK)
                kt_prev, vt_prev = k_ref[lanes, before], v_ref[lanes, before]
            kt_ext = jnp.concatenate([kt_prev, kt], 1)
            vt_ext = jnp.concatenate([vt_prev, vt], 1)
            q2 = split_heads(qp * SCALE)
            da2 = split_heads(da)
            score = nn(q2, kt_ext)
            d_prob = nn(da2, vt_ext)
            yield
            state = states_ref[sub, p]
            sums = sums_ref[sub, p]
            back = r_ref[p]
            back_low = back.astype(BF16)
            from_state = nt(da, state) * carry
            to_later = nn(back_low, jnp.concatenate([vt * tail, tail_rows], 0))
            fq, slope_q = features(qp.astype(F32))
            fk, slope_k = features(kt.astype(F32))
            fk = [f.astype(BF16) for f in fk]
            fq = [f.astype(BF16) for f in fq]
            fq2 = [split_heads(f) for f in fq]
            yield
            part = [jnp.where(far_mask, nn(fq2[m], fk[m]), 0.0) for m in range(2)]
            lse = stats_ref[sub, p, 0]
            prob = jnp.exp(jnp.where(band, score - jnp.concatenate([lse, lse], 1), NEG))
            delta = jnp.sum(prob * d_prob, -1, keepdims=True)
            d_score = (prob * (d_prob - delta)).astype(BF16)
            yield
            dq = SCALE * pick(nt(d_score, kt_ext))
            dk_ext = tn(q2, d_score)
            dk = dk_ext[:, CHUNK:] + dkc_ref[lanes]
            dkc_ref[lanes] = dk_ext[:, :CHUNK]
            d_own = d_prob[:, CHUNK:]
            weight = prob[:, CHUNK:]
            yield
            scaled = []
            d_part = []
            entries = []
            right = jnp.zeros((CHUNK, CHUNK), F32)
            for m in range(2):
                part_lanes = slice(m * 128, (m + 1) * 128)
                fq_wide = fq[m].astype(F32)
                inv_z = stats_ref[sub, p, m + 1]
                weighted = part[m] * inv_z
                weight = weight + weighted
                entered = from_state[:, part_lanes]
                inv_wide = pick(inv_z)
                taken = fq_wide * inv_wide
                dot = jnp.sum(
                    weighted * d_own + split_heads(taken * entered), -1, keepdims=True
                )
                d_part.append(jnp.where(far_mask, (d_own - dot) * inv_z, 0.0).astype(BF16))
                entries.append(
                    inv_wide * (entered - over_lanes(dot) * (carry * sums[:1, part_lanes]))
                )
                scaled.append((taken * carry).astype(BF16))
                right = jnp.where(lane == 2 * m, -dot[:CHUNK], right)
                right = jnp.where(lane == 2 * m + 1, -dot[CHUNK:], right)
            both = jnp.concatenate([prob[:, :CHUNK].astype(BF16), weight.astype(BF16)], 1)
            yield
            dv_ext = tn(da2, both)
            dv = dv_ext[:, CHUNK:] + dvc_ref[lanes]
            dv = dv + tn(back_low[:, :CHUNK], jnp.concatenate(fk, 0) * tail)
            dvc_ref[lanes] = dv_ext[:, :CHUNK]
            update = tn(
                jnp.concatenate(scaled, 1), jnp.concatenate([da, right.astype(BF16)], 1)
            )
            r_ref[p] = keep * back + jnp.where(same_head, update, 0.0)
            dv_ref[lanes, rows] = dv.astype(BF16)
            yield
            for m in range(2):
                dq = dq + slope_q[m] * (pick(nt(d_part[m], fk[m])) + entries[m])
                dk = dk + slope_k[m] * (
                    tn(fq2[m], d_part[m]) + to_later[m * 128 : (m + 1) * 128]
                )
            dq_ref[rows, lanes] = dq.astype(BF16)
            dk_ref[lanes, rows] = dk.astype(BF16)

        in_step(body(p) for p in range(r_ref.shape[0]))
    for end_ref, ref in zip(end_refs, (r_ref, dkc_ref, dvc_ref)):
        end_ref[...] = ref[...]
    dim = h_ref.shape[1]
    hidden_t = h_ref[...].T
    dwq_acc[...] += nn(hidden_t, dq_ref[...])
    dwk_acc[...] += nt(hidden_t, dk_ref[...])
    dwv_acc[...] += nt(hidden_t, dv_ref[...])
    if last:
        mine = (dq_ref, dk_ref, dv_ref)
        dq, dk, dv = (
            jnp.concatenate([ref[...] for ref in earlier_refs[n::3] + [mine[n]]], min(n, 1) ^ 1)
            for n in range(3)
        )
        d_hidden = nt(dq, wq_ref[...]) + tn(dk, wkt_ref[...]) + tn(dv, wvt_ref[...])
        d_norm, d_gain = norm_backward(x_ref[...].astype(F32), ga_ref[...], d_hidden)
        dg_acc[...] += jnp.broadcast_to(d_gain, dg_acc.shape)
        dx_ref[...] = (dx1_ref[...] + d_norm).astype(BF16)

    @pl.when(step == pl.num_programs(0) - 1)
    def _():
        core = place_ref[2]
        at = put_halves((dwq_acc, dwk_acc, dwv_acc), core, keep_ref, send_ref)
        keep_ref[at:] = jnp.zeros((GAIN_ROWS, keep_ref.shape[1]), BF16)
        send_ref[at:] = jnp.zeros((GAIN_ROWS, keep_ref.shape[1]), BF16)
        if last:
            width = keep_ref.shape[1]
            gains = [
                ref[:1, n : n + width] for ref in (dg_acc, dgf_ref) for n in range(0, dim, width)
            ]
            gains += [jnp.zeros((16 - len(gains), width), F32)]
            gains = jnp.concatenate(gains, 0)
            keep_ref[at : at + 16] = jnp.where(core == 0, gains, 0.0).astype(BF16)
            send_ref[at : at + 16] = jnp.where(core == 0, 0.0, gains).astype(BF16)


def whole(shape):
    return pl.BlockSpec(shape, lambda i: (0,) * len(shape))


def tokens_of(width, index=lambda i: i):
    return pl.BlockSpec((BLOCK, width), lambda i: (index(i), 0))


def params():
    return pltpu.CompilerParams(
        vmem_limit_bytes=VMEM_LIMIT, dimension_semantics=("arbitrary",)
    )


def sds(shape, dtype):
    return jax.ShapeDtypeStruct(shape, dtype)


def run_forward(x, segments, place, gain_attn, gain_ffn, wq, wk, wv, wo, wu, wd, entry):
    length, dim = x.shape
    ff = wu.shape[1]
    chunks = length // CHUNK
    per = BLOCK // CHUNK
    row = tokens_of(dim)
    column = pl.BlockSpec((dim, BLOCK), lambda i: (0, i))
    state_shape = (PAIRS, 4 * HEAD, 2 * HEAD)
    sum_shape = (PAIRS, 8, 4 * HEAD)
    stat_shape = (PAIRS, 3, 2 * CHUNK, CHUNK)
    ends = [(state_shape, F32), (sum_shape, F32)][: len(entry)]
    return pl.pallas_call(
        functools.partial(forward_kernel, len(entry)),
        grid=(length // BLOCK,),
        in_specs=[
            row, whole(segments.shape), SMEM, whole((1, dim)), whole((1, dim)),
            whole((dim, dim)), whole((dim, dim)), whole((dim, dim)), whole((dim, dim)),
            whole((dim, ff)), whole((ff, dim)),
        ] + [whole(array.shape) for array in entry],
        out_specs=[
            row, row, row, row, row, column, column,
            pl.BlockSpec((per,) + stat_shape, lambda i: (i, 0, 0, 0, 0)),
            pl.BlockSpec((per,) + state_shape, lambda i: (i, 0, 0, 0)),
            pl.BlockSpec((per,) + sum_shape, lambda i: (i, 0, 0, 0)),
        ] + [whole(shape) for shape, _ in ends],
        out_shape=[
            sds((length, dim), BF16), sds((length, dim), F32), sds((length, dim), BF16),
            sds((length, dim), BF16), sds((length, dim), BF16),
            sds((dim, length), BF16), sds((dim, length), BF16),
            sds((chunks,) + stat_shape, F32),
            sds((chunks,) + state_shape, BF16), sds((chunks,) + sum_shape, F32),
        ] + [sds(*end) for end in ends],
        scratch_shapes=[
            pltpu.VMEM(state_shape, F32), pltpu.VMEM(sum_shape, F32),
            pltpu.VMEM((dim, CHUNK), BF16), pltpu.VMEM((dim, CHUNK), BF16),
            pltpu.VMEM((dim, dim), BF16), pltpu.VMEM((dim, dim), BF16),
        ],
        compiler_params=params(),
        name="layer_forward",
    )(x, segments, place, gain_attn, gain_ffn, wq, wk, wv, wo, wu, wd, *entry)


SMEM = pl.BlockSpec(memory_space=pltpu.SMEM)
ANY = pl.BlockSpec(memory_space=pl.ANY)


def run_ffn_backward(part, part_count, dy, x1, gain_ffn, wu, wd, core, d_hidden, a, wo):
    first, last = part == 0, part == part_count - 1
    length, dim = dy.shape
    ff = wu.shape[1] // part_count
    half = ff + (dim // 2 if last else 0)
    row = tokens_of(dim)
    more_in, more_args, outs, shapes, scratch = [], [], [], [], []
    if not first:
        more_in, more_args = [row], [d_hidden]
    if last:
        more_in += [row, whole((dim, dim))]
        more_args += [a, wo]
        outs = [row, row, whole((8, dim))]
        shapes = [sds((length, dim), F32), sds((length, dim), BF16), sds((8, dim), F32)]
        scratch = [pltpu.VMEM((dim, dim), F32), pltpu.VMEM((8, dim), F32)]
    else:
        outs, shapes = [row], [sds((length, dim), F32)]
    return pl.pallas_call(
        functools.partial(ffn_backward_kernel, first, last),
        grid=(length // BLOCK,),
        in_specs=[
            row, row, whole((1, dim)),
            pl.BlockSpec((dim, ff), lambda i: (0, part)),
            pl.BlockSpec((ff, dim), lambda i: (part, 0)),
            SMEM,
        ] + more_in,
        out_specs=outs + [whole((half, dim))] * 2,
        out_shape=shapes + [sds((half, dim), BF16)] * 2,
        scratch_shapes=[pltpu.VMEM((ff, dim), F32), pltpu.VMEM((ff, dim), F32)] + scratch,
        compiler_params=params(),
        name="ffn_backward",
    )(dy, x1, gain_ffn, wu, wd, core, *more_args)


def run_attention_backward(
    first, pairs, after, through, x, dx1, da, h, q, k, v, stats, states, sums, segments, place,
    gain_attn, dgf, wq, wk, wv, earlier, entry,
):
    last = first + pairs == PAIRS
    length, dim = x.shape
    width = 2 * HEAD * pairs
    call = first // pairs
    half = 3 * dim // 2 + GAIN_ROWS
    steps = length // BLOCK
    per = BLOCK // CHUNK
    back = lambda i: steps - 1 - i
    row = tokens_of(dim, back)
    part_row = pl.BlockSpec((BLOCK, width), lambda i: (back(i), call))
    part_column = pl.BlockSpec((width, BLOCK), lambda i: (call, back(i)))
    prev = pl.BlockSpec((width, CHUNK), lambda i: (call, jnp.maximum(back(i) * per - 1, 0)))
    rim_in = pl.BlockSpec((width, CHUNK), lambda i: (call, 0))
    rim = whole((width, CHUNK))
    r_shape = (pairs, 4 * HEAD, 4 * HEAD)
    rim_shape = (width, CHUNK)

    def of_pairs(array):
        shape = array.shape[2:]
        return pl.BlockSpec((per, pairs) + shape, lambda i: (back(i), call) + (0,) * len(shape))

    entry_in = [whole(r_shape), rim, rim, rim_in, rim_in][: len(entry)]
    ends = [r_shape, rim_shape, rim_shape][: len(entry)]
    more_in, more_args, outs, shapes, scratch = [], [], [], [], []
    if last:
        square = whole((dim, dim))
        more_in = [row, row, whole((1, dim)), whole(dgf.shape), square, square, square]
        more_args = [x, dx1, gain_attn, dgf, wq, wk, wv]
        for group in earlier:
            size = group[0].shape[1]
            column = pl.BlockSpec((size, BLOCK), lambda i: (0, back(i)))
            more_in += [tokens_of(size, back), column, column]
            more_args += group
        outs = [row]
        shapes = [sds((length, dim), BF16)]
        scratch = [
            pltpu.VMEM((8, dim), F32), pltpu.VMEM((dim, dim), BF16), pltpu.VMEM((dim, dim), BF16),
        ]
    kernel = functools.partial(attention_backward_kernel, last, len(earlier), len(entry))
    skip = len(after) + len(through)
    args = [
        da, q, k, v, k, v, stats, states, sums, segments, h, place, *entry, *more_args,
    ]
    inputs = skip + len(args)

    def body(*refs):
        kernel(*refs[skip:inputs], *refs[inputs + len(through) :])

    return pl.pallas_call(
        body,
        grid=(steps,),
        input_output_aliases={len(after) + n: n for n in range(len(through))},
        in_specs=[ANY] * skip + [
            part_row, part_row, part_column, part_column, prev, prev,
            of_pairs(stats), of_pairs(states), of_pairs(sums), whole(segments.shape), row, SMEM,
        ] + entry_in + more_in,
        out_specs=[ANY] * len(through) + outs + [
            tokens_of(width, back),
            pl.BlockSpec((width, BLOCK), lambda i: (0, back(i))),
            pl.BlockSpec((width, BLOCK), lambda i: (0, back(i))),
            whole((half, width)), whole((half, width)),
        ] + [whole(shape) for shape in ends],
        out_shape=[sds(array.shape, array.dtype) for array in through] + shapes + [
            sds((length, width), BF16), sds((width, length), BF16), sds((width, length), BF16),
            sds((half, width), BF16), sds((half, width), BF16),
        ] + [sds(shape, F32) for shape in ends],
        scratch_shapes=[
            pltpu.VMEM(r_shape, F32), pltpu.VMEM(rim_shape, F32), pltpu.VMEM(rim_shape, F32),
            pltpu.VMEM((dim, width), F32), pltpu.VMEM((dim, width), F32),
            pltpu.VMEM((dim, width), F32),
        ] + scratch,
        compiler_params=params(),
        name="attention_backward",
    )(*after, *through, *args)


def finish_kernel(skip, across, core_ref, own_ref, other_ref, *refs):
    out_refs = refs[skip:]
    at = 0
    width = own_ref.shape[1]
    for wide, out_ref in zip(across, out_refs):
        half = out_ref.shape[0] * out_ref.shape[1] // width // 2
        for ref, which in ((own_ref, core_ref[0]), (other_ref, 1 - core_ref[0])):
            if wide:
                rows = out_ref.shape[0]
                for c in range(half // rows):
                    start = pl.multiple_of((which * (half // rows) + c) * width, width)
                    block = ref[at + c * rows : at + (c + 1) * rows]
                    out_ref[:, pl.ds(start, width)] = block.astype(F32)
            else:
                rows = pl.ds(pl.multiple_of(which * half, half), half)
                out_ref[rows] = ref[at : at + half].astype(F32)
        at += half


def run_finish(core_ref, own, other, across, shapes, after):
    full = pl.BlockSpec(memory_space=pltpu.VMEM)
    return pl.pallas_call(
        functools.partial(finish_kernel, len(after), across),
        in_specs=[SMEM, full, full] + [ANY] * len(after),
        out_specs=[full] * len(shapes),
        out_shape=[sds(shape, F32) for shape in shapes],
        compiler_params=pltpu.CompilerParams(vmem_limit_bytes=VMEM_LIMIT),
        name="finish",
    )(core_ref, own, other, *after)


def partner(array, seq_bits, row_bits):
    seq_count, row_groups = lax.axis_size("seq"), lax.axis_size("rows")
    pairs = [
        (s * row_groups + r, (s ^ seq_bits) * row_groups + (r ^ row_bits))
        for s in range(seq_count)
        for r in range(row_groups)
    ]
    return lax.ppermute(array, ("seq", "rows"), pairs)


def add(*parts):
    parts = [part.astype(F32) for part in parts]
    if len(parts) == 4:
        return ((parts[0] + parts[1]) + (parts[2] + parts[3])).astype(BF16)
    return (parts[0] + parts[1]).astype(BF16)


def take(array, index, size):
    return lax.dynamic_slice_in_dim(array, index * size, size, 0)


PLANE_BITS = ((1, 0), (0, 2), (1, 2))
DEPTH_BITS = ((2, 0), (4, 0), (6, 0))


def cut(total, place):
    size = total.shape[0] // 4
    return [take(total, place ^ d, size) for d in range(4)]


def traded(parts, all_bits):
    return [parts[0]] + [partner(part, *bits) for part, bits in zip(parts[1:], all_bits)]


def joined(parts, place):
    blocks = jnp.stack(parts)
    blocks = [lax.dynamic_index_in_dim(blocks, place ^ d, 0, False) for d in range(4)]
    return jnp.concatenate(blocks, 0)


def all_reduce(places, halves):
    core, plane, depth = places
    others = [partner(send, 0, 1) for _, send in halves]
    keeps = yield [keep for keep, _ in halves]
    sums = [add(keep, other) for keep, other in zip(keeps, others)]
    parts = yield cut(jnp.concatenate(sums, 1) if len(sums) > 1 else sums[0], plane)
    parts = traded(parts, PLANE_BITS)
    parts = yield parts
    parts = yield cut(add(*parts), depth)
    parts = traded(parts, DEPTH_BITS)
    parts = yield parts
    total = add(*parts)
    for bits in further_bits():
        total = add(total, partner(total, *bits))
    (total,) = yield [total]
    parts = traded([total] * 4, DEPTH_BITS)
    parts = yield parts
    (block,) = yield [joined(parts, depth)]
    parts = traded([block] * 4, PLANE_BITS)
    parts = yield parts
    (own,) = yield [joined(parts, plane)]
    yield [own, partner(own, 0, 1)]


class Reduction:
    def __init__(self, *args):
        self.steps = all_reduce(*args)
        self.arrays = next(self.steps)

    def step(self):
        self.arrays = self.steps.send(self.arrays)

    def finish(self):
        for arrays in iter(lambda: self.steps.send(self.arrays), None):
            self.arrays = arrays
            if len(arrays) == 2:
                return arrays


def further_bits():
    bits = []
    bit = 8
    while bit < lax.axis_size("seq"):
        bits.append((bit, 0))
        bit *= 2
    bit = 4
    while bit < lax.axis_size("rows"):
        bits.append((0, bit))
        bit *= 2
    return bits


def all_reduce_small(small):
    small = small + partner(small, 0, 1)
    for bits in (((1, 0), (0, 2), (1, 2)), ((2, 0), (4, 0), (6, 0))):
        got = [small] + [partner(small, *b) for b in bits]
        small = (got[0] + got[1]) + (got[2] + got[3])
    for b in further_bits():
        small = small + partner(small, *b)
    return small


def local(
    tokens, segments, gain_attn, gain_ffn, w_query, w_key, w_value, w_out, w_up, w_down, cotangent
):
    row_count, shard_len, dim = tokens.shape
    seq_count = lax.axis_size("seq")
    parts = seq_count // row_count
    groups = [[g * row_count + r for r in range(row_count)] for g in range(parts)]
    length = row_count * shard_len
    index = lax.axis_index("seq")
    my_row = index % row_count
    my_part = index // row_count

    def trade(array):
        return lax.all_to_all(
            array.reshape(row_count, shard_len, dim), "seq", 0, 0, axis_index_groups=groups
        )

    def shifted(arrays, by):
        pairs = [
            (i, i + by * row_count)
            for i in range(seq_count)
            if 0 <= i + by * row_count < seq_count
        ]
        return lax.ppermute(arrays, "seq", pairs)

    ga, gf = gain_attn.reshape(1, dim), gain_ffn.reshape(1, dim)
    seq_index, row_index = lax.axis_index("seq"), lax.axis_index("rows")
    core, plane = row_index % 2, seq_index % 2 + 2 * (row_index // 2 % 2)
    places = core, plane, seq_index // 2 % 4
    place = jnp.stack([my_row, my_part * (length // CHUNK), core]).astype(jnp.int32)

    x = trade(tokens).reshape(length, dim)
    dy = trade(cotangent).reshape(length, dim)
    entry = ()
    if parts > 1:
        rim_zero = jnp.zeros((dim, CHUNK), BF16)
        entry = (
            jnp.zeros((PAIRS, 4 * HEAD, 2 * HEAD), F32), jnp.zeros((PAIRS, 8, 4 * HEAD), F32),
            rim_zero, rim_zero,
        )
    for turn in range(parts):
        out, x1, a, h, q, k, v, stats, states, sums, *ends = run_forward(
            x, segments, place, ga, gf, w_query, w_key, w_value, w_out, w_up, w_down, entry
        )
        if turn < parts - 1:
            entry = shifted((*ends, k[:, length - CHUNK :], v[:, length - CHUNK :]), 1)
    output = trade(out)
    core_ref = place[2:]
    dx1, da, dgf, keep, send = run_ffn_backward(
        0, 1, dy, x1, gf, w_up, w_down, core_ref, None, a, w_out
    )
    ffn = Reduction(places, [(keep, send)])
    backs = [()] * len(CALLS)
    if parts > 1:
        backs = [
            (
                jnp.zeros((pairs, 4 * HEAD, 4 * HEAD), F32),
                jnp.zeros((pairs * 2 * HEAD, CHUNK), F32),
                jnp.zeros((pairs * 2 * HEAD, CHUNK), F32),
            )
            for _, pairs in CALLS
        ]
    for turn in range(parts):
        earlier, halves = [], []
        for n, (first, pairs) in enumerate(CALLS):
            after, through = [], []
            if turn == parts - 1:
                for _ in range(STEPS_BEFORE[n]):
                    ffn.step()
                through, after = ffn.arrays[:1], ffn.arrays[1:]
                if first + pairs == PAIRS:
                    after.append(output)
            outs = run_attention_backward(
                first, pairs, after, through, x, dx1, da, h, q, k, v, stats, states, sums,
                segments, place, ga, dgf, w_query, w_key, w_value, earlier,
                backs[n] + entry[2:] if parts > 1 else (),
            )
            if through:
                ffn.arrays[0], *outs = outs
            if first + pairs == PAIRS:
                dx, *outs = outs
            dq, dk, dv, keep, send, *ends = outs
            earlier.append((dq, dk, dv))
            halves.append((keep, send))
            if turn < parts - 1:
                backs[n] = shifted(tuple(ends), -1)
    d_tokens = trade(dx)
    attention = Reduction(places, halves)
    ff = w_up.shape[1]
    own, other = ffn.finish()
    dwd, dwu, dwo = run_finish(
        core_ref, own, other, (False, True, False), ((ff, dim), (dim, ff), (dim, dim)), []
    )
    own, other = attention.finish()
    dwq, dwk, dwv = run_finish(
        core_ref, own, other, (False,) * 3, ((dim, dim),) * 3, [dwd, dwu, dwo]
    )
    at = 3 * dim // 2
    gains = jnp.where(core == 0, own[at : at + 16], other[at : at + 16])
    gains = gains[:, dim - 2 * HEAD * CALLS[-1][1] :].astype(F32).reshape(-1)
    return output, d_tokens, gains[:dim], gains[dim : 2 * dim], dwq, dwk, dwv, dwo, dwu, dwd


def solution(mesh):
    act = P("rows", "seq", None)
    return jax.shard_map(
        local,
        mesh=mesh,
        in_specs=(act, P("rows", None)) + (P(),) * 8 + (act,),
        out_specs=(act, act) + (P(),) * 8,
        check_vma=False,
    )
```

```python
import functools

import jax
import jax.numpy as jnp
from jax import lax
from jax.experimental import pallas as pl
from jax.experimental.pallas import tpu as pltpu
from jax.sharding import PartitionSpec as P

HEADS = 8
HEAD = 64
BAND = 30
EPSILON = 1e-06
SCALE = 0.125
CHUNK = 128
BLOCK = 256
PAIRS = HEADS // 2
NEG = -1e30
STEP_PAIRS = 2
GAIN_ROWS = 64
TAIL = "faffafaafaafa"
GATE_KIB = 512
TRADED = 11
FFN_ROWS = 2
FORWARD_MIB, FFN_MIB, ATTENTION_MIB = 52, 50, 54
GELU_A = 0.7978845608028654
GELU_B = 0.044715
F32 = jnp.float32
BF16 = jnp.bfloat16
VMEM_LIMIT = 56 * 1024 * 1024


def nn(a, b):
    return lax.dot_general(a, b, (((1,), (0,)), ((), ())), preferred_element_type=F32)


def nt(a, b):
    return lax.dot_general(a, b, (((1,), (1,)), ((), ())), preferred_element_type=F32)


def tn(a, b):
    return lax.dot_general(a, b, (((0,), (0,)), ((), ())), preferred_element_type=F32)


def low_lanes(shape):
    return lax.broadcasted_iota(jnp.int32, shape, len(shape) - 1) < HEAD


def split_heads(pair):
    low = low_lanes(pair.shape)
    zero = jnp.zeros_like(pair)
    return jnp.concatenate([jnp.where(low, pair, zero), jnp.where(low, zero, pair)], 0)


def pick(both):
    half = both.shape[0] // 2
    return jnp.where(low_lanes((half, both.shape[1])), both[:half], both[half:])


def over_lanes(column):
    half = column.shape[0] // 2
    return jnp.where(low_lanes((half, 2 * HEAD)), column[:half], column[half:])


def in_step(bodies):
    bodies = list(bodies)
    while bodies:
        bodies = [body for body in bodies if next(body, True) is None]


def features(t):
    expo = jnp.exp(jnp.minimum(t, 0.0))
    tanh = jnp.tanh(t)
    return (jnp.where(t > 0, t + 1.0, expo), 1.0 + tanh), (expo, 1.0 - tanh * tanh)


def head_mask(lanes):
    row = lax.broadcasted_iota(jnp.int32, (4 * HEAD, lanes), 0)
    lane = lax.broadcasted_iota(jnp.int32, (4 * HEAD, lanes), 1)
    head = (row // HEAD) % 2
    same = (lane < 2 * HEAD) & (lane // HEAD == head)
    return same | (lane == 2 * HEAD + row // HEAD)


def chunk_masks(seg_ref, place_ref, chunk):
    chunk = place_ref[1] + chunk

    def stretch(at):
        rows = seg_ref[:, pl.ds(pl.multiple_of(at * CHUNK, CHUNK), CHUNK)]
        mine = lax.broadcasted_iota(jnp.int32, rows.shape, 0) == place_ref[0]
        return jnp.max(jnp.where(mine, rows, -1), 0, keepdims=True).astype(F32)

    seg_own = stretch(chunk)
    seg_prev = jnp.where(chunk == 0, -1.0, stretch(jnp.maximum(chunk - 1, 0)))
    seg_q = jnp.broadcast_to(seg_own, (CHUNK, CHUNK)).T
    row = lax.broadcasted_iota(jnp.int32, (CHUNK, CHUNK), 0)
    col = lax.broadcasted_iota(jnp.int32, (CHUNK, CHUNK), 1)
    gap = row - col
    far = (seg_q == seg_own) & (gap >= 0)
    band_own = far & (gap <= BAND)
    band_prev = (seg_q == seg_prev) & (gap + CHUNK <= BAND)
    band = jnp.concatenate([band_prev, band_own], 1)
    before = seg_prev[:, CHUNK - 1 :]
    last = seg_own[:, CHUNK - 1 :]
    carry = (seg_q[:, :1] == before).astype(F32)
    tail = (seg_own == last).astype(BF16)
    keep = (before == last).astype(F32)
    return jnp.concatenate([band, band], 0), jnp.concatenate([far, far], 0), carry, tail, keep


def start_with(refs, entry_refs):
    for n, ref in enumerate(refs):
        ref[...] = entry_refs[n][...] if entry_refs else jnp.zeros_like(ref)


def forward_kernel(entries, *refs):
    (x_ref, seg_ref, place_ref, ga_ref, gf_ref, wq_ref, wk_ref, wv_ref, wo_ref, wu_ref, wd_ref,
     *refs) = refs
    entry_refs, refs = refs[:entries], refs[entries:]
    (out_ref, x1_ref, a_ref, h_ref, q_ref, k_ref, v_ref, stats_ref, states_ref, sums_ref,
     *refs) = refs
    end_refs, refs = refs[: min(entries, 2)], refs[min(entries, 2) :]
    s_ref, z_ref, kp_ref, vp_ref, wkt_ref, wvt_ref = refs
    step = pl.program_id(0)

    @pl.when(step == 0)
    def _():
        start_with((s_ref, z_ref, kp_ref, vp_ref), entry_refs)
        wkt_ref[...] = wk_ref[...].T
        wvt_ref[...] = wv_ref[...].T

    block = pl.ds(pl.multiple_of(step * BLOCK, BLOCK), BLOCK)
    x = x_ref[...].astype(F32)
    inv = lax.rsqrt(jnp.mean(x * x, -1, keepdims=True) + EPSILON)
    hidden = (x * inv * ga_ref[...]).astype(BF16)
    h_ref[...] = hidden
    q_ref[...] = nn(hidden, wq_ref[...]).astype(BF16)
    k_ref[...] = nt(wkt_ref[...], hidden).astype(BF16)
    v_ref[...] = nt(wvt_ref[...], hidden).astype(BF16)
    same_head = head_mask(CHUNK)
    for sub in range(BLOCK // CHUNK):
        chunk = step * (BLOCK // CHUNK) + sub
        rows = slice(sub * CHUNK, (sub + 1) * CHUNK)
        tokens = pl.ds(pl.multiple_of(chunk * CHUNK, CHUNK), CHUNK)
        band, far_mask, carry, tail, keep = chunk_masks(seg_ref, place_ref, chunk)
        tail_rows = jnp.broadcast_to(tail, (16, CHUNK))

        def body(p):
            lanes = slice(p * 128, (p + 1) * 128)
            qp = q_ref[rows, lanes]
            kt = k_ref[lanes, rows]
            vt = v_ref[lanes, rows]
            kt_ext = jnp.concatenate([kp_ref[lanes], kt], 1)
            vt_ext = jnp.concatenate([vp_ref[lanes], vt], 1)
            score = nn(split_heads(qp * SCALE), kt_ext)
            fq, _ = features(qp.astype(F32))
            fk, _ = features(kt.astype(F32))
            fk = [f.astype(BF16) for f in fk]
            fq = [f.astype(BF16) for f in fq]
            yield
            part = [
                jnp.where(far_mask, nn(split_heads(fq[m]), fk[m]), 0.0) for m in range(2)
            ]
            score = jnp.where(band, score, NEG)
            top = jnp.max(score, -1, keepdims=True)
            yield
            state = s_ref[p]
            state_low = state.astype(BF16)
            sums = z_ref[p]
            states_ref[sub, p] = state_low
            sums_ref[sub, p] = sums
            fk_both = jnp.concatenate(fk, 0)
            update = nt(fk_both * tail, vt)
            s_ref[p] = keep * state + jnp.where(same_head, update, 0.0)
            z_ref[p] = keep * sums + nt(tail_rows, fk_both)[:8]
            expo = jnp.exp(score - top)
            total = jnp.sum(expo, -1, keepdims=True)
            yield
            inv_total = 1.0 / total
            prob_prev = (expo[:, :CHUNK] * inv_total).astype(BF16)
            weight = expo[:, CHUNK:] * inv_total
            columns = [top + jnp.log(total)]
            scaled = []
            for m in range(2):
                fq_carry = fq[m].astype(F32) * carry
                entered = split_heads(fq_carry * sums[:1, m * 128 : (m + 1) * 128])
                inv_z = 1.0 / jnp.sum(part[m] + entered, -1, keepdims=True)
                columns.append(inv_z)
                weight = weight + part[m] * inv_z
                scaled.append((fq_carry * over_lanes(inv_z)).astype(BF16))
            both = jnp.concatenate([prob_prev, weight.astype(BF16)], 1)
            yield
            attended = pick(nt(both, vt_ext)) + nn(jnp.concatenate(scaled, 1), state_low)
            a_ref[tokens, lanes] = attended.astype(BF16)
            for n, column in enumerate(columns):
                stats_ref[sub, p, n] = jnp.broadcast_to(column, (2 * CHUNK, CHUNK))

        for first in range(0, PAIRS, STEP_PAIRS):
            in_step(body(p) for p in range(first, first + STEP_PAIRS))
        kp_ref[...] = k_ref[:, rows]
        vp_ref[...] = v_ref[:, rows]
    for end_ref, ref in zip(end_refs, (s_ref, z_ref)):
        end_ref[...] = ref[...]
    x1 = x + nn(a_ref[block], wo_ref[...])
    x1_ref[block] = x1
    inv = lax.rsqrt(jnp.mean(x1 * x1, -1, keepdims=True) + EPSILON)
    hidden = (x1 * inv * gf_ref[...]).astype(BF16)
    total = x1
    width = 512
    for f in range(wu_ref.shape[1] // width):
        cols = slice(f * width, (f + 1) * width)
        up = nn(hidden, wu_ref[:, cols])
        act = 0.5 * up * (1.0 + jnp.tanh(GELU_A * (up + GELU_B * up * up * up)))
        total = total + nn(act.astype(BF16), wd_ref[cols])
    out_ref[...] = total.astype(BF16)


def norm_backward(x, gain, grad):
    inv = lax.rsqrt(jnp.mean(x * x, -1, keepdims=True) + EPSILON)
    unit = x * inv
    scaled = grad * gain
    d_gain = jnp.sum(grad * unit, 0, keepdims=True)
    return inv * (scaled - unit * jnp.mean(unit * scaled, -1, keepdims=True)), d_gain


def ffn_backward_kernel(
    dy_ref, x1_ref, a_ref, gf_ref, wo_ref, wu_ref, wd_ref, core_ref,
    dx1_ref, da_ref, dg_ref, keep_ref, send_ref, keep_out_ref, send_out_ref,
    hidden_ref, dh_ref, dwd_ref, dwu_ref,
):
    step = pl.program_id(0)
    core = core_ref[0]
    gain = gf_ref[...]

    @pl.when(step == 0)
    def _():
        x1 = x1_ref[...]
        inv = lax.rsqrt(jnp.mean(x1 * x1, -1, keepdims=True) + EPSILON)
        hidden_ref[...] = (x1 * inv * gain).astype(BF16)
        dh_ref[...] = jnp.zeros_like(dh_ref)

    for part in range(FFN_ROWS):
        size = dy_ref.shape[0] // FFN_ROWS
        rows = slice(part * size, (part + 1) * size)
        dy = dy_ref[rows]
        hidden = hidden_ref[rows]
        up = nn(hidden, wu_ref[...])
        square = up * up
        tanh = jnp.tanh(GELU_A * up * (1.0 + GELU_B * square))
        half = 0.5 * (1.0 + tanh)
        act = (up * half).astype(BF16)
        slope = half + 0.5 * up * (1.0 - tanh * tanh) * (
            GELU_A + (3.0 * GELU_A * GELU_B) * square
        )
        d_up = (slope * nt(dy, wd_ref[...])).astype(BF16)
        dh_ref[rows] += nt(d_up, wu_ref[...])
        dwd, dwu = tn(act, dy), tn(hidden, d_up)
        if part:
            dwd, dwu = dwd + dwd_ref[...], dwu + dwu_ref[...]
        dwd_ref[...], dwu_ref[...] = dwd, dwu
    put_halves((dwd_ref, dwu_ref), core, keep_ref, send_ref)

    @pl.when(step == pl.num_programs(0) - 1)
    def _():
        x1 = x1_ref[...]
        d_norm, d_gain = norm_backward(x1, gain, dh_ref[...])
        dx1 = dy_ref[...].astype(F32) + d_norm
        dg_ref[...] = jnp.broadcast_to(d_gain, dg_ref.shape)
        dx1_ref[...] = dx1
        d_branch = dx1.astype(BF16)
        da_ref[...] = nt(d_branch, wo_ref[...]).astype(BF16)
        dwd_ref[...] = tn(a_ref[...], d_branch)
        put_halves((dwd_ref,), core, keep_out_ref, send_out_ref)


def put_halves(sums, core, keep_ref, send_ref):
    at = 0
    for total in sums:
        half = total.shape[0] // 2
        for ref, which in ((keep_ref, core), (send_ref, 1 - core)):
            rows = total[pl.ds(pl.multiple_of(which * half, half), half)]
            ref[at : at + half] = rows.astype(BF16)
        at += half
    return at


def attention_backward_kernel(entries, *refs):
    (x_ref, q_ref, h_ref, k_ref, v_ref, kprev_ref, vprev_ref, stats_ref, states_ref, sums_ref,
     da_ref, seg_ref, dx1_ref, place_ref, ga_ref, dgf_ref, wq_ref, wk_ref, wv_ref, *refs) = refs
    entry_refs, refs = refs[:entries], refs[entries:]
    dx_ref, keep_ref, send_ref, *refs = refs
    end_refs, refs = refs[: min(entries, 3)], refs[min(entries, 3) :]
    (r_ref, dkc_ref, dvc_ref, dq_ref, dk_ref, dv_ref, dwq_acc, dwk_acc, dwv_acc, dg_acc,
     wkt_ref, wvt_ref) = refs
    step = pl.program_id(0)
    block = pl.num_programs(0) - 1 - step

    @pl.when(step == 0)
    def _():
        start_with((r_ref, dkc_ref, dvc_ref), entry_refs)
        dwq_acc[...] = jnp.zeros_like(dwq_acc)
        dwk_acc[...] = jnp.zeros_like(dwk_acc)
        dwv_acc[...] = jnp.zeros_like(dwv_acc)
        dg_acc[...] = jnp.zeros_like(dg_acc)
        wkt_ref[...] = wk_ref[...].T
        wvt_ref[...] = wv_ref[...].T

    lane = lax.broadcasted_iota(jnp.int32, (CHUNK, CHUNK), 1)
    same_head = head_mask(2 * CHUNK)
    for sub in reversed(range(BLOCK // CHUNK)):
        chunk = block * (BLOCK // CHUNK) + sub
        rows = slice(sub * CHUNK, (sub + 1) * CHUNK)
        tokens = pl.ds(pl.multiple_of(chunk * CHUNK, CHUNK), CHUNK)
        band, far_mask, carry, tail, keep = chunk_masks(seg_ref, place_ref, chunk)
        tail_rows = jnp.broadcast_to(tail, (CHUNK, CHUNK))

        def body(p):
            lanes = slice(p * 128, (p + 1) * 128)
            qp = q_ref[rows, lanes]
            da = da_ref[tokens, lanes]
            kt = k_ref[lanes, rows]
            vt = v_ref[lanes, rows]
            if sub == 0:
                kt_prev, vt_prev = kprev_ref[lanes], vprev_ref[lanes]
                if entry_refs:
                    kt_prev = jnp.where(block == 0, entry_refs[3][lanes], kt_prev)
                    vt_prev = jnp.where(block == 0, entry_refs[4][lanes], vt_prev)
            else:
                before = slice((sub - 1) * CHUNK, sub * CHUNK)
                kt_prev, vt_prev = k_ref[lanes, before], v_ref[lanes, before]
            kt_ext = jnp.concatenate([kt_prev, kt], 1)
            vt_ext = jnp.concatenate([vt_prev, vt], 1)
            q2 = split_heads(qp * SCALE)
            da2 = split_heads(da)
            score = nn(q2, kt_ext)
            d_prob = nn(da2, vt_ext)
            yield
            state = states_ref[sub, p]
            sums = sums_ref[sub, p]
            back = r_ref[p]
            back_low = back.astype(BF16)
            from_state = nt(da, state) * carry
            to_later = nn(back_low, jnp.concatenate([vt * tail, tail_rows], 0))
            fq, slope_q = features(qp.astype(F32))
            fk, slope_k = features(kt.astype(F32))
            fk = [f.astype(BF16) for f in fk]
            fq = [f.astype(BF16) for f in fq]
            fq2 = [split_heads(f) for f in fq]
            yield
            part = [jnp.where(far_mask, nn(fq2[m], fk[m]), 0.0) for m in range(2)]
            lse = stats_ref[sub, p, 0]
            prob = jnp.exp(jnp.where(band, score - jnp.concatenate([lse, lse], 1), NEG))
            delta = jnp.sum(prob * d_prob, -1, keepdims=True)
            d_score = (prob * (d_prob - delta)).astype(BF16)
            yield
            dq = SCALE * pick(nt(d_score, kt_ext))
            dk_ext = tn(q2, d_score)
            dk = dk_ext[:, CHUNK:] + dkc_ref[lanes]
            dkc_ref[lanes] = dk_ext[:, :CHUNK]
            d_own = d_prob[:, CHUNK:]
            weight = prob[:, CHUNK:]
            yield
            scaled = []
            d_part = []
            entries = []
            right = jnp.zeros((CHUNK, CHUNK), F32)
            for m in range(2):
                part_lanes = slice(m * 128, (m + 1) * 128)
                fq_wide = fq[m].astype(F32)
                inv_z = stats_ref[sub, p, m + 1]
                weighted = part[m] * inv_z
                weight = weight + weighted
                entered = from_state[:, part_lanes]
                inv_wide = pick(inv_z)
                taken = fq_wide * inv_wide
                dot = jnp.sum(
                    weighted * d_own + split_heads(taken * entered), -1, keepdims=True
                )
                d_part.append(jnp.where(far_mask, (d_own - dot) * inv_z, 0.0).astype(BF16))
                entries.append(
                    inv_wide * (entered - over_lanes(dot) * (carry * sums[:1, part_lanes]))
                )
                scaled.append((taken * carry).astype(BF16))
                right = jnp.where(lane == 2 * m, -dot[:CHUNK], right)
                right = jnp.where(lane == 2 * m + 1, -dot[CHUNK:], right)
            both = jnp.concatenate([prob[:, :CHUNK].astype(BF16), weight.astype(BF16)], 1)
            yield
            dv_ext = tn(da2, both)
            dv = dv_ext[:, CHUNK:] + dvc_ref[lanes]
            dv = dv + tn(back_low[:, :CHUNK], jnp.concatenate(fk, 0) * tail)
            dvc_ref[lanes] = dv_ext[:, :CHUNK]
            update = tn(
                jnp.concatenate(scaled, 1), jnp.concatenate([da, right.astype(BF16)], 1)
            )
            r_ref[p] = keep * back + jnp.where(same_head, update, 0.0)
            dv_ref[lanes, rows] = dv.astype(BF16)
            yield
            for m in range(2):
                dq = dq + slope_q[m] * (pick(nt(d_part[m], fk[m])) + entries[m])
                dk = dk + slope_k[m] * (
                    tn(fq2[m], d_part[m]) + to_later[m * 128 : (m + 1) * 128]
                )
            dq_ref[rows, lanes] = dq.astype(BF16)
            dk_ref[lanes, rows] = dk.astype(BF16)

        for first in range(0, PAIRS, STEP_PAIRS):
            in_step(body(p) for p in range(first, first + STEP_PAIRS))
    for end_ref, ref in zip(end_refs, (r_ref, dkc_ref, dvc_ref)):
        end_ref[...] = ref[...]
    dim = x_ref.shape[1]
    tokens = pl.ds(pl.multiple_of(block * BLOCK, BLOCK), BLOCK)
    hidden_t = h_ref[...].T
    dq, dk, dv = dq_ref[...], dk_ref[...], dv_ref[...]
    dwq_acc[...] += nn(hidden_t, dq)
    dwk_acc[...] += nt(hidden_t, dk)
    dwv_acc[...] += nt(hidden_t, dv)
    d_hidden = nt(dq, wq_ref[...]) + tn(dk, wkt_ref[...]) + tn(dv, wvt_ref[...])
    d_norm, d_gain = norm_backward(x_ref[...].astype(F32), ga_ref[...], d_hidden)
    dg_acc[...] += jnp.broadcast_to(d_gain, dg_acc.shape)
    dx_ref[...] = (dx1_ref[tokens] + d_norm).astype(BF16)

    @pl.when(step == pl.num_programs(0) - 1)
    def _():
        core = place_ref[2]
        at = put_halves((dwq_acc, dwk_acc, dwv_acc), core, keep_ref, send_ref)
        keep_ref[at:] = jnp.zeros((GAIN_ROWS, keep_ref.shape[1]), BF16)
        send_ref[at:] = jnp.zeros((GAIN_ROWS, keep_ref.shape[1]), BF16)
        gains = jnp.concatenate([dg_acc[:1], dgf_ref[:1], jnp.zeros((14, dim), F32)], 0)
        keep_ref[at : at + 16] = jnp.where(core == 0, gains, 0.0).astype(BF16)
        send_ref[at : at + 16] = jnp.where(core == 0, 0.0, gains).astype(BF16)


HELD = pl.BlockSpec(memory_space=pltpu.VMEM)


def whole(shape):
    return pl.BlockSpec(shape, lambda i: (0,) * len(shape))


FFN_IN = HELD


def tokens_of(width, index=lambda i: i):
    return pl.BlockSpec((BLOCK, width), lambda i: (index(i), 0))


def of_chunks(shape, index=lambda i: i):
    return pl.BlockSpec((BLOCK // CHUNK,) + shape, lambda i: (index(i),) + (0,) * len(shape))


def params(mib):
    return pltpu.CompilerParams(
        vmem_limit_bytes=mib * 1024 * 1024, dimension_semantics=("arbitrary",)
    )


def sds(shape, dtype):
    return jax.ShapeDtypeStruct(shape, dtype)


def run_forward(x, segments, place, gain_attn, gain_ffn, wq, wk, wv, wo, wu, wd, entry):
    length, dim = x.shape
    ff = wu.shape[1]
    chunks = length // CHUNK
    row = tokens_of(dim)
    column = pl.BlockSpec((dim, BLOCK), lambda i: (0, i))
    state_shape = (PAIRS, 4 * HEAD, 2 * HEAD)
    sum_shape = (PAIRS, 8, 4 * HEAD)
    stat_shape = (PAIRS, 3, 2 * CHUNK, CHUNK)
    ends = [(state_shape, F32), (sum_shape, F32)][: len(entry)]
    return pl.pallas_call(
        functools.partial(forward_kernel, len(entry)),
        grid=(length // BLOCK,),
        in_specs=[
            row, HELD, SMEM, HELD, HELD, HELD, HELD, HELD, HELD, HELD, HELD,
        ] + [whole(array.shape) for array in entry],
        out_specs=[
            row, HELD, HELD, row, row, column, column,
            of_chunks(stat_shape), of_chunks(state_shape), of_chunks(sum_shape),
        ] + [whole(shape) for shape, _ in ends],
        out_shape=[
            sds((length, dim), BF16), sds((length, dim), F32), sds((length, dim), BF16),
            sds((length, dim), BF16), sds((length, dim), BF16),
            sds((dim, length), BF16), sds((dim, length), BF16),
            sds((chunks,) + stat_shape, F32),
            sds((chunks,) + state_shape, BF16), sds((chunks,) + sum_shape, F32),
        ] + [sds(*end) for end in ends],
        scratch_shapes=[
            pltpu.VMEM(state_shape, F32), pltpu.VMEM(sum_shape, F32),
            pltpu.VMEM((dim, CHUNK), BF16), pltpu.VMEM((dim, CHUNK), BF16),
            pltpu.VMEM((dim, dim), BF16), pltpu.VMEM((dim, dim), BF16),
        ],
        compiler_params=params(FORWARD_MIB),
        name="layer_forward",
    )(x, segments, place, gain_attn, gain_ffn, wq, wk, wv, wo, wu, wd, *entry)


SMEM = pl.BlockSpec(memory_space=pltpu.SMEM)
ANY = pl.BlockSpec(memory_space=pl.ANY)


def run_ffn_backward(dy, x1, a, gain_ffn, wo, wu, wd, core):
    length, dim = dy.shape
    ff = wu.shape[1]
    step_half = pl.BlockSpec((dim, dim), lambda i: (i, 0))
    return pl.pallas_call(
        ffn_backward_kernel,
        grid=(ff // dim,),
        in_specs=[
            FFN_IN, FFN_IN, FFN_IN, HELD, HELD,
            pl.BlockSpec((dim, dim), lambda i: (0, i)), step_half, SMEM,
        ],
        out_specs=[FFN_IN, FFN_IN, HELD, step_half, step_half, HELD, HELD],
        out_shape=[
            sds((length, dim), F32), sds((length, dim), BF16), sds((8, dim), F32),
            sds((ff, dim), BF16), sds((ff, dim), BF16),
            sds((dim // 2, dim), BF16), sds((dim // 2, dim), BF16),
        ],
        scratch_shapes=[
            pltpu.VMEM((length, dim), BF16), pltpu.VMEM((length, dim), F32),
            pltpu.VMEM((dim, dim), F32), pltpu.VMEM((dim, dim), F32),
        ],
        compiler_params=params(FFN_MIB),
        name="ffn_backward",
    )(dy, x1, a, gain_ffn, wo, wu, wd, core)


def run_attention_backward(
    after, through, x, dx1, da, h, q, k, v, stats, states, sums, segments, place,
    gain_attn, dgf, wq, wk, wv, entry,
):
    length, dim = x.shape
    half = 3 * dim // 2 + GAIN_ROWS
    steps = length // BLOCK
    back = lambda i: steps - 1 - i
    row = tokens_of(dim, back)
    column = pl.BlockSpec((dim, BLOCK), lambda i: (0, back(i)))
    per = BLOCK // CHUNK
    prev = pl.BlockSpec((dim, CHUNK), lambda i: (0, jnp.maximum(back(i) * per - 1, 0)))
    streams = [of_chunks(array.shape[1:], back) for array in (stats, states, sums)]
    r_shape = (PAIRS, 4 * HEAD, 4 * HEAD)
    rim_shape = (dim, CHUNK)
    ends = [r_shape, rim_shape, rim_shape][: len(entry)]
    kernel = functools.partial(attention_backward_kernel, len(entry))
    skip = len(after) + len(through)
    streamed = [x, q, h, k, v, k, v, stats, states, sums]
    held = [da, segments, dx1, place, gain_attn, dgf, wq, wk, wv, *entry]
    inputs = skip + len(streamed) + len(held)

    def body(*refs):
        kernel(*refs[skip:inputs], *refs[inputs + len(through) :])

    return pl.pallas_call(
        body,
        grid=(steps,),
        input_output_aliases={len(after) + n: n for n in range(len(through))},
        in_specs=[ANY] * skip + [row, row, row, column, column, prev, prev] + streams
        + [SMEM if array is place else HELD for array in held],
        out_specs=[ANY] * len(through) + [row, HELD, HELD] + [whole(shape) for shape in ends],
        out_shape=[sds(array.shape, array.dtype) for array in through] + [
            sds((length, dim), BF16), sds((half, dim), BF16), sds((half, dim), BF16),
        ] + [sds(shape, F32) for shape in ends],
        scratch_shapes=[
            pltpu.VMEM(r_shape, F32), pltpu.VMEM(rim_shape, F32), pltpu.VMEM(rim_shape, F32),
            pltpu.VMEM((BLOCK, dim), BF16), pltpu.VMEM((dim, BLOCK), BF16),
            pltpu.VMEM((dim, BLOCK), BF16),
            pltpu.VMEM((dim, dim), F32), pltpu.VMEM((dim, dim), F32), pltpu.VMEM((dim, dim), F32),
            pltpu.VMEM((8, dim), F32),
            pltpu.VMEM((dim, dim), BF16), pltpu.VMEM((dim, dim), BF16),
        ],
        compiler_params=params(ATTENTION_MIB),
        name="attention_backward",
    )(*after, *through, *streamed, *held)


def finish_ffn_kernel(core_ref, own_ref, other_ref, down_ref, up_ref, done_ref):
    half = down_ref.shape[0] // 2
    for ref, which in ((own_ref, core_ref[0]), (other_ref, 1 - core_ref[0])):
        rows = pl.ds(pl.multiple_of(which * half, half), half)
        down_ref[rows] = ref[:half].astype(F32)
        up_ref[rows] = ref[half:].astype(F32)
    done_ref[...] = jnp.zeros_like(done_ref)


def run_finish_ffn(core_ref, own, other, dim):
    ff = own.shape[0]
    block = pl.BlockSpec((dim, dim), lambda i: (i, 0))
    return pl.pallas_call(
        finish_ffn_kernel,
        grid=(ff // dim,),
        in_specs=[SMEM, block, block],
        out_specs=[block, pl.BlockSpec((dim, dim), lambda i: (0, i)), whole((8, 128))],
        out_shape=[sds((ff, dim), F32), sds((dim, ff), F32), sds((8, 128), F32)],
        compiler_params=params(12),
        name="finish_ffn",
    )(core_ref, own, other)


def finish_kernel(starts, core_ref, own_ref, other_ref, *out_refs):
    for at, out_ref in zip(starts, out_refs):
        half = out_ref.shape[0] // 2
        for ref, which in ((own_ref, core_ref[0]), (other_ref, 1 - core_ref[0])):
            rows = pl.ds(pl.multiple_of(which * half, half), half)
            out_ref[rows] = ref[at : at + half].astype(F32)


def run_finish(core_ref, own, other, starts, shape):
    return pl.pallas_call(
        functools.partial(finish_kernel, starts),
        in_specs=[SMEM, HELD, HELD],
        out_specs=[HELD] * len(starts),
        out_shape=[sds(shape, F32)] * len(starts),
        compiler_params=pltpu.CompilerParams(vmem_limit_bytes=12 * 1024 * 1024),
        name="finish",
    )(core_ref, own, other)


def partner(array, seq_bits, row_bits):
    seq_count, row_groups = lax.axis_size("seq"), lax.axis_size("rows")
    pairs = [
        (s * row_groups + r, (s ^ seq_bits) * row_groups + (r ^ row_bits))
        for s in range(seq_count)
        for r in range(row_groups)
    ]
    return lax.ppermute(array, ("seq", "rows"), pairs)


def add(*parts):
    parts = [part.astype(F32) for part in parts]
    if len(parts) == 4:
        return ((parts[0] + parts[1]) + (parts[2] + parts[3])).astype(BF16)
    return (parts[0] + parts[1]).astype(BF16)


def take(array, index, size):
    return lax.dynamic_slice_in_dim(array, index * size, size, 0)


PLANE_BITS = ((1, 0), (0, 2), (1, 2))
DEPTH_BITS = (2, 4)


def cut(total, place):
    size = total.shape[0] // 4
    return [take(total, place ^ d, size) for d in range(4)]


def traded(parts, all_bits):
    return [parts[0]] + [partner(part, *bits) for part, bits in zip(parts[1:], all_bits)]


def cut_half(total, bit):
    size = total.shape[0] // 2
    return [take(total, bit, size), take(total, 1 - bit, size)]


def joined_half(own, other, bit):
    return jnp.where(bit == 0, jnp.concatenate([own, other], 0), jnp.concatenate([other, own], 0))


def joined(parts, place):
    blocks = jnp.stack(parts)
    blocks = [lax.dynamic_index_in_dim(blocks, place ^ d, 0, False) for d in range(4)]
    return jnp.concatenate(blocks, 0)


def all_reduce(places, halves):
    core, plane, depth = places
    others = [partner(send, 0, 1) for _, send in halves]
    keeps = yield [keep for keep, _ in halves]
    sums = [add(keep, other) for keep, other in zip(keeps, others)]
    parts = yield cut(jnp.concatenate(sums, 0) if len(sums) > 1 else sums[0], plane)
    parts = traded(parts, PLANE_BITS)
    parts = yield parts
    total = add(*parts)
    for bits, bit in zip(DEPTH_BITS, depth):
        keep, send = yield cut_half(total, bit)
        other = partner(send, bits, 0)
        keep, other = yield [keep, other]
        total = add(keep, other)
    for bits in further_bits():
        total = add(total, partner(total, *bits))
    for bits, bit in reversed(list(zip(DEPTH_BITS, depth))):
        (total,) = yield [total]
        other = partner(total, bits, 0)
        total, other = yield [total, other]
        total = joined_half(total, other, bit)
    (block,) = yield [total]
    parts = traded([block] * 4, PLANE_BITS)
    parts = yield parts
    (own,) = yield [joined(parts, plane)]
    yield [own, partner(own, 0, 1)]


def gate(array, *others):
    return pl.pallas_call(
        lambda *refs: None,
        in_specs=[ANY] * (1 + len(others)),
        out_specs=ANY,
        out_shape=sds(array.shape, array.dtype),
        input_output_aliases={0: 0},
        compiler_params=pltpu.CompilerParams(vmem_limit_bytes=GATE_KIB * 1024),
        name="gate",
    )(array, *others)


class Reduction:
    def __init__(self, *args):
        self.steps = all_reduce(*args)
        self.arrays = next(self.steps)

    def step(self):
        self.arrays = self.steps.send(self.arrays)

    def run(self, count):
        for _ in range(count):
            self.step()

    def hold(self, *others):
        self.arrays[0] = gate(self.arrays[0], *others)


def further_bits():
    bits = []
    bit = 8
    while bit < lax.axis_size("seq"):
        bits.append((bit, 0))
        bit *= 2
    bit = 4
    while bit < lax.axis_size("rows"):
        bits.append((0, bit))
        bit *= 2
    return bits


def all_reduce_small(small):
    small = small + partner(small, 0, 1)
    for bits in (((1, 0), (0, 2), (1, 2)), ((2, 0), (4, 0), (6, 0))):
        got = [small] + [partner(small, *b) for b in bits]
        small = (got[0] + got[1]) + (got[2] + got[3])
    for b in further_bits():
        small = small + partner(small, *b)
    return small


def local(
    tokens, segments, gain_attn, gain_ffn, w_query, w_key, w_value, w_out, w_up, w_down, cotangent
):
    row_count, shard_len, dim = tokens.shape
    seq_count = lax.axis_size("seq")
    parts = seq_count // row_count
    groups = [[g * row_count + r for r in range(row_count)] for g in range(parts)]
    length = row_count * shard_len
    index = lax.axis_index("seq")
    my_row = index % row_count
    my_part = index // row_count

    def trade(array):
        return lax.all_to_all(
            array.reshape(row_count, shard_len, dim), "seq", 0, 0, axis_index_groups=groups
        )

    def shifted(arrays, by):
        pairs = [
            (i, i + by * row_count)
            for i in range(seq_count)
            if 0 <= i + by * row_count < seq_count
        ]
        return lax.ppermute(arrays, "seq", pairs)

    ga, gf = gain_attn.reshape(1, dim), gain_ffn.reshape(1, dim)
    seq_index, row_index = lax.axis_index("seq"), lax.axis_index("rows")
    core, plane = row_index % 2, seq_index % 2 + 2 * (row_index // 2 % 2)
    places = core, plane, (seq_index // 2 % 2, seq_index // 4 % 2)
    place = jnp.stack([my_row, my_part * (length // CHUNK), core]).astype(jnp.int32)

    x = trade(tokens).reshape(length, dim)
    dy = trade(cotangent).reshape(length, dim)
    entry = ()
    if parts > 1:
        rim_zero = jnp.zeros((dim, CHUNK), BF16)
        entry = (
            jnp.zeros((PAIRS, 4 * HEAD, 2 * HEAD), F32), jnp.zeros((PAIRS, 8, 4 * HEAD), F32),
            rim_zero, rim_zero,
        )
    for turn in range(parts):
        out, x1, a, h, q, k, v, stats, states, sums, *ends = run_forward(
            x, segments, place, ga, gf, w_query, w_key, w_value, w_out, w_up, w_down, entry
        )
        if turn < parts - 1:
            entry = shifted((*ends, k[:, length - CHUNK :], v[:, length - CHUNK :]), 1)
    output = trade(out)
    core_ref = place[2:]
    dx1, da, dgf, keep, send, keep_out, send_out = run_ffn_backward(
        dy, x1, a, gf, w_out, w_up, w_down, core_ref
    )
    ffn = Reduction(places, [(keep, send)])
    ffn.run(1)
    back = ()
    if parts > 1:
        rim = jnp.zeros((dim, CHUNK), F32)
        back = (jnp.zeros((PAIRS, 4 * HEAD, 4 * HEAD), F32), rim, rim)
    for turn in range(parts):
        through, after = [], []
        if turn == parts - 1:
            through, after = ffn.arrays[:1], ffn.arrays[1:]
        outs = run_attention_backward(
            after, through, x, dx1, da, h, q, k, v, stats, states, sums,
            segments, place, ga, dgf, w_query, w_key, w_value,
            back + entry[2:] if parts > 1 else (),
        )
        if turn < parts - 1:
            back = shifted(tuple(outs[3:]), -1)
    ffn.arrays[0], dx, keep, send = outs[:4]
    d_tokens = trade(dx)
    attention = Reduction(places, [(keep, send), (keep_out, send_out)])
    before = [output[0, :16, :128]]
    for n, name in enumerate(TAIL):
        reduction = ffn if name == "f" else attention
        if name == "f" or n != TAIL.index("a"):
            reduction.run(1)
        reduction.hold(*before)
        reduction.run(1)
        before = reduction.arrays[-3:] if len(reduction.arrays) < 4 else reduction.arrays[1:]
        if n == TRADED:
            before = before + [d_tokens[0, :16, :128]]
        if n == len(TAIL) - 2:
            ffn.run(1)
            dwd, dwu, finished = run_finish_ffn(core_ref, *ffn.arrays, dim)
            before = [finished]
    attention.run(1)
    own, other = attention.arrays
    half = dim // 2
    dwq, dwk, dwv, dwo = run_finish(
        core_ref, own, other, (0, half, 2 * half, 3 * half + GAIN_ROWS), (dim, dim)
    )
    at = 3 * dim // 2
    gains = jnp.where(core == 0, own[at : at + 2], other[at : at + 2]).astype(F32)
    return output, d_tokens, gains[0], gains[1], dwq, dwk, dwv, dwo, dwu, dwd


def solution(mesh):
    act = P("rows", "seq", None)
    return jax.shard_map(
        local,
        mesh=mesh,
        in_specs=(act, P("rows", None)) + (P(),) * 8 + (act,),
        out_specs=(act, act) + (P(),) * 8,
        check_vma=False,
    )
```

```python
import functools

import jax
import jax.numpy as jnp
from jax import lax
from jax.experimental import pallas as pl
from jax.experimental.pallas import tpu as pltpu
from jax.sharding import PartitionSpec as P

HEADS = 8
HEAD = 64
BAND = 30
EPSILON = 1e-06
SCALE = 0.125
CHUNK = 128
BLOCK = 256
PAIRS = HEADS // 2
NEG = -1e30
STEP_PAIRS = 2
GAIN_ROWS = 64
TAIL = "duadudAuaduaaduaduDUa"
GATE_KIB = 512
TRADE_AFTER = 13
TRADED = 18
FFN_ROWS = 2
FORWARD_MIB, FFN_MIB, ATTENTION_MIB = 52, 50, 54
GELU_A = 0.7978845608028654
GELU_B = 0.044715
F32 = jnp.float32
BF16 = jnp.bfloat16
VMEM_LIMIT = 56 * 1024 * 1024


def nn(a, b):
    return lax.dot_general(a, b, (((1,), (0,)), ((), ())), preferred_element_type=F32)


def nt(a, b):
    return lax.dot_general(a, b, (((1,), (1,)), ((), ())), preferred_element_type=F32)


def tn(a, b):
    return lax.dot_general(a, b, (((0,), (0,)), ((), ())), preferred_element_type=F32)


def low_lanes(shape):
    return lax.broadcasted_iota(jnp.int32, shape, len(shape) - 1) < HEAD


def split_heads(pair):
    low = low_lanes(pair.shape)
    zero = jnp.zeros_like(pair)
    return jnp.concatenate([jnp.where(low, pair, zero), jnp.where(low, zero, pair)], 0)


def pick(both):
    half = both.shape[0] // 2
    return jnp.where(low_lanes((half, both.shape[1])), both[:half], both[half:])


def over_lanes(column):
    half = column.shape[0] // 2
    return jnp.where(low_lanes((half, 2 * HEAD)), column[:half], column[half:])


def in_step(bodies):
    bodies = list(bodies)
    while bodies:
        bodies = [body for body in bodies if next(body, True) is None]


def features(t):
    expo = jnp.exp(jnp.minimum(t, 0.0))
    tanh = jnp.tanh(t)
    return (jnp.where(t > 0, t + 1.0, expo), 1.0 + tanh), (expo, 1.0 - tanh * tanh)


def head_mask(lanes):
    row = lax.broadcasted_iota(jnp.int32, (4 * HEAD, lanes), 0)
    lane = lax.broadcasted_iota(jnp.int32, (4 * HEAD, lanes), 1)
    head = (row // HEAD) % 2
    same = (lane < 2 * HEAD) & (lane // HEAD == head)
    return same | (lane == 2 * HEAD + row // HEAD)


def chunk_masks(seg_ref, place_ref, chunk):
    chunk = place_ref[1] + chunk

    def stretch(at):
        rows = seg_ref[:, pl.ds(pl.multiple_of(at * CHUNK, CHUNK), CHUNK)]
        mine = lax.broadcasted_iota(jnp.int32, rows.shape, 0) == place_ref[0]
        return jnp.max(jnp.where(mine, rows, -1), 0, keepdims=True).astype(F32)

    seg_own = stretch(chunk)
    seg_prev = jnp.where(chunk == 0, -1.0, stretch(jnp.maximum(chunk - 1, 0)))
    seg_q = jnp.broadcast_to(seg_own, (CHUNK, CHUNK)).T
    row = lax.broadcasted_iota(jnp.int32, (CHUNK, CHUNK), 0)
    col = lax.broadcasted_iota(jnp.int32, (CHUNK, CHUNK), 1)
    gap = row - col
    far = (seg_q == seg_own) & (gap >= 0)
    band_own = far & (gap <= BAND)
    band_prev = (seg_q == seg_prev) & (gap + CHUNK <= BAND)
    band = jnp.concatenate([band_prev, band_own], 1)
    before = seg_prev[:, CHUNK - 1 :]
    last = seg_own[:, CHUNK - 1 :]
    carry = (seg_q[:, :1] == before).astype(F32)
    tail = (seg_own == last).astype(BF16)
    keep = (before == last).astype(F32)
    return jnp.concatenate([band, band], 0), jnp.concatenate([far, far], 0), carry, tail, keep


def start_with(refs, entry_refs):
    for n, ref in enumerate(refs):
        ref[...] = entry_refs[n][...] if entry_refs else jnp.zeros_like(ref)


def forward_kernel(entries, *refs):
    (x_ref, seg_ref, place_ref, ga_ref, gf_ref, wq_ref, wk_ref, wv_ref, wo_ref, wu_ref, wd_ref,
     *refs) = refs
    entry_refs, refs = refs[:entries], refs[entries:]
    (out_ref, x1_ref, a_ref, h_ref, q_ref, k_ref, v_ref, stats_ref, states_ref, sums_ref,
     *refs) = refs
    end_refs, refs = refs[: min(entries, 2)], refs[min(entries, 2) :]
    s_ref, z_ref, kp_ref, vp_ref, wkt_ref, wvt_ref = refs
    step = pl.program_id(0)

    @pl.when(step == 0)
    def _():
        start_with((s_ref, z_ref, kp_ref, vp_ref), entry_refs)
        wkt_ref[...] = wk_ref[...].T
        wvt_ref[...] = wv_ref[...].T

    block = pl.ds(pl.multiple_of(step * BLOCK, BLOCK), BLOCK)
    x = x_ref[...].astype(F32)
    inv = lax.rsqrt(jnp.mean(x * x, -1, keepdims=True) + EPSILON)
    hidden = (x * inv * ga_ref[...]).astype(BF16)
    h_ref[...] = hidden
    q_ref[...] = nn(hidden, wq_ref[...]).astype(BF16)
    k_ref[...] = nt(wkt_ref[...], hidden).astype(BF16)
    v_ref[...] = nt(wvt_ref[...], hidden).astype(BF16)
    same_head = head_mask(CHUNK)
    for sub in range(BLOCK // CHUNK):
        chunk = step * (BLOCK // CHUNK) + sub
        rows = slice(sub * CHUNK, (sub + 1) * CHUNK)
        tokens = pl.ds(pl.multiple_of(chunk * CHUNK, CHUNK), CHUNK)
        band, far_mask, carry, tail, keep = chunk_masks(seg_ref, place_ref, chunk)
        tail_rows = jnp.broadcast_to(tail, (16, CHUNK))

        def body(p):
            lanes = slice(p * 128, (p + 1) * 128)
            qp = q_ref[rows, lanes]
            kt = k_ref[lanes, rows]
            vt = v_ref[lanes, rows]
            kt_ext = jnp.concatenate([kp_ref[lanes], kt], 1)
            vt_ext = jnp.concatenate([vp_ref[lanes], vt], 1)
            score = nn(split_heads(qp * SCALE), kt_ext)
            fq, _ = features(qp.astype(F32))
            fk, _ = features(kt.astype(F32))
            fk = [f.astype(BF16) for f in fk]
            fq = [f.astype(BF16) for f in fq]
            yield
            part = [
                jnp.where(far_mask, nn(split_heads(fq[m]), fk[m]), 0.0) for m in range(2)
            ]
            score = jnp.where(band, score, NEG)
            top = jnp.max(score, -1, keepdims=True)
            yield
            state = s_ref[p]
            state_low = state.astype(BF16)
            sums = z_ref[p]
            states_ref[sub, p] = state_low
            sums_ref[sub, p] = sums
            fk_both = jnp.concatenate(fk, 0)
            update = nt(fk_both * tail, vt)
            s_ref[p] = keep * state + jnp.where(same_head, update, 0.0)
            z_ref[p] = keep * sums + nt(tail_rows, fk_both)[:8]
            expo = jnp.exp(score - top)
            total = jnp.sum(expo, -1, keepdims=True)
            yield
            inv_total = 1.0 / total
            prob_prev = (expo[:, :CHUNK] * inv_total).astype(BF16)
            weight = expo[:, CHUNK:] * inv_total
            columns = [top + jnp.log(total)]
            scaled = []
            for m in range(2):
                fq_carry = fq[m].astype(F32) * carry
                entered = split_heads(fq_carry * sums[:1, m * 128 : (m + 1) * 128])
                inv_z = 1.0 / jnp.sum(part[m] + entered, -1, keepdims=True)
                columns.append(inv_z)
                weight = weight + part[m] * inv_z
                scaled.append((fq_carry * over_lanes(inv_z)).astype(BF16))
            both = jnp.concatenate([prob_prev, weight.astype(BF16)], 1)
            yield
            attended = pick(nt(both, vt_ext)) + nn(jnp.concatenate(scaled, 1), state_low)
            a_ref[tokens, lanes] = attended.astype(BF16)
            for n, column in enumerate(columns):
                stats_ref[sub, p, n] = jnp.broadcast_to(column, (2 * CHUNK, CHUNK))

        for first in range(0, PAIRS, STEP_PAIRS):
            in_step(body(p) for p in range(first, first + STEP_PAIRS))
        kp_ref[...] = k_ref[:, rows]
        vp_ref[...] = v_ref[:, rows]
    for end_ref, ref in zip(end_refs, (s_ref, z_ref)):
        end_ref[...] = ref[...]
    x1 = x + nn(a_ref[block], wo_ref[...])
    x1_ref[block] = x1
    inv = lax.rsqrt(jnp.mean(x1 * x1, -1, keepdims=True) + EPSILON)
    hidden = (x1 * inv * gf_ref[...]).astype(BF16)
    total = x1
    width = 512
    for f in range(wu_ref.shape[1] // width):
        cols = slice(f * width, (f + 1) * width)
        up = nn(hidden, wu_ref[:, cols])
        act = 0.5 * up * (1.0 + jnp.tanh(GELU_A * (up + GELU_B * up * up * up)))
        total = total + nn(act.astype(BF16), wd_ref[cols])
    out_ref[...] = total.astype(BF16)


def norm_backward(x, gain, grad):
    inv = lax.rsqrt(jnp.mean(x * x, -1, keepdims=True) + EPSILON)
    unit = x * inv
    scaled = grad * gain
    d_gain = jnp.sum(grad * unit, 0, keepdims=True)
    return inv * (scaled - unit * jnp.mean(unit * scaled, -1, keepdims=True)), d_gain


def ffn_backward_kernel(
    dy_ref, x1_ref, a_ref, gf_ref, wo_ref, wu_ref, wd_ref, core_ref,
    dx1_ref, da_ref, dg_ref, keep_ref, send_ref, keep_out_ref, send_out_ref,
    hidden_ref, dh_ref, dwd_ref, dwu_ref,
):
    step = pl.program_id(0)
    core = core_ref[0]
    gain = gf_ref[...]

    @pl.when(step == 0)
    def _():
        x1 = x1_ref[...]
        inv = lax.rsqrt(jnp.mean(x1 * x1, -1, keepdims=True) + EPSILON)
        hidden_ref[...] = (x1 * inv * gain).astype(BF16)
        dh_ref[...] = jnp.zeros_like(dh_ref)

    for part in range(FFN_ROWS):
        size = dy_ref.shape[0] // FFN_ROWS
        rows = slice(part * size, (part + 1) * size)
        dy = dy_ref[rows]
        hidden = hidden_ref[rows]
        up = nn(hidden, wu_ref[...])
        square = up * up
        tanh = jnp.tanh(GELU_A * up * (1.0 + GELU_B * square))
        half = 0.5 * (1.0 + tanh)
        act = (up * half).astype(BF16)
        slope = half + 0.5 * up * (1.0 - tanh * tanh) * (
            GELU_A + (3.0 * GELU_A * GELU_B) * square
        )
        d_up = (slope * nt(dy, wd_ref[...])).astype(BF16)
        dh_ref[rows] += nt(d_up, wu_ref[...])
        dwd, dwu = tn(act, dy), tn(hidden, d_up)
        if part:
            dwd, dwu = dwd + dwd_ref[...], dwu + dwu_ref[...]
        dwd_ref[...], dwu_ref[...] = dwd, dwu
    put_halves((dwd_ref, dwu_ref), core, keep_ref, send_ref)

    @pl.when(step == pl.num_programs(0) - 1)
    def _():
        x1 = x1_ref[...]
        d_norm, d_gain = norm_backward(x1, gain, dh_ref[...])
        dx1 = dy_ref[...].astype(F32) + d_norm
        dg_ref[...] = jnp.broadcast_to(d_gain, dg_ref.shape)
        dx1_ref[...] = dx1
        d_branch = dx1.astype(BF16)
        da_ref[...] = nt(d_branch, wo_ref[...]).astype(BF16)
        dwd_ref[...] = tn(a_ref[...], d_branch)
        put_halves((dwd_ref,), core, keep_out_ref, send_out_ref)


def put_halves(sums, core, keep_ref, send_ref):
    at = 0
    for total in sums:
        half = total.shape[0] // 2
        for ref, which in ((keep_ref, core), (send_ref, 1 - core)):
            rows = total[pl.ds(pl.multiple_of(which * half, half), half)]
            ref[at : at + half] = rows.astype(BF16)
        at += half
    return at


def attention_backward_kernel(entries, *refs):
    (x_ref, q_ref, h_ref, k_ref, v_ref, kprev_ref, vprev_ref, stats_ref, states_ref, sums_ref,
     da_ref, seg_ref, dx1_ref, place_ref, ga_ref, dgf_ref, wq_ref, wk_ref, wv_ref, *refs) = refs
    entry_refs, refs = refs[:entries], refs[entries:]
    dx_ref, keep_ref, send_ref, *refs = refs
    end_refs, refs = refs[: min(entries, 3)], refs[min(entries, 3) :]
    (r_ref, dkc_ref, dvc_ref, dq_ref, dk_ref, dv_ref, dwq_acc, dwk_acc, dwv_acc, dg_acc,
     wkt_ref, wvt_ref) = refs
    step = pl.program_id(0)
    block = pl.num_programs(0) - 1 - step

    @pl.when(step == 0)
    def _():
        start_with((r_ref, dkc_ref, dvc_ref), entry_refs)
        dwq_acc[...] = jnp.zeros_like(dwq_acc)
        dwk_acc[...] = jnp.zeros_like(dwk_acc)
        dwv_acc[...] = jnp.zeros_like(dwv_acc)
        dg_acc[...] = jnp.zeros_like(dg_acc)
        wkt_ref[...] = wk_ref[...].T
        wvt_ref[...] = wv_ref[...].T

    lane = lax.broadcasted_iota(jnp.int32, (CHUNK, CHUNK), 1)
    same_head = head_mask(2 * CHUNK)
    for sub in reversed(range(BLOCK // CHUNK)):
        chunk = block * (BLOCK // CHUNK) + sub
        rows = slice(sub * CHUNK, (sub + 1) * CHUNK)
        tokens = pl.ds(pl.multiple_of(chunk * CHUNK, CHUNK), CHUNK)
        band, far_mask, carry, tail, keep = chunk_masks(seg_ref, place_ref, chunk)
        tail_rows = jnp.broadcast_to(tail, (CHUNK, CHUNK))

        def body(p):
            lanes = slice(p * 128, (p + 1) * 128)
            qp = q_ref[rows, lanes]
            da = da_ref[tokens, lanes]
            kt = k_ref[lanes, rows]
            vt = v_ref[lanes, rows]
            if sub == 0:
                kt_prev, vt_prev = kprev_ref[lanes], vprev_ref[lanes]
                if entry_refs:
                    kt_prev = jnp.where(block == 0, entry_refs[3][lanes], kt_prev)
                    vt_prev = jnp.where(block == 0, entry_refs[4][lanes], vt_prev)
            else:
                before = slice((sub - 1) * CHUNK, sub * CHUNK)
                kt_prev, vt_prev = k_ref[lanes, before], v_ref[lanes, before]
            kt_ext = jnp.concatenate([kt_prev, kt], 1)
            vt_ext = jnp.concatenate([vt_prev, vt], 1)
            q2 = split_heads(qp * SCALE)
            da2 = split_heads(da)
            score = nn(q2, kt_ext)
            d_prob = nn(da2, vt_ext)
            yield
            state = states_ref[sub, p]
            sums = sums_ref[sub, p]
            back = r_ref[p]
            back_low = back.astype(BF16)
            from_state = nt(da, state) * carry
            to_later = nn(back_low, jnp.concatenate([vt * tail, tail_rows], 0))
            fq, slope_q = features(qp.astype(F32))
            fk, slope_k = features(kt.astype(F32))
            fk = [f.astype(BF16) for f in fk]
            fq = [f.astype(BF16) for f in fq]
            fq2 = [split_heads(f) for f in fq]
            yield
            part = [jnp.where(far_mask, nn(fq2[m], fk[m]), 0.0) for m in range(2)]
            lse = stats_ref[sub, p, 0]
            prob = jnp.exp(jnp.where(band, score - jnp.concatenate([lse, lse], 1), NEG))
            delta = jnp.sum(prob * d_prob, -1, keepdims=True)
            d_score = (prob * (d_prob - delta)).astype(BF16)
            yield
            dq = SCALE * pick(nt(d_score, kt_ext))
            dk_ext = tn(q2, d_score)
            dk = dk_ext[:, CHUNK:] + dkc_ref[lanes]
            dkc_ref[lanes] = dk_ext[:, :CHUNK]
            d_own = d_prob[:, CHUNK:]
            weight = prob[:, CHUNK:]
            yield
            scaled = []
            d_part = []
            entries = []
            right = jnp.zeros((CHUNK, CHUNK), F32)
            for m in range(2):
                part_lanes = slice(m * 128, (m + 1) * 128)
                fq_wide = fq[m].astype(F32)
                inv_z = stats_ref[sub, p, m + 1]
                weighted = part[m] * inv_z
                weight = weight + weighted
                entered = from_state[:, part_lanes]
                inv_wide = pick(inv_z)
                taken = fq_wide * inv_wide
                dot = jnp.sum(
                    weighted * d_own + split_heads(taken * entered), -1, keepdims=True
                )
                d_part.append(jnp.where(far_mask, (d_own - dot) * inv_z, 0.0).astype(BF16))
                entries.append(
                    inv_wide * (entered - over_lanes(dot) * (carry * sums[:1, part_lanes]))
                )
                scaled.append((taken * carry).astype(BF16))
                right = jnp.where(lane == 2 * m, -dot[:CHUNK], right)
                right = jnp.where(lane == 2 * m + 1, -dot[CHUNK:], right)
            both = jnp.concatenate([prob[:, :CHUNK].astype(BF16), weight.astype(BF16)], 1)
            yield
            dv_ext = tn(da2, both)
            dv = dv_ext[:, CHUNK:] + dvc_ref[lanes]
            dv = dv + tn(back_low[:, :CHUNK], jnp.concatenate(fk, 0) * tail)
            dvc_ref[lanes] = dv_ext[:, :CHUNK]
            update = tn(
                jnp.concatenate(scaled, 1), jnp.concatenate([da, right.astype(BF16)], 1)
            )
            r_ref[p] = keep * back + jnp.where(same_head, update, 0.0)
            dv_ref[lanes, rows] = dv.astype(BF16)
            yield
            for m in range(2):
                dq = dq + slope_q[m] * (pick(nt(d_part[m], fk[m])) + entries[m])
                dk = dk + slope_k[m] * (
                    tn(fq2[m], d_part[m]) + to_later[m * 128 : (m + 1) * 128]
                )
            dq_ref[rows, lanes] = dq.astype(BF16)
            dk_ref[lanes, rows] = dk.astype(BF16)

        for first in range(0, PAIRS, STEP_PAIRS):
            in_step(body(p) for p in range(first, first + STEP_PAIRS))
    for end_ref, ref in zip(end_refs, (r_ref, dkc_ref, dvc_ref)):
        end_ref[...] = ref[...]
    dim = x_ref.shape[1]
    tokens = pl.ds(pl.multiple_of(block * BLOCK, BLOCK), BLOCK)
    hidden_t = h_ref[...].T
    dq, dk, dv = dq_ref[...], dk_ref[...], dv_ref[...]
    dwq_acc[...] += nn(hidden_t, dq)
    dwk_acc[...] += nt(hidden_t, dk)
    dwv_acc[...] += nt(hidden_t, dv)
    d_hidden = nt(dq, wq_ref[...]) + tn(dk, wkt_ref[...]) + tn(dv, wvt_ref[...])
    d_norm, d_gain = norm_backward(x_ref[...].astype(F32), ga_ref[...], d_hidden)
    dg_acc[...] += jnp.broadcast_to(d_gain, dg_acc.shape)
    dx_ref[...] = (dx1_ref[tokens] + d_norm).astype(BF16)

    @pl.when(step == pl.num_programs(0) - 1)
    def _():
        core = place_ref[2]
        at = put_halves((dwq_acc, dwk_acc, dwv_acc), core, keep_ref, send_ref)
        keep_ref[at:] = jnp.zeros((GAIN_ROWS, keep_ref.shape[1]), BF16)
        send_ref[at:] = jnp.zeros((GAIN_ROWS, keep_ref.shape[1]), BF16)
        gains = jnp.concatenate([dg_acc[:1], dgf_ref[:1], jnp.zeros((14, dim), F32)], 0)
        keep_ref[at : at + 16] = jnp.where(core == 0, gains, 0.0).astype(BF16)
        send_ref[at : at + 16] = jnp.where(core == 0, 0.0, gains).astype(BF16)


HELD = pl.BlockSpec(memory_space=pltpu.VMEM)


def whole(shape):
    return pl.BlockSpec(shape, lambda i: (0,) * len(shape))


FFN_IN = HELD


def tokens_of(width, index=lambda i: i):
    return pl.BlockSpec((BLOCK, width), lambda i: (index(i), 0))


def of_chunks(shape, index=lambda i: i):
    return pl.BlockSpec((BLOCK // CHUNK,) + shape, lambda i: (index(i),) + (0,) * len(shape))


def params(mib):
    return pltpu.CompilerParams(
        vmem_limit_bytes=mib * 1024 * 1024, dimension_semantics=("arbitrary",)
    )


def sds(shape, dtype):
    return jax.ShapeDtypeStruct(shape, dtype)


def run_forward(x, segments, place, gain_attn, gain_ffn, wq, wk, wv, wo, wu, wd, entry):
    length, dim = x.shape
    ff = wu.shape[1]
    chunks = length // CHUNK
    row = tokens_of(dim)
    column = pl.BlockSpec((dim, BLOCK), lambda i: (0, i))
    state_shape = (PAIRS, 4 * HEAD, 2 * HEAD)
    sum_shape = (PAIRS, 8, 4 * HEAD)
    stat_shape = (PAIRS, 3, 2 * CHUNK, CHUNK)
    ends = [(state_shape, F32), (sum_shape, F32)][: len(entry)]
    return pl.pallas_call(
        functools.partial(forward_kernel, len(entry)),
        grid=(length // BLOCK,),
        in_specs=[
            row, HELD, SMEM, HELD, HELD, HELD, HELD, HELD, HELD, HELD, HELD,
        ] + [whole(array.shape) for array in entry],
        out_specs=[
            row, HELD, HELD, row, row, column, column,
            of_chunks(stat_shape), of_chunks(state_shape), of_chunks(sum_shape),
        ] + [whole(shape) for shape, _ in ends],
        out_shape=[
            sds((length, dim), BF16), sds((length, dim), F32), sds((length, dim), BF16),
            sds((length, dim), BF16), sds((length, dim), BF16),
            sds((dim, length), BF16), sds((dim, length), BF16),
            sds((chunks,) + stat_shape, F32),
            sds((chunks,) + state_shape, BF16), sds((chunks,) + sum_shape, F32),
        ] + [sds(*end) for end in ends],
        scratch_shapes=[
            pltpu.VMEM(state_shape, F32), pltpu.VMEM(sum_shape, F32),
            pltpu.VMEM((dim, CHUNK), BF16), pltpu.VMEM((dim, CHUNK), BF16),
            pltpu.VMEM((dim, dim), BF16), pltpu.VMEM((dim, dim), BF16),
        ],
        compiler_params=params(FORWARD_MIB),
        name="layer_forward",
    )(x, segments, place, gain_attn, gain_ffn, wq, wk, wv, wo, wu, wd, *entry)


SMEM = pl.BlockSpec(memory_space=pltpu.SMEM)
ANY = pl.BlockSpec(memory_space=pl.ANY)


def run_ffn_backward(dy, x1, a, gain_ffn, wo, wu, wd, core):
    length, dim = dy.shape
    ff = wu.shape[1]
    step_half = pl.BlockSpec((dim, dim), lambda i: (i, 0))
    return pl.pallas_call(
        ffn_backward_kernel,
        grid=(ff // dim,),
        in_specs=[
            FFN_IN, FFN_IN, FFN_IN, HELD, HELD,
            pl.BlockSpec((dim, dim), lambda i: (0, i)), step_half, SMEM,
        ],
        out_specs=[FFN_IN, FFN_IN, HELD, step_half, step_half, HELD, HELD],
        out_shape=[
            sds((length, dim), F32), sds((length, dim), BF16), sds((8, dim), F32),
            sds((ff, dim), BF16), sds((ff, dim), BF16),
            sds((dim // 2, dim), BF16), sds((dim // 2, dim), BF16),
        ],
        scratch_shapes=[
            pltpu.VMEM((length, dim), BF16), pltpu.VMEM((length, dim), F32),
            pltpu.VMEM((dim, dim), F32), pltpu.VMEM((dim, dim), F32),
        ],
        compiler_params=params(FFN_MIB),
        name="ffn_backward",
    )(dy, x1, a, gain_ffn, wo, wu, wd, core)


def run_attention_backward(
    after, through, x, dx1, da, h, q, k, v, stats, states, sums, segments, place,
    gain_attn, dgf, wq, wk, wv, entry,
):
    length, dim = x.shape
    half = 3 * dim // 2 + GAIN_ROWS
    steps = length // BLOCK
    back = lambda i: steps - 1 - i
    row = tokens_of(dim, back)
    column = pl.BlockSpec((dim, BLOCK), lambda i: (0, back(i)))
    per = BLOCK // CHUNK
    prev = pl.BlockSpec((dim, CHUNK), lambda i: (0, jnp.maximum(back(i) * per - 1, 0)))
    streams = [of_chunks(array.shape[1:], back) for array in (stats, states, sums)]
    r_shape = (PAIRS, 4 * HEAD, 4 * HEAD)
    rim_shape = (dim, CHUNK)
    ends = [r_shape, rim_shape, rim_shape][: len(entry)]
    kernel = functools.partial(attention_backward_kernel, len(entry))
    skip = len(after) + len(through)
    streamed = [x, q, h, k, v, k, v, stats, states, sums]
    held = [da, segments, dx1, place, gain_attn, dgf, wq, wk, wv, *entry]
    inputs = skip + len(streamed) + len(held)

    def body(*refs):
        kernel(*refs[skip:inputs], *refs[inputs + len(through) :])

    return pl.pallas_call(
        body,
        grid=(steps,),
        input_output_aliases={len(after) + n: n for n in range(len(through))},
        in_specs=[ANY] * skip + [row, row, row, column, column, prev, prev] + streams
        + [SMEM if array is place else HELD for array in held],
        out_specs=[ANY] * len(through) + [row, HELD, HELD] + [whole(shape) for shape in ends],
        out_shape=[sds(array.shape, array.dtype) for array in through] + [
            sds((length, dim), BF16), sds((half, dim), BF16), sds((half, dim), BF16),
        ] + [sds(shape, F32) for shape in ends],
        scratch_shapes=[
            pltpu.VMEM(r_shape, F32), pltpu.VMEM(rim_shape, F32), pltpu.VMEM(rim_shape, F32),
            pltpu.VMEM((BLOCK, dim), BF16), pltpu.VMEM((dim, BLOCK), BF16),
            pltpu.VMEM((dim, BLOCK), BF16),
            pltpu.VMEM((dim, dim), F32), pltpu.VMEM((dim, dim), F32), pltpu.VMEM((dim, dim), F32),
            pltpu.VMEM((8, dim), F32),
            pltpu.VMEM((dim, dim), BF16), pltpu.VMEM((dim, dim), BF16),
        ],
        compiler_params=params(ATTENTION_MIB),
        name="attention_backward",
    )(*after, *through, *streamed, *held)


def finish_ffn_kernel(core_ref, own_ref, other_ref, out_ref, done_ref):
    half = out_ref.shape[0] // 2
    for ref, which in ((own_ref, core_ref[0]), (other_ref, 1 - core_ref[0])):
        rows = pl.ds(pl.multiple_of(which * half, half), half)
        out_ref[rows] = ref[...].astype(F32)
    done_ref[...] = jnp.zeros_like(done_ref)


def run_finish_ffn(core_ref, own, other, across):
    dim = own.shape[1]
    ff = own.shape[0] * 2
    block = pl.BlockSpec((dim // 2, dim), lambda i: (i, 0))
    return pl.pallas_call(
        finish_ffn_kernel,
        grid=(ff // dim,),
        in_specs=[SMEM, block, block],
        out_specs=[
            pl.BlockSpec((dim, dim), (lambda i: (0, i)) if across else (lambda i: (i, 0))),
            whole((8, 128)),
        ],
        out_shape=[sds((dim, ff) if across else (ff, dim), F32), sds((8, 128), F32)],
        compiler_params=params(12),
        name="finish_ffn",
    )(core_ref, own, other)


def finish_kernel(starts, core_ref, own_ref, other_ref, *out_refs):
    for at, out_ref in zip(starts, out_refs):
        half = out_ref.shape[0] // 2
        for ref, which in ((own_ref, core_ref[0]), (other_ref, 1 - core_ref[0])):
            rows = pl.ds(pl.multiple_of(which * half, half), half)
            out_ref[rows] = ref[at : at + half].astype(F32)


def run_finish(core_ref, own, other, starts, shape):
    return pl.pallas_call(
        functools.partial(finish_kernel, starts),
        in_specs=[SMEM, HELD, HELD],
        out_specs=[HELD] * len(starts),
        out_shape=[sds(shape, F32)] * len(starts),
        compiler_params=pltpu.CompilerParams(vmem_limit_bytes=12 * 1024 * 1024),
        name="finish",
    )(core_ref, own, other)


def partner(array, seq_bits, row_bits):
    seq_count, row_groups = lax.axis_size("seq"), lax.axis_size("rows")
    pairs = [
        (s * row_groups + r, (s ^ seq_bits) * row_groups + (r ^ row_bits))
        for s in range(seq_count)
        for r in range(row_groups)
    ]
    return lax.ppermute(array, ("seq", "rows"), pairs)


def add(*parts):
    parts = [part.astype(F32) for part in parts]
    if len(parts) == 4:
        return ((parts[0] + parts[1]) + (parts[2] + parts[3])).astype(BF16)
    return (parts[0] + parts[1]).astype(BF16)


def take(array, index, size):
    return lax.dynamic_slice_in_dim(array, index * size, size, 0)


PLANE_BITS = ((1, 0), (0, 2), (1, 2))
DEPTH_BITS = (2, 4)


def cut(total, place):
    size = total.shape[0] // 4
    return [take(total, place ^ d, size) for d in range(4)]


def traded(parts, all_bits):
    return [parts[0]] + [partner(part, *bits) for part, bits in zip(parts[1:], all_bits)]


def cut_half(total, bit):
    size = total.shape[0] // 2
    return [take(total, bit, size), take(total, 1 - bit, size)]


def joined_half(own, other, bit):
    return jnp.where(bit == 0, jnp.concatenate([own, other], 0), jnp.concatenate([other, own], 0))


def joined(parts, place):
    blocks = jnp.stack(parts)
    blocks = [lax.dynamic_index_in_dim(blocks, place ^ d, 0, False) for d in range(4)]
    return jnp.concatenate(blocks, 0)


def sum_planes(places, halves):
    core, plane, depth = places
    others = [partner(send, 0, 1) for _, send in halves]
    keeps = yield [keep for keep, _ in halves]
    sums = [add(keep, other) for keep, other in zip(keeps, others)]
    parts = yield cut(jnp.concatenate(sums, 0) if len(sums) > 1 else sums[0], plane)
    parts = traded(parts, PLANE_BITS)
    parts = yield parts
    yield [add(*parts)]


def sum_depth_and_gather(places, total):
    core, plane, depth = places
    (total,) = yield [total]
    for n, (bits, bit) in enumerate(zip(DEPTH_BITS, depth)):
        keep, send = yield cut_half(total, bit)
        other = partner(send, bits, 0)
        keep, other = yield [keep, other]
        total = add(keep, other)
    for bits in further_bits():
        total = add(total, partner(total, *bits))
    for bits, bit in reversed(list(zip(DEPTH_BITS, depth))):
        (total,) = yield [total]
        other = partner(total, bits, 0)
        total, other = yield [total, other]
        total = joined_half(total, other, bit)
    (block,) = yield [total]
    parts = traded([block] * 4, PLANE_BITS)
    parts = yield parts
    (own,) = yield [joined(parts, plane)]
    yield [own, partner(own, 0, 1)]


def gate(array, *others):
    return pl.pallas_call(
        lambda *refs: None,
        in_specs=[ANY] * (1 + len(others)),
        out_specs=ANY,
        out_shape=sds(array.shape, array.dtype),
        input_output_aliases={0: 0},
        compiler_params=pltpu.CompilerParams(vmem_limit_bytes=GATE_KIB * 1024),
        name="gate",
    )(array, *others)


def settled(array):
    def kernel(in_ref, out_ref, done_ref):
        out_ref[...] = in_ref[...]
        done_ref[...] = jnp.zeros_like(done_ref)

    block = pl.BlockSpec((1,) + array.shape[1:], lambda i: (i, 0, 0))
    return pl.pallas_call(
        kernel,
        grid=(array.shape[0],),
        in_specs=[block],
        out_specs=[block, whole((8, 128))],
        out_shape=[sds(array.shape, array.dtype), sds((8, 128), F32)],
        compiler_params=params(2),
        name="settled",
    )(array)


class Reduction:
    def __init__(self, steps):
        self.steps = steps
        self.arrays = next(steps)
        self.waits = False

    def step(self):
        self.arrays = self.steps.send(self.arrays)

    def turn(self, before):
        if self.waits:
            self.step()
        if before:
            self.arrays[0] = gate(self.arrays[0], *before)
        self.step()
        self.waits = True
        return self.arrays[1:] or self.arrays


def further_bits():
    bits = []
    bit = 8
    while bit < lax.axis_size("seq"):
        bits.append((bit, 0))
        bit *= 2
    bit = 4
    while bit < lax.axis_size("rows"):
        bits.append((0, bit))
        bit *= 2
    return bits


def all_reduce_small(small):
    small = small + partner(small, 0, 1)
    for bits in (((1, 0), (0, 2), (1, 2)), ((2, 0), (4, 0), (6, 0))):
        got = [small] + [partner(small, *b) for b in bits]
        small = (got[0] + got[1]) + (got[2] + got[3])
    for b in further_bits():
        small = small + partner(small, *b)
    return small


def local(
    tokens, segments, gain_attn, gain_ffn, w_query, w_key, w_value, w_out, w_up, w_down, cotangent
):
    row_count, shard_len, dim = tokens.shape
    seq_count = lax.axis_size("seq")
    parts = seq_count // row_count
    groups = [[g * row_count + r for r in range(row_count)] for g in range(parts)]
    length = row_count * shard_len
    index = lax.axis_index("seq")
    my_row = index % row_count
    my_part = index // row_count

    def trade(array):
        return lax.all_to_all(
            array.reshape(row_count, shard_len, dim), "seq", 0, 0, axis_index_groups=groups
        )

    def shifted(arrays, by):
        pairs = [
            (i, i + by * row_count)
            for i in range(seq_count)
            if 0 <= i + by * row_count < seq_count
        ]
        return lax.ppermute(arrays, "seq", pairs)

    ga, gf = gain_attn.reshape(1, dim), gain_ffn.reshape(1, dim)
    seq_index, row_index = lax.axis_index("seq"), lax.axis_index("rows")
    core, plane = row_index % 2, seq_index % 2 + 2 * (row_index // 2 % 2)
    places = core, plane, (seq_index // 2 % 2, seq_index // 4 % 2)
    place = jnp.stack([my_row, my_part * (length // CHUNK), core]).astype(jnp.int32)

    x = trade(tokens).reshape(length, dim)
    dy = trade(cotangent).reshape(length, dim)
    entry = ()
    if parts > 1:
        rim_zero = jnp.zeros((dim, CHUNK), BF16)
        entry = (
            jnp.zeros((PAIRS, 4 * HEAD, 2 * HEAD), F32), jnp.zeros((PAIRS, 8, 4 * HEAD), F32),
            rim_zero, rim_zero,
        )
    for turn in range(parts):
        out, x1, a, h, q, k, v, stats, states, sums, *ends = run_forward(
            x, segments, place, ga, gf, w_query, w_key, w_value, w_out, w_up, w_down, entry
        )
        if turn < parts - 1:
            entry = shifted((*ends, k[:, length - CHUNK :], v[:, length - CHUNK :]), 1)
    output = trade(out)
    core_ref = place[2:]
    dx1, da, dgf, keep, send, keep_out, send_out = run_ffn_backward(
        dy, x1, a, gf, w_out, w_up, w_down, core_ref
    )
    ffn = Reduction(sum_planes(places, [(keep, send)]))
    ffn.step()
    back = ()
    if parts > 1:
        rim = jnp.zeros((dim, CHUNK), F32)
        back = (jnp.zeros((PAIRS, 4 * HEAD, 4 * HEAD), F32), rim, rim)
    for turn in range(parts):
        through, after = [], []
        if turn == parts - 1:
            through, after = ffn.arrays[:1], ffn.arrays[1:]
        outs = run_attention_backward(
            after, through, x, dx1, da, h, q, k, v, stats, states, sums,
            segments, place, ga, dgf, w_query, w_key, w_value,
            back + entry[2:] if parts > 1 else (),
        )
        if turn < parts - 1:
            back = shifted(tuple(outs[3:]), -1)
    ffn.arrays[0], dx, keep, send = outs[:4]
    attention = Reduction(sum_planes(places, [(keep, send), (keep_out, send_out)]))
    output, arrived = settled(output)
    ffn.step()
    ffn.arrays[0] = gate(ffn.arrays[0], arrived)
    ffn.step()
    (total,) = ffn.arrays
    middle = total.shape[0] // 2
    sums = {
        "d": Reduction(sum_depth_and_gather(places, total[:middle])),
        "u": Reduction(sum_depth_and_gather(places, total[middle:])),
    }
    done = {}
    before = []
    for n, name in enumerate(TAIL):
        if name == "a" and "a" not in sums:
            sums["a"] = attention
            before = attention.turn(before)
        elif name == "A":
            attention.turn(before)
            sums["a"] = attention = Reduction(sum_depth_and_gather(places, attention.arrays[0]))
            before = attention.turn([])
        elif name in "DU":
            reduction = sums[name.lower()]
            reduction.step()
            done[name], finished = run_finish_ffn(core_ref, *reduction.arrays, name == "U")
            before = before + [finished]
        else:
            before = sums[name].turn(before)
        if n == TRADE_AFTER:
            d_tokens = trade(gate(dx, *before))
        if n == TRADED:
            d_tokens, arrived = settled(d_tokens)
            before = before + [arrived]
    attention.step()
    dwd, dwu = done["D"], done["U"]
    own, other = attention.arrays
    half = dim // 2
    dwq, dwk, dwv, dwo = run_finish(
        core_ref, own, other, (0, half, 2 * half, 3 * half + GAIN_ROWS), (dim, dim)
    )
    at = 3 * dim // 2
    gains = jnp.where(core == 0, own[at : at + 2], other[at : at + 2]).astype(F32)
    return output, d_tokens, gains[0], gains[1], dwq, dwk, dwv, dwo, dwu, dwd


def solution(mesh):
    act = P("rows", "seq", None)
    return jax.shard_map(
        local,
        mesh=mesh,
        in_specs=(act, P("rows", None)) + (P(),) * 8 + (act,),
        out_specs=(act, act) + (P(),) * 8,
        check_vma=False,
    )
```

```python
import functools

import jax
import jax.numpy as jnp
from jax import lax
from jax.experimental import pallas as pl
from jax.experimental.pallas import tpu as pltpu
from jax.sharding import PartitionSpec as P

HEADS = 8
HEAD = 64
BAND = 30
EPSILON = 1e-06
SCALE = 0.125
CHUNK = 128
BLOCK = 256
PAIRS = HEADS // 2
NEG = -1e30
STEP_PAIRS = 2
GAIN_ROWS = 64
TAIL = "duadudAuaduaaduaduDUa"
GATE_KIB = 512
SETTLE = 12
TRADE_AFTER = 12
TRADED = 18
FFN_ROWS = 2
FORWARD_MIB = 52
FFN_MIB = 50
ATTENTION_MIB = 54
GELU_A = 0.7978845608028654
GELU_B = 0.044715
F32 = jnp.float32
BF16 = jnp.bfloat16
VMEM_LIMIT = 56 * 1024 * 1024


def nn(a, b):
    return lax.dot_general(a, b, (((1,), (0,)), ((), ())), preferred_element_type=F32)


def nt(a, b):
    return lax.dot_general(a, b, (((1,), (1,)), ((), ())), preferred_element_type=F32)


def tn(a, b):
    return lax.dot_general(a, b, (((0,), (0,)), ((), ())), preferred_element_type=F32)


def low_lanes(shape):
    return lax.broadcasted_iota(jnp.int32, shape, len(shape) - 1) < HEAD


def split_heads(pair):
    low = low_lanes(pair.shape)
    zero = jnp.zeros_like(pair)
    return jnp.concatenate([jnp.where(low, pair, zero), jnp.where(low, zero, pair)], 0)


def pick(both):
    half = both.shape[0] // 2
    return jnp.where(low_lanes((half, both.shape[1])), both[:half], both[half:])


def over_lanes(column):
    half = column.shape[0] // 2
    return jnp.where(low_lanes((half, 2 * HEAD)), column[:half], column[half:])


def in_step(bodies):
    bodies = list(bodies)
    while bodies:
        bodies = [body for body in bodies if next(body, True) is None]


def features(t):
    expo = jnp.exp(jnp.minimum(t, 0.0))
    tanh = jnp.tanh(t)
    return (jnp.where(t > 0, t + 1.0, expo), 1.0 + tanh), (expo, 1.0 - tanh * tanh)


def head_mask(lanes):
    row = lax.broadcasted_iota(jnp.int32, (4 * HEAD, lanes), 0)
    lane = lax.broadcasted_iota(jnp.int32, (4 * HEAD, lanes), 1)
    head = (row // HEAD) % 2
    same = (lane < 2 * HEAD) & (lane // HEAD == head)
    return same | (lane == 2 * HEAD + row // HEAD)


def chunk_masks(seg_ref, place_ref, chunk):
    chunk = place_ref[1] + chunk

    def stretch(at):
        rows = seg_ref[:, pl.ds(pl.multiple_of(at * CHUNK, CHUNK), CHUNK)]
        mine = lax.broadcasted_iota(jnp.int32, rows.shape, 0) == place_ref[0]
        return jnp.max(jnp.where(mine, rows, -1), 0, keepdims=True).astype(F32)

    seg_own = stretch(chunk)
    seg_prev = jnp.where(chunk == 0, -1.0, stretch(jnp.maximum(chunk - 1, 0)))
    seg_q = jnp.broadcast_to(seg_own, (CHUNK, CHUNK)).T
    row = lax.broadcasted_iota(jnp.int32, (CHUNK, CHUNK), 0)
    col = lax.broadcasted_iota(jnp.int32, (CHUNK, CHUNK), 1)
    gap = row - col
    far = (seg_q == seg_own) & (gap >= 0)
    band_own = far & (gap <= BAND)
    band_prev = (seg_q == seg_prev) & (gap + CHUNK <= BAND)
    band = jnp.concatenate([band_prev, band_own], 1)
    before = seg_prev[:, CHUNK - 1 :]
    last = seg_own[:, CHUNK - 1 :]
    carry = (seg_q[:, :1] == before).astype(F32)
    tail = (seg_own == last).astype(BF16)
    keep = (before == last).astype(F32)
    return jnp.concatenate([band, band], 0), jnp.concatenate([far, far], 0), carry, tail, keep


def start_with(refs, entry_refs):
    for n, ref in enumerate(refs):
        ref[...] = entry_refs[n][...] if entry_refs else jnp.zeros_like(ref)


def forward_kernel(entries, *refs):
    (x_ref, seg_ref, place_ref, ga_ref, gf_ref, wq_ref, wk_ref, wv_ref, wo_ref, wu_ref, wd_ref,
     *refs) = refs
    entry_refs, refs = refs[:entries], refs[entries:]
    (out_ref, x1_ref, a_ref, h_ref, q_ref, k_ref, v_ref, stats_ref, states_ref, sums_ref,
     *refs) = refs
    end_refs, refs = refs[: min(entries, 2)], refs[min(entries, 2) :]
    s_ref, z_ref, kp_ref, vp_ref, wkt_ref, wvt_ref = refs
    step = pl.program_id(0)

    @pl.when(step == 0)
    def _():
        start_with((s_ref, z_ref, kp_ref, vp_ref), entry_refs)
        wkt_ref[...] = wk_ref[...].T
        wvt_ref[...] = wv_ref[...].T

    block = pl.ds(pl.multiple_of(step * BLOCK, BLOCK), BLOCK)
    x = x_ref[...].astype(F32)
    inv = lax.rsqrt(jnp.mean(x * x, -1, keepdims=True) + EPSILON)
    hidden = (x * inv * ga_ref[...]).astype(BF16)
    h_ref[...] = hidden
    q_ref[...] = nn(hidden, wq_ref[...]).astype(BF16)
    k_ref[...] = nt(wkt_ref[...], hidden).astype(BF16)
    v_ref[...] = nt(wvt_ref[...], hidden).astype(BF16)
    same_head = head_mask(CHUNK)
    for sub in range(BLOCK // CHUNK):
        chunk = step * (BLOCK // CHUNK) + sub
        rows = slice(sub * CHUNK, (sub + 1) * CHUNK)
        tokens = pl.ds(pl.multiple_of(chunk * CHUNK, CHUNK), CHUNK)
        band, far_mask, carry, tail, keep = chunk_masks(seg_ref, place_ref, chunk)
        tail_rows = jnp.broadcast_to(tail, (16, CHUNK))

        def body(p):
            lanes = slice(p * 128, (p + 1) * 128)
            qp = q_ref[rows, lanes]
            kt = k_ref[lanes, rows]
            vt = v_ref[lanes, rows]
            kt_ext = jnp.concatenate([kp_ref[lanes], kt], 1)
            vt_ext = jnp.concatenate([vp_ref[lanes], vt], 1)
            score = nn(split_heads(qp * SCALE), kt_ext)
            fq, _ = features(qp.astype(F32))
            fk, _ = features(kt.astype(F32))
            fk = [f.astype(BF16) for f in fk]
            fq = [f.astype(BF16) for f in fq]
            yield
            part = [
                jnp.where(far_mask, nn(split_heads(fq[m]), fk[m]), 0.0) for m in range(2)
            ]
            score = jnp.where(band, score, NEG)
            top = jnp.max(score, -1, keepdims=True)
            yield
            state = s_ref[p]
            state_low = state.astype(BF16)
            sums = z_ref[p]
            states_ref[sub, p] = state_low
            sums_ref[sub, p] = sums
            fk_both = jnp.concatenate(fk, 0)
            update = nt(fk_both * tail, vt)
            s_ref[p] = keep * state + jnp.where(same_head, update, 0.0)
            z_ref[p] = keep * sums + nt(tail_rows, fk_both)[:8]
            expo = jnp.exp(score - top)
            total = jnp.sum(expo, -1, keepdims=True)
            yield
            inv_total = 1.0 / total
            prob_prev = (expo[:, :CHUNK] * inv_total).astype(BF16)
            weight = expo[:, CHUNK:] * inv_total
            columns = [top + jnp.log(total)]
            scaled = []
            for m in range(2):
                fq_carry = fq[m].astype(F32) * carry
                entered = split_heads(fq_carry * sums[:1, m * 128 : (m + 1) * 128])
                inv_z = 1.0 / jnp.sum(part[m] + entered, -1, keepdims=True)
                columns.append(inv_z)
                weight = weight + part[m] * inv_z
                scaled.append((fq_carry * over_lanes(inv_z)).astype(BF16))
            both = jnp.concatenate([prob_prev, weight.astype(BF16)], 1)
            yield
            attended = pick(nt(both, vt_ext)) + nn(jnp.concatenate(scaled, 1), state_low)
            a_ref[tokens, lanes] = attended.astype(BF16)
            for n, column in enumerate(columns):
                stats_ref[sub, p, n] = jnp.broadcast_to(column, (2 * CHUNK, CHUNK))

        for first in range(0, PAIRS, STEP_PAIRS):
            in_step(body(p) for p in range(first, first + STEP_PAIRS))
        kp_ref[...] = k_ref[:, rows]
        vp_ref[...] = v_ref[:, rows]
    for end_ref, ref in zip(end_refs, (s_ref, z_ref)):
        end_ref[...] = ref[...]
    x1 = x + nn(a_ref[block], wo_ref[...])
    x1_ref[block] = x1
    inv = lax.rsqrt(jnp.mean(x1 * x1, -1, keepdims=True) + EPSILON)
    hidden = (x1 * inv * gf_ref[...]).astype(BF16)
    total = x1
    width = 512
    for f in range(wu_ref.shape[1] // width):
        cols = slice(f * width, (f + 1) * width)
        up = nn(hidden, wu_ref[:, cols])
        act = 0.5 * up * (1.0 + jnp.tanh(GELU_A * (up + GELU_B * up * up * up)))
        total = total + nn(act.astype(BF16), wd_ref[cols])
    out_ref[...] = total.astype(BF16)


def norm_backward(x, gain, grad):
    inv = lax.rsqrt(jnp.mean(x * x, -1, keepdims=True) + EPSILON)
    unit = x * inv
    scaled = grad * gain
    d_gain = jnp.sum(grad * unit, 0, keepdims=True)
    return inv * (scaled - unit * jnp.mean(unit * scaled, -1, keepdims=True)), d_gain


def ffn_backward_kernel(
    dy_ref, x1_ref, a_ref, gf_ref, wo_ref, wu_ref, wd_ref, core_ref,
    dx1_ref, da_ref, dg_ref, keep_ref, send_ref, keep_out_ref, send_out_ref,
    hidden_ref, dh_ref, dwd_ref, dwu_ref,
):
    step = pl.program_id(0)
    core = core_ref[0]
    gain = gf_ref[...]

    @pl.when(step == 0)
    def _():
        x1 = x1_ref[...]
        inv = lax.rsqrt(jnp.mean(x1 * x1, -1, keepdims=True) + EPSILON)
        hidden_ref[...] = (x1 * inv * gain).astype(BF16)
        dh_ref[...] = jnp.zeros_like(dh_ref)

    for part in range(FFN_ROWS):
        size = dy_ref.shape[0] // FFN_ROWS
        rows = slice(part * size, (part + 1) * size)
        dy = dy_ref[rows]
        hidden = hidden_ref[rows]
        up = nn(hidden, wu_ref[...])
        square = up * up
        tanh = jnp.tanh(GELU_A * up * (1.0 + GELU_B * square))
        half = 0.5 * (1.0 + tanh)
        act = (up * half).astype(BF16)
        slope = half + 0.5 * up * (1.0 - tanh * tanh) * (
            GELU_A + (3.0 * GELU_A * GELU_B) * square
        )
        d_up = (slope * nt(dy, wd_ref[...])).astype(BF16)
        dh_ref[rows] += nt(d_up, wu_ref[...])
        dwd, dwu = tn(act, dy), tn(hidden, d_up)
        if part:
            dwd, dwu = dwd + dwd_ref[...], dwu + dwu_ref[...]
        dwd_ref[...], dwu_ref[...] = dwd, dwu
    put_halves((dwd_ref, dwu_ref), core, keep_ref, send_ref)

    @pl.when(step == pl.num_programs(0) - 1)
    def _():
        x1 = x1_ref[...]
        d_norm, d_gain = norm_backward(x1, gain, dh_ref[...])
        dx1 = dy_ref[...].astype(F32) + d_norm
        dg_ref[...] = jnp.broadcast_to(d_gain, dg_ref.shape)
        dx1_ref[...] = dx1
        d_branch = dx1.astype(BF16)
        da_ref[...] = nt(d_branch, wo_ref[...]).astype(BF16)
        dwd_ref[...] = tn(a_ref[...], d_branch)
        put_halves((dwd_ref,), core, keep_out_ref, send_out_ref)


def put_halves(sums, core, keep_ref, send_ref):
    at = 0
    for total in sums:
        half = total.shape[0] // 2
        for ref, which in ((keep_ref, core), (send_ref, 1 - core)):
            rows = total[pl.ds(pl.multiple_of(which * half, half), half)]
            ref[at : at + half] = rows.astype(BF16)
        at += half
    return at


def attention_backward_kernel(entries, *refs):
    (x_ref, q_ref, h_ref, k_ref, v_ref, kprev_ref, vprev_ref, stats_ref, states_ref, sums_ref,
     da_ref, seg_ref, dx1_ref, place_ref, ga_ref, dgf_ref, wq_ref, wk_ref, wv_ref, *refs) = refs
    entry_refs, refs = refs[:entries], refs[entries:]
    dx_ref, keep_ref, send_ref, *refs = refs
    end_refs, refs = refs[: min(entries, 3)], refs[min(entries, 3) :]
    (r_ref, dkc_ref, dvc_ref, dq_ref, dk_ref, dv_ref, dwq_acc, dwk_acc, dwv_acc, dg_acc,
     wkt_ref, wvt_ref) = refs
    step = pl.program_id(0)
    block = pl.num_programs(0) - 1 - step

    @pl.when(step == 0)
    def _():
        start_with((r_ref, dkc_ref, dvc_ref), entry_refs)
        dwq_acc[...] = jnp.zeros_like(dwq_acc)
        dwk_acc[...] = jnp.zeros_like(dwk_acc)
        dwv_acc[...] = jnp.zeros_like(dwv_acc)
        dg_acc[...] = jnp.zeros_like(dg_acc)
        wkt_ref[...] = wk_ref[...].T
        wvt_ref[...] = wv_ref[...].T

    lane = lax.broadcasted_iota(jnp.int32, (CHUNK, CHUNK), 1)
    same_head = head_mask(2 * CHUNK)
    for sub in reversed(range(BLOCK // CHUNK)):
        chunk = block * (BLOCK // CHUNK) + sub
        rows = slice(sub * CHUNK, (sub + 1) * CHUNK)
        tokens = pl.ds(pl.multiple_of(chunk * CHUNK, CHUNK), CHUNK)
        band, far_mask, carry, tail, keep = chunk_masks(seg_ref, place_ref, chunk)
        tail_rows = jnp.broadcast_to(tail, (CHUNK, CHUNK))

        def body(p):
            lanes = slice(p * 128, (p + 1) * 128)
            qp = q_ref[rows, lanes]
            da = da_ref[tokens, lanes]
            kt = k_ref[lanes, rows]
            vt = v_ref[lanes, rows]
            if sub == 0:
                kt_prev, vt_prev = kprev_ref[lanes], vprev_ref[lanes]
                if entry_refs:
                    kt_prev = jnp.where(block == 0, entry_refs[3][lanes], kt_prev)
                    vt_prev = jnp.where(block == 0, entry_refs[4][lanes], vt_prev)
            else:
                before = slice((sub - 1) * CHUNK, sub * CHUNK)
                kt_prev, vt_prev = k_ref[lanes, before], v_ref[lanes, before]
            kt_ext = jnp.concatenate([kt_prev, kt], 1)
            vt_ext = jnp.concatenate([vt_prev, vt], 1)
            q2 = split_heads(qp * SCALE)
            da2 = split_heads(da)
            score = nn(q2, kt_ext)
            d_prob = nn(da2, vt_ext)
            yield
            state = states_ref[sub, p]
            sums = sums_ref[sub, p]
            back = r_ref[p]
            back_low = back.astype(BF16)
            from_state = nt(da, state) * carry
            to_later = nn(back_low, jnp.concatenate([vt * tail, tail_rows], 0))
            fq, slope_q = features(qp.astype(F32))
            fk, slope_k = features(kt.astype(F32))
            fk = [f.astype(BF16) for f in fk]
            fq = [f.astype(BF16) for f in fq]
            fq2 = [split_heads(f) for f in fq]
            yield
            part = [jnp.where(far_mask, nn(fq2[m], fk[m]), 0.0) for m in range(2)]
            lse = stats_ref[sub, p, 0]
            prob = jnp.exp(jnp.where(band, score - jnp.concatenate([lse, lse], 1), NEG))
            delta = jnp.sum(prob * d_prob, -1, keepdims=True)
            d_score = (prob * (d_prob - delta)).astype(BF16)
            yield
            dq = SCALE * pick(nt(d_score, kt_ext))
            dk_ext = tn(q2, d_score)
            dk = dk_ext[:, CHUNK:] + dkc_ref[lanes]
            dkc_ref[lanes] = dk_ext[:, :CHUNK]
            d_own = d_prob[:, CHUNK:]
            weight = prob[:, CHUNK:]
            yield
            scaled = []
            d_part = []
            entries = []
            right = jnp.zeros((CHUNK, CHUNK), F32)
            for m in range(2):
                part_lanes = slice(m * 128, (m + 1) * 128)
                fq_wide = fq[m].astype(F32)
                inv_z = stats_ref[sub, p, m + 1]
                weighted = part[m] * inv_z
                weight = weight + weighted
                entered = from_state[:, part_lanes]
                inv_wide = pick(inv_z)
                taken = fq_wide * inv_wide
                dot = jnp.sum(
                    weighted * d_own + split_heads(taken * entered), -1, keepdims=True
                )
                d_part.append(jnp.where(far_mask, (d_own - dot) * inv_z, 0.0).astype(BF16))
                entries.append(
                    inv_wide * (entered - over_lanes(dot) * (carry * sums[:1, part_lanes]))
                )
                scaled.append((taken * carry).astype(BF16))
                right = jnp.where(lane == 2 * m, -dot[:CHUNK], right)
                right = jnp.where(lane == 2 * m + 1, -dot[CHUNK:], right)
            both = jnp.concatenate([prob[:, :CHUNK].astype(BF16), weight.astype(BF16)], 1)
            yield
            dv_ext = tn(da2, both)
            dv = dv_ext[:, CHUNK:] + dvc_ref[lanes]
            dv = dv + tn(back_low[:, :CHUNK], jnp.concatenate(fk, 0) * tail)
            dvc_ref[lanes] = dv_ext[:, :CHUNK]
            update = tn(
                jnp.concatenate(scaled, 1), jnp.concatenate([da, right.astype(BF16)], 1)
            )
            r_ref[p] = keep * back + jnp.where(same_head, update, 0.0)
            dv_ref[lanes, rows] = dv.astype(BF16)
            yield
            for m in range(2):
                dq = dq + slope_q[m] * (pick(nt(d_part[m], fk[m])) + entries[m])
                dk = dk + slope_k[m] * (
                    tn(fq2[m], d_part[m]) + to_later[m * 128 : (m + 1) * 128]
                )
            dq_ref[rows, lanes] = dq.astype(BF16)
            dk_ref[lanes, rows] = dk.astype(BF16)

        for first in range(0, PAIRS, STEP_PAIRS):
            in_step(body(p) for p in range(first, first + STEP_PAIRS))
    for end_ref, ref in zip(end_refs, (r_ref, dkc_ref, dvc_ref)):
        end_ref[...] = ref[...]
    dim = x_ref.shape[1]
    tokens = pl.ds(pl.multiple_of(block * BLOCK, BLOCK), BLOCK)
    hidden_t = h_ref[...].T
    dq, dk, dv = dq_ref[...], dk_ref[...], dv_ref[...]
    dwq_acc[...] += nn(hidden_t, dq)
    dwk_acc[...] += nt(hidden_t, dk)
    dwv_acc[...] += nt(hidden_t, dv)
    d_hidden = nt(dq, wq_ref[...]) + tn(dk, wkt_ref[...]) + tn(dv, wvt_ref[...])
    d_norm, d_gain = norm_backward(x_ref[...].astype(F32), ga_ref[...], d_hidden)
    dg_acc[...] += jnp.broadcast_to(d_gain, dg_acc.shape)
    dx_ref[...] = (dx1_ref[tokens] + d_norm).astype(BF16)

    @pl.when(step == pl.num_programs(0) - 1)
    def _():
        core = place_ref[2]
        at = put_halves((dwq_acc, dwk_acc, dwv_acc), core, keep_ref, send_ref)
        keep_ref[at:] = jnp.zeros((GAIN_ROWS, keep_ref.shape[1]), BF16)
        send_ref[at:] = jnp.zeros((GAIN_ROWS, keep_ref.shape[1]), BF16)
        gains = jnp.concatenate([dg_acc[:1], dgf_ref[:1], jnp.zeros((14, dim), F32)], 0)
        keep_ref[at : at + 16] = jnp.where(core == 0, gains, 0.0).astype(BF16)
        send_ref[at : at + 16] = jnp.where(core == 0, 0.0, gains).astype(BF16)


HELD = pl.BlockSpec(memory_space=pltpu.VMEM)


def whole(shape):
    return pl.BlockSpec(shape, lambda i: (0,) * len(shape))


FFN_IN = HELD


def tokens_of(width, index=lambda i: i):
    return pl.BlockSpec((BLOCK, width), lambda i: (index(i), 0))


def of_chunks(shape, index=lambda i: i):
    return pl.BlockSpec((BLOCK // CHUNK,) + shape, lambda i: (index(i),) + (0,) * len(shape))


def params(mib):
    return pltpu.CompilerParams(
        vmem_limit_bytes=mib * 1024 * 1024, dimension_semantics=("arbitrary",)
    )


def sds(shape, dtype):
    return jax.ShapeDtypeStruct(shape, dtype)


def run_forward(x, segments, place, gain_attn, gain_ffn, wq, wk, wv, wo, wu, wd, entry):
    length, dim = x.shape
    ff = wu.shape[1]
    chunks = length // CHUNK
    row = tokens_of(dim)
    column = pl.BlockSpec((dim, BLOCK), lambda i: (0, i))
    state_shape = (PAIRS, 4 * HEAD, 2 * HEAD)
    sum_shape = (PAIRS, 8, 4 * HEAD)
    stat_shape = (PAIRS, 3, 2 * CHUNK, CHUNK)
    ends = [(state_shape, F32), (sum_shape, F32)][: len(entry)]
    return pl.pallas_call(
        functools.partial(forward_kernel, len(entry)),
        grid=(length // BLOCK,),
        in_specs=[
            row, HELD, SMEM, HELD, HELD, HELD, HELD, HELD, HELD, HELD, HELD,
        ] + [whole(array.shape) for array in entry],
        out_specs=[
            row, HELD, HELD, row, row, column, column,
            of_chunks(stat_shape), of_chunks(state_shape), of_chunks(sum_shape),
        ] + [whole(shape) for shape, _ in ends],
        out_shape=[
            sds((length, dim), BF16), sds((length, dim), F32), sds((length, dim), BF16),
            sds((length, dim), BF16), sds((length, dim), BF16),
            sds((dim, length), BF16), sds((dim, length), BF16),
            sds((chunks,) + stat_shape, F32),
            sds((chunks,) + state_shape, BF16), sds((chunks,) + sum_shape, F32),
        ] + [sds(*end) for end in ends],
        scratch_shapes=[
            pltpu.VMEM(state_shape, F32), pltpu.VMEM(sum_shape, F32),
            pltpu.VMEM((dim, CHUNK), BF16), pltpu.VMEM((dim, CHUNK), BF16),
            pltpu.VMEM((dim, dim), BF16), pltpu.VMEM((dim, dim), BF16),
        ],
        compiler_params=params(FORWARD_MIB),
        name="layer_forward",
    )(x, segments, place, gain_attn, gain_ffn, wq, wk, wv, wo, wu, wd, *entry)


SMEM = pl.BlockSpec(memory_space=pltpu.SMEM)
ANY = pl.BlockSpec(memory_space=pl.ANY)


def run_ffn_backward(dy, x1, a, gain_ffn, wo, wu, wd, core):
    length, dim = dy.shape
    ff = wu.shape[1]
    step_half = pl.BlockSpec((dim, dim), lambda i: (i, 0))
    return pl.pallas_call(
        ffn_backward_kernel,
        grid=(ff // dim,),
        in_specs=[
            FFN_IN, FFN_IN, FFN_IN, HELD, HELD,
            pl.BlockSpec((dim, dim), lambda i: (0, i)), step_half, SMEM,
        ],
        out_specs=[FFN_IN, FFN_IN, HELD, step_half, step_half, HELD, HELD],
        out_shape=[
            sds((length, dim), F32), sds((length, dim), BF16), sds((8, dim), F32),
            sds((ff, dim), BF16), sds((ff, dim), BF16),
            sds((dim // 2, dim), BF16), sds((dim // 2, dim), BF16),
        ],
        scratch_shapes=[
            pltpu.VMEM((length, dim), BF16), pltpu.VMEM((length, dim), F32),
            pltpu.VMEM((dim, dim), F32), pltpu.VMEM((dim, dim), F32),
        ],
        compiler_params=params(FFN_MIB),
        name="ffn_backward",
    )(dy, x1, a, gain_ffn, wo, wu, wd, core)


def run_attention_backward(
    after, through, x, dx1, da, h, q, k, v, stats, states, sums, segments, place,
    gain_attn, dgf, wq, wk, wv, entry,
):
    length, dim = x.shape
    half = 3 * dim // 2 + GAIN_ROWS
    steps = length // BLOCK
    back = lambda i: steps - 1 - i
    row = tokens_of(dim, back)
    column = pl.BlockSpec((dim, BLOCK), lambda i: (0, back(i)))
    per = BLOCK // CHUNK
    prev = pl.BlockSpec((dim, CHUNK), lambda i: (0, jnp.maximum(back(i) * per - 1, 0)))
    streams = [of_chunks(array.shape[1:], back) for array in (stats, states, sums)]
    r_shape = (PAIRS, 4 * HEAD, 4 * HEAD)
    rim_shape = (dim, CHUNK)
    ends = [r_shape, rim_shape, rim_shape][: len(entry)]
    kernel = functools.partial(attention_backward_kernel, len(entry))
    skip = len(after) + len(through)
    streamed = [x, q, h, k, v, k, v, stats, states, sums]
    held = [da, segments, dx1, place, gain_attn, dgf, wq, wk, wv, *entry]
    inputs = skip + len(streamed) + len(held)

    def body(*refs):
        kernel(*refs[skip:inputs], *refs[inputs + len(through) :])

    return pl.pallas_call(
        body,
        grid=(steps,),
        input_output_aliases={len(after) + n: n for n in range(len(through))},
        in_specs=[ANY] * skip + [row, row, row, column, column, prev, prev] + streams
        + [SMEM if array is place else HELD for array in held],
        out_specs=[ANY] * len(through) + [row, HELD, HELD] + [whole(shape) for shape in ends],
        out_shape=[sds(array.shape, array.dtype) for array in through] + [
            sds((length, dim), BF16), sds((half, dim), BF16), sds((half, dim), BF16),
        ] + [sds(shape, F32) for shape in ends],
        scratch_shapes=[
            pltpu.VMEM(r_shape, F32), pltpu.VMEM(rim_shape, F32), pltpu.VMEM(rim_shape, F32),
            pltpu.VMEM((BLOCK, dim), BF16), pltpu.VMEM((dim, BLOCK), BF16),
            pltpu.VMEM((dim, BLOCK), BF16),
            pltpu.VMEM((dim, dim), F32), pltpu.VMEM((dim, dim), F32), pltpu.VMEM((dim, dim), F32),
            pltpu.VMEM((8, dim), F32),
            pltpu.VMEM((dim, dim), BF16), pltpu.VMEM((dim, dim), BF16),
        ],
        compiler_params=params(ATTENTION_MIB),
        name="attention_backward",
    )(*after, *through, *streamed, *held)


def finish_ffn_kernel(core_ref, own_ref, other_ref, out_ref, done_ref):
    half = out_ref.shape[0] // 2
    for ref, which in ((own_ref, core_ref[0]), (other_ref, 1 - core_ref[0])):
        rows = pl.ds(pl.multiple_of(which * half, half), half)
        out_ref[rows] = ref[...].astype(F32)
    done_ref[...] = jnp.zeros_like(done_ref)


def run_finish_ffn(core_ref, own, other, across):
    dim = own.shape[1]
    ff = own.shape[0] * 2
    block = pl.BlockSpec((dim // 2, dim), lambda i: (i, 0))
    return pl.pallas_call(
        finish_ffn_kernel,
        grid=(ff // dim,),
        in_specs=[SMEM, block, block],
        out_specs=[
            pl.BlockSpec((dim, dim), (lambda i: (0, i)) if across else (lambda i: (i, 0))),
            whole((8, 128)),
        ],
        out_shape=[sds((dim, ff) if across else (ff, dim), F32), sds((8, 128), F32)],
        compiler_params=params(12),
        name="finish_ffn",
    )(core_ref, own, other)


def finish_kernel(starts, core_ref, own_ref, other_ref, *out_refs):
    for at, out_ref in zip(starts, out_refs):
        half = out_ref.shape[0] // 2
        for ref, which in ((own_ref, core_ref[0]), (other_ref, 1 - core_ref[0])):
            rows = pl.ds(pl.multiple_of(which * half, half), half)
            out_ref[rows] = ref[at : at + half].astype(F32)


def run_finish(core_ref, own, other, starts, shape):
    return pl.pallas_call(
        functools.partial(finish_kernel, starts),
        in_specs=[SMEM, HELD, HELD],
        out_specs=[HELD] * len(starts),
        out_shape=[sds(shape, F32)] * len(starts),
        compiler_params=pltpu.CompilerParams(vmem_limit_bytes=12 * 1024 * 1024),
        name="finish",
    )(core_ref, own, other)


def partner(array, seq_bits, row_bits):
    seq_count, row_groups = lax.axis_size("seq"), lax.axis_size("rows")
    pairs = [
        (s * row_groups + r, (s ^ seq_bits) * row_groups + (r ^ row_bits))
        for s in range(seq_count)
        for r in range(row_groups)
    ]
    return lax.ppermute(array, ("seq", "rows"), pairs)


def add(*parts):
    parts = [part.astype(F32) for part in parts]
    if len(parts) == 4:
        return ((parts[0] + parts[1]) + (parts[2] + parts[3])).astype(BF16)
    return (parts[0] + parts[1]).astype(BF16)


def take(array, index, size):
    return lax.dynamic_slice_in_dim(array, index * size, size, 0)


PLANE_BITS = ((1, 0), (0, 2), (1, 2))
DEPTH_BITS = (2, 4)


def cut(total, place):
    size = total.shape[0] // 4
    return [take(total, place ^ d, size) for d in range(4)]


def traded(parts, all_bits):
    return [parts[0]] + [partner(part, *bits) for part, bits in zip(parts[1:], all_bits)]


def cut_half(total, bit):
    size = total.shape[0] // 2
    return [take(total, bit, size), take(total, 1 - bit, size)]


def joined_half(own, other, bit):
    return jnp.where(bit == 0, jnp.concatenate([own, other], 0), jnp.concatenate([other, own], 0))


def joined(parts, place):
    blocks = jnp.stack(parts)
    blocks = [lax.dynamic_index_in_dim(blocks, place ^ d, 0, False) for d in range(4)]
    return jnp.concatenate(blocks, 0)


def sum_planes(places, halves):
    core, plane, depth = places
    others = [partner(send, 0, 1) for _, send in halves]
    keeps = yield [keep for keep, _ in halves]
    sums = [add(keep, other) for keep, other in zip(keeps, others)]
    parts = yield cut(jnp.concatenate(sums, 0) if len(sums) > 1 else sums[0], plane)
    parts = traded(parts, PLANE_BITS)
    parts = yield parts
    yield [add(*parts)]


def sum_depth_and_gather(places, total):
    core, plane, depth = places
    (total,) = yield [total]
    for n, (bits, bit) in enumerate(zip(DEPTH_BITS, depth)):
        keep, send = yield cut_half(total, bit)
        other = partner(send, bits, 0)
        keep, other = yield [keep, other]
        total = add(keep, other)
    for bits in further_bits():
        total = add(total, partner(total, *bits))
    for bits, bit in reversed(list(zip(DEPTH_BITS, depth))):
        (total,) = yield [total]
        other = partner(total, bits, 0)
        total, other = yield [total, other]
        total = joined_half(total, other, bit)
    (block,) = yield [total]
    parts = traded([block] * 4, PLANE_BITS)
    parts = yield parts
    (own,) = yield [joined(parts, plane)]
    yield [own, partner(own, 0, 1)]


def gate(array, *others, mib=None):
    return pl.pallas_call(
        lambda *refs: None,
        in_specs=[ANY] * (1 + len(others)),
        out_specs=ANY,
        out_shape=sds(array.shape, array.dtype),
        input_output_aliases={0: 0},
        compiler_params=pltpu.CompilerParams(vmem_limit_bytes=mib * 2**20 if mib else GATE_KIB * 1024),
        name="gate",
    )(array, *others)


def settled(array):
    def kernel(in_ref, out_ref, done_ref):
        out_ref[...] = in_ref[...]
        done_ref[...] = jnp.zeros_like(done_ref)

    block = pl.BlockSpec((1,) + array.shape[1:], lambda i: (i, 0, 0))
    return pl.pallas_call(
        kernel,
        grid=(array.shape[0],),
        in_specs=[block],
        out_specs=[block, whole((8, 128))],
        out_shape=[sds(array.shape, array.dtype), sds((8, 128), F32)],
        compiler_params=params(2),
        name="settled",
    )(array)


class Reduction:
    def __init__(self, steps):
        self.steps = steps
        self.arrays = next(steps)
        self.waits = False

    def step(self):
        self.arrays = self.steps.send(self.arrays)

    def turn(self, before):
        if self.waits:
            self.step()
        if before:
            self.arrays[0] = gate(self.arrays[0], *before)
        self.step()
        self.waits = True
        return self.arrays[1:] or self.arrays


def further_bits():
    bits = []
    bit = 8
    while bit < lax.axis_size("seq"):
        bits.append((bit, 0))
        bit *= 2
    bit = 4
    while bit < lax.axis_size("rows"):
        bits.append((0, bit))
        bit *= 2
    return bits


def all_reduce_small(small):
    small = small + partner(small, 0, 1)
    for bits in (((1, 0), (0, 2), (1, 2)), ((2, 0), (4, 0), (6, 0))):
        got = [small] + [partner(small, *b) for b in bits]
        small = (got[0] + got[1]) + (got[2] + got[3])
    for b in further_bits():
        small = small + partner(small, *b)
    return small


def local(
    tokens, segments, gain_attn, gain_ffn, w_query, w_key, w_value, w_out, w_up, w_down, cotangent
):
    row_count, shard_len, dim = tokens.shape
    seq_count = lax.axis_size("seq")
    parts = seq_count // row_count
    groups = [[g * row_count + r for r in range(row_count)] for g in range(parts)]
    length = row_count * shard_len
    index = lax.axis_index("seq")
    my_row = index % row_count
    my_part = index // row_count

    def trade(array):
        return lax.all_to_all(
            array.reshape(row_count, shard_len, dim), "seq", 0, 0, axis_index_groups=groups
        )

    def shifted(arrays, by):
        pairs = [
            (i, i + by * row_count)
            for i in range(seq_count)
            if 0 <= i + by * row_count < seq_count
        ]
        return lax.ppermute(arrays, "seq", pairs)

    ga, gf = gain_attn.reshape(1, dim), gain_ffn.reshape(1, dim)
    seq_index, row_index = lax.axis_index("seq"), lax.axis_index("rows")
    core, plane = row_index % 2, seq_index % 2 + 2 * (row_index // 2 % 2)
    places = core, plane, (seq_index // 2 % 2, seq_index // 4 % 2)
    place = jnp.stack([my_row, my_part * (length // CHUNK), core]).astype(jnp.int32)

    x = trade(tokens).reshape(length, dim)
    dy = trade(cotangent).reshape(length, dim)
    entry = ()
    if parts > 1:
        rim_zero = jnp.zeros((dim, CHUNK), BF16)
        entry = (
            jnp.zeros((PAIRS, 4 * HEAD, 2 * HEAD), F32), jnp.zeros((PAIRS, 8, 4 * HEAD), F32),
            rim_zero, rim_zero,
        )
    for turn in range(parts):
        out, x1, a, h, q, k, v, stats, states, sums, *ends = run_forward(
            x, segments, place, ga, gf, w_query, w_key, w_value, w_out, w_up, w_down, entry
        )
        if turn < parts - 1:
            entry = shifted((*ends, k[:, length - CHUNK :], v[:, length - CHUNK :]), 1)
    output = trade(out)
    core_ref = place[2:]
    dx1, da, dgf, keep, send, keep_out, send_out = run_ffn_backward(
        dy, x1, a, gf, w_out, w_up, w_down, core_ref
    )
    ffn = Reduction(sum_planes(places, [(keep, send)]))
    ffn.step()
    back = ()
    if parts > 1:
        rim = jnp.zeros((dim, CHUNK), F32)
        back = (jnp.zeros((PAIRS, 4 * HEAD, 4 * HEAD), F32), rim, rim)
    for turn in range(parts):
        through, after = [], []
        if turn == parts - 1:
            through, after = ffn.arrays[:1], ffn.arrays[1:]
        outs = run_attention_backward(
            after, through, x, dx1, da, h, q, k, v, stats, states, sums,
            segments, place, ga, dgf, w_query, w_key, w_value,
            back + entry[2:] if parts > 1 else (),
        )
        if turn < parts - 1:
            back = shifted(tuple(outs[3:]), -1)
    ffn.arrays[0], dx, keep, send = outs[:4]
    attention = Reduction(sum_planes(places, [(keep, send), (keep_out, send_out)]))
    ffn.step()
    ffn.arrays[0] = gate(ffn.arrays[0], output, mib=FFN_MIB)
    ffn.step()
    (total,) = ffn.arrays
    middle = total.shape[0] // 2
    sums = {
        "d": Reduction(sum_depth_and_gather(places, total[:middle])),
        "u": Reduction(sum_depth_and_gather(places, total[middle:])),
    }
    done = {}
    before = []
    for n, name in enumerate(TAIL):
        if name == "a" and "a" not in sums:
            sums["a"] = attention
            before = attention.turn(before)
        elif name == "A":
            attention.turn(before)
            sums["a"] = attention = Reduction(sum_depth_and_gather(places, attention.arrays[0]))
            before = attention.turn([])
        elif name in "DU":
            reduction = sums[name.lower()]
            reduction.step()
            done[name], finished = run_finish_ffn(core_ref, *reduction.arrays, name == "U")
            before = before + [finished]
        else:
            before = sums[name].turn(before)
        if n == SETTLE:
            output, arrived = settled(output)
            before = before + [arrived]
        if n == TRADE_AFTER:
            d_tokens = trade(gate(dx, *before))
        if n == TRADED:
            d_tokens, arrived = settled(d_tokens)
            before = before + [arrived]
    attention.step()
    dwd, dwu = done["D"], done["U"]
    own, other = attention.arrays
    half = dim // 2
    dwq, dwk, dwv, dwo = run_finish(
        core_ref, own, other, (0, half, 2 * half, 3 * half + GAIN_ROWS), (dim, dim)
    )
    at = 3 * dim // 2
    gains = jnp.where(core == 0, own[at : at + 2], other[at : at + 2]).astype(F32)
    return output, d_tokens, gains[0], gains[1], dwq, dwk, dwv, dwo, dwu, dwd


def solution(mesh):
    act = P("rows", "seq", None)
    return jax.shard_map(
        local,
        mesh=mesh,
        in_specs=(act, P("rows", None)) + (P(),) * 8 + (act,),
        out_specs=(act, act) + (P(),) * 8,
        check_vma=False,
    )
```

```python
import functools

import jax
import jax.numpy as jnp
from jax import lax
from jax.experimental import pallas as pl
from jax.experimental.pallas import tpu as pltpu
from jax.sharding import PartitionSpec as P

HEADS = 8
HEAD = 64
BAND = 30
EPSILON = 1e-06
SCALE = 0.125
CHUNK = 128
BLOCK = 256
PAIRS = HEADS // 2
NEG = -1e30
STEP_PAIRS = 2
GAIN_ROWS = 64
FLOPS_PER_US = 1000000000
TAIL = "duadudAuaduaaduaduDUa"
GATE_KIB = 512
SETTLE = 12
TRADE_AFTER = 12
TRADED = 18
FFN_ROWS = 1
FORWARD_MIB = 52
FFN_MIB = 50
ATTENTION_MIB = 54
GELU_A = 0.7978845608028654
GELU_B = 0.044715
F32 = jnp.float32
BF16 = jnp.bfloat16
VMEM_LIMIT = 56 * 1024 * 1024


def nn(a, b):
    return lax.dot_general(a, b, (((1,), (0,)), ((), ())), preferred_element_type=F32)


def nt(a, b):
    return lax.dot_general(a, b, (((1,), (1,)), ((), ())), preferred_element_type=F32)


def tn(a, b):
    return lax.dot_general(a, b, (((0,), (0,)), ((), ())), preferred_element_type=F32)


def low_lanes(shape):
    return lax.broadcasted_iota(jnp.int32, shape, len(shape) - 1) < HEAD


def split_heads(pair):
    low = low_lanes(pair.shape)
    zero = jnp.zeros_like(pair)
    return jnp.concatenate([jnp.where(low, pair, zero), jnp.where(low, zero, pair)], 0)


def pick(both):
    half = both.shape[0] // 2
    return jnp.where(low_lanes((half, both.shape[1])), both[:half], both[half:])


def over_lanes(column):
    half = column.shape[0] // 2
    return jnp.where(low_lanes((half, 2 * HEAD)), column[:half], column[half:])


def in_step(bodies):
    bodies = list(bodies)
    while bodies:
        bodies = [body for body in bodies if next(body, True) is None]


def features(t):
    expo = jnp.exp(jnp.minimum(t, 0.0))
    tanh = jnp.tanh(t)
    return (jnp.where(t > 0, t + 1.0, expo), 1.0 + tanh), (expo, 1.0 - tanh * tanh)


def head_mask(lanes):
    row = lax.broadcasted_iota(jnp.int32, (4 * HEAD, lanes), 0)
    lane = lax.broadcasted_iota(jnp.int32, (4 * HEAD, lanes), 1)
    head = (row // HEAD) % 2
    same = (lane < 2 * HEAD) & (lane // HEAD == head)
    return same | (lane == 2 * HEAD + row // HEAD)


def chunk_masks(seg_ref, place_ref, chunk):
    chunk = place_ref[1] + chunk

    def stretch(at):
        rows = seg_ref[:, pl.ds(pl.multiple_of(at * CHUNK, CHUNK), CHUNK)]
        mine = lax.broadcasted_iota(jnp.int32, rows.shape, 0) == place_ref[0]
        return jnp.max(jnp.where(mine, rows, -1), 0, keepdims=True).astype(F32)

    seg_own = stretch(chunk)
    seg_prev = jnp.where(chunk == 0, -1.0, stretch(jnp.maximum(chunk - 1, 0)))
    seg_q = jnp.broadcast_to(seg_own, (CHUNK, CHUNK)).T
    row = lax.broadcasted_iota(jnp.int32, (CHUNK, CHUNK), 0)
    col = lax.broadcasted_iota(jnp.int32, (CHUNK, CHUNK), 1)
    gap = row - col
    far = (seg_q == seg_own) & (gap >= 0)
    band_own = far & (gap <= BAND)
    band_prev = (seg_q == seg_prev) & (gap + CHUNK <= BAND)
    band = jnp.concatenate([band_prev, band_own], 1)
    before = seg_prev[:, CHUNK - 1 :]
    last = seg_own[:, CHUNK - 1 :]
    carry = (seg_q[:, :1] == before).astype(F32)
    tail = (seg_own == last).astype(BF16)
    keep = (before == last).astype(F32)
    return jnp.concatenate([band, band], 0), jnp.concatenate([far, far], 0), carry, tail, keep


def start_with(refs, entry_refs):
    for n, ref in enumerate(refs):
        ref[...] = entry_refs[n][...] if entry_refs else jnp.zeros_like(ref)


def forward_kernel(entries, *refs):
    (x_ref, seg_ref, place_ref, ga_ref, gf_ref, wq_ref, wk_ref, wv_ref, wo_ref, wu_ref, wd_ref,
     *refs) = refs
    entry_refs, refs = refs[:entries], refs[entries:]
    (out_ref, x1_ref, a_ref, h_ref, q_ref, k_ref, v_ref, stats_ref, states_ref, sums_ref,
     *refs) = refs
    end_refs, refs = refs[: min(entries, 2)], refs[min(entries, 2) :]
    s_ref, z_ref, kp_ref, vp_ref, wkt_ref, wvt_ref = refs
    step = pl.program_id(0)

    @pl.when(step == 0)
    def _():
        start_with((s_ref, z_ref, kp_ref, vp_ref), entry_refs)
        wkt_ref[...] = wk_ref[...].T
        wvt_ref[...] = wv_ref[...].T

    block = pl.ds(pl.multiple_of(step * BLOCK, BLOCK), BLOCK)
    x = x_ref[...].astype(F32)
    inv = lax.rsqrt(jnp.mean(x * x, -1, keepdims=True) + EPSILON)
    hidden = (x * inv * ga_ref[...]).astype(BF16)
    h_ref[...] = hidden
    q_ref[...] = nn(hidden, wq_ref[...]).astype(BF16)
    k_ref[...] = nt(wkt_ref[...], hidden).astype(BF16)
    v_ref[...] = nt(wvt_ref[...], hidden).astype(BF16)
    same_head = head_mask(CHUNK)
    for sub in range(BLOCK // CHUNK):
        chunk = step * (BLOCK // CHUNK) + sub
        rows = slice(sub * CHUNK, (sub + 1) * CHUNK)
        tokens = pl.ds(pl.multiple_of(chunk * CHUNK, CHUNK), CHUNK)
        band, far_mask, carry, tail, keep = chunk_masks(seg_ref, place_ref, chunk)
        tail_rows = jnp.broadcast_to(tail, (16, CHUNK))

        def body(p):
            lanes = slice(p * 128, (p + 1) * 128)
            qp = q_ref[rows, lanes]
            kt = k_ref[lanes, rows]
            vt = v_ref[lanes, rows]
            kt_ext = jnp.concatenate([kp_ref[lanes], kt], 1)
            vt_ext = jnp.concatenate([vp_ref[lanes], vt], 1)
            score = nn(split_heads(qp * SCALE), kt_ext)
            fq, _ = features(qp.astype(F32))
            fk, _ = features(kt.astype(F32))
            fk = [f.astype(BF16) for f in fk]
            fq = [f.astype(BF16) for f in fq]
            yield
            part = [
                jnp.where(far_mask, nn(split_heads(fq[m]), fk[m]), 0.0) for m in range(2)
            ]
            score = jnp.where(band, score, NEG)
            top = jnp.max(score, -1, keepdims=True)
            yield
            state = s_ref[p]
            state_low = state.astype(BF16)
            sums = z_ref[p]
            states_ref[sub, p] = state_low
            sums_ref[sub, p] = sums
            fk_both = jnp.concatenate(fk, 0)
            update = nt(fk_both * tail, vt)
            s_ref[p] = keep * state + jnp.where(same_head, update, 0.0)
            z_ref[p] = keep * sums + nt(tail_rows, fk_both)[:8]
            expo = jnp.exp(score - top)
            total = jnp.sum(expo, -1, keepdims=True)
            yield
            inv_total = 1.0 / total
            prob_prev = (expo[:, :CHUNK] * inv_total).astype(BF16)
            weight = expo[:, CHUNK:] * inv_total
            columns = [top + jnp.log(total)]
            scaled = []
            for m in range(2):
                fq_carry = fq[m].astype(F32) * carry
                entered = split_heads(fq_carry * sums[:1, m * 128 : (m + 1) * 128])
                inv_z = 1.0 / jnp.sum(part[m] + entered, -1, keepdims=True)
                columns.append(inv_z)
                weight = weight + part[m] * inv_z
                scaled.append((fq_carry * over_lanes(inv_z)).astype(BF16))
            both = jnp.concatenate([prob_prev, weight.astype(BF16)], 1)
            yield
            attended = pick(nt(both, vt_ext)) + nn(jnp.concatenate(scaled, 1), state_low)
            a_ref[tokens, lanes] = attended.astype(BF16)
            for n, column in enumerate(columns):
                stats_ref[sub, p, n] = jnp.broadcast_to(column, (2 * CHUNK, CHUNK))

        for first in range(0, PAIRS, STEP_PAIRS):
            in_step(body(p) for p in range(first, first + STEP_PAIRS))
        kp_ref[...] = k_ref[:, rows]
        vp_ref[...] = v_ref[:, rows]
    for end_ref, ref in zip(end_refs, (s_ref, z_ref)):
        end_ref[...] = ref[...]
    x1 = x + nn(a_ref[block], wo_ref[...])
    x1_ref[block] = x1
    inv = lax.rsqrt(jnp.mean(x1 * x1, -1, keepdims=True) + EPSILON)
    hidden = (x1 * inv * gf_ref[...]).astype(BF16)
    total = x1
    width = 512
    for f in range(wu_ref.shape[1] // width):
        cols = slice(f * width, (f + 1) * width)
        up = nn(hidden, wu_ref[:, cols])
        act = 0.5 * up * (1.0 + jnp.tanh(GELU_A * (up + GELU_B * up * up * up)))
        total = total + nn(act.astype(BF16), wd_ref[cols])
    out_ref[...] = total.astype(BF16)


def norm_backward(x, gain, grad):
    inv = lax.rsqrt(jnp.mean(x * x, -1, keepdims=True) + EPSILON)
    unit = x * inv
    scaled = grad * gain
    d_gain = jnp.sum(grad * unit, 0, keepdims=True)
    return inv * (scaled - unit * jnp.mean(unit * scaled, -1, keepdims=True)), d_gain


def ffn_backward_kernel(
    dy_ref, x1_ref, a_ref, gf_ref, wo_ref, wu_ref, wd_ref, core_ref,
    dx1_ref, da_ref, dg_ref, keep_ref, send_ref, keep_out_ref, send_out_ref,
    hidden_ref, dh_ref, dwd_ref, dwu_ref,
):
    step = pl.program_id(0)
    core = core_ref[0]
    gain = gf_ref[...]

    @pl.when(step == 0)
    def _():
        x1 = x1_ref[...]
        inv = lax.rsqrt(jnp.mean(x1 * x1, -1, keepdims=True) + EPSILON)
        hidden_ref[...] = (x1 * inv * gain).astype(BF16)
        dh_ref[...] = jnp.zeros_like(dh_ref)

    for part in range(FFN_ROWS):
        size = dy_ref.shape[0] // FFN_ROWS
        rows = slice(part * size, (part + 1) * size)
        dy = dy_ref[rows]
        hidden = hidden_ref[rows]
        up = nn(hidden, wu_ref[...])
        square = up * up
        tanh = jnp.tanh(GELU_A * up * (1.0 + GELU_B * square))
        half = 0.5 * (1.0 + tanh)
        act = (up * half).astype(BF16)
        slope = half + 0.5 * up * (1.0 - tanh * tanh) * (
            GELU_A + (3.0 * GELU_A * GELU_B) * square
        )
        d_up = (slope * nt(dy, wd_ref[...])).astype(BF16)
        dh_ref[rows] += nt(d_up, wu_ref[...])
        dwd, dwu = tn(act, dy), tn(hidden, d_up)
        if part:
            dwd, dwu = dwd + dwd_ref[...], dwu + dwu_ref[...]
        dwd_ref[...], dwu_ref[...] = dwd, dwu
    put_halves((dwd_ref, dwu_ref), core, keep_ref, send_ref)

    @pl.when(step == pl.num_programs(0) - 1)
    def _():
        x1 = x1_ref[...]
        d_norm, d_gain = norm_backward(x1, gain, dh_ref[...])
        dx1 = dy_ref[...].astype(F32) + d_norm
        dg_ref[...] = jnp.broadcast_to(d_gain, dg_ref.shape)
        dx1_ref[...] = dx1
        d_branch = dx1.astype(BF16)
        da_ref[...] = nt(d_branch, wo_ref[...]).astype(BF16)
        dwd_ref[...] = tn(a_ref[...], d_branch)
        put_halves((dwd_ref,), core, keep_out_ref, send_out_ref)


def put_halves(sums, core, keep_ref, send_ref):
    at = 0
    for total in sums:
        half = total.shape[0] // 2
        for ref, which in ((keep_ref, core), (send_ref, 1 - core)):
            rows = total[pl.ds(pl.multiple_of(which * half, half), half)]
            ref[at : at + half] = rows.astype(BF16)
        at += half
    return at


def attention_backward_kernel(entries, *refs):
    (x_ref, q_ref, h_ref, k_ref, v_ref, kprev_ref, vprev_ref, stats_ref, states_ref, sums_ref,
     da_ref, seg_ref, dx1_ref, place_ref, ga_ref, dgf_ref, wq_ref, wk_ref, wv_ref, *refs) = refs
    entry_refs, refs = refs[:entries], refs[entries:]
    dx_ref, keep_ref, send_ref, *refs = refs
    end_refs, refs = refs[: min(entries, 3)], refs[min(entries, 3) :]
    (r_ref, dkc_ref, dvc_ref, dq_ref, dk_ref, dv_ref, dwq_acc, dwk_acc, dwv_acc, dg_acc,
     wkt_ref, wvt_ref) = refs
    step = pl.program_id(0)
    block = pl.num_programs(0) - 1 - step

    @pl.when(step == 0)
    def _():
        start_with((r_ref, dkc_ref, dvc_ref), entry_refs)
        dwq_acc[...] = jnp.zeros_like(dwq_acc)
        dwk_acc[...] = jnp.zeros_like(dwk_acc)
        dwv_acc[...] = jnp.zeros_like(dwv_acc)
        dg_acc[...] = jnp.zeros_like(dg_acc)
        wkt_ref[...] = wk_ref[...].T
        wvt_ref[...] = wv_ref[...].T

    lane = lax.broadcasted_iota(jnp.int32, (CHUNK, CHUNK), 1)
    same_head = head_mask(2 * CHUNK)
    for sub in reversed(range(BLOCK // CHUNK)):
        chunk = block * (BLOCK // CHUNK) + sub
        rows = slice(sub * CHUNK, (sub + 1) * CHUNK)
        tokens = pl.ds(pl.multiple_of(chunk * CHUNK, CHUNK), CHUNK)
        band, far_mask, carry, tail, keep = chunk_masks(seg_ref, place_ref, chunk)
        tail_rows = jnp.broadcast_to(tail, (CHUNK, CHUNK))

        def body(p):
            lanes = slice(p * 128, (p + 1) * 128)
            qp = q_ref[rows, lanes]
            da = da_ref[tokens, lanes]
            kt = k_ref[lanes, rows]
            vt = v_ref[lanes, rows]
            if sub == 0:
                kt_prev, vt_prev = kprev_ref[lanes], vprev_ref[lanes]
                if entry_refs:
                    kt_prev = jnp.where(block == 0, entry_refs[3][lanes], kt_prev)
                    vt_prev = jnp.where(block == 0, entry_refs[4][lanes], vt_prev)
            else:
                before = slice((sub - 1) * CHUNK, sub * CHUNK)
                kt_prev, vt_prev = k_ref[lanes, before], v_ref[lanes, before]
            kt_ext = jnp.concatenate([kt_prev, kt], 1)
            vt_ext = jnp.concatenate([vt_prev, vt], 1)
            q2 = split_heads(qp * SCALE)
            da2 = split_heads(da)
            score = nn(q2, kt_ext)
            d_prob = nn(da2, vt_ext)
            yield
            state = states_ref[sub, p]
            sums = sums_ref[sub, p]
            back = r_ref[p]
            back_low = back.astype(BF16)
            from_state = nt(da, state) * carry
            to_later = nn(back_low, jnp.concatenate([vt * tail, tail_rows], 0))
            fq, slope_q = features(qp.astype(F32))
            fk, slope_k = features(kt.astype(F32))
            fk = [f.astype(BF16) for f in fk]
            fq = [f.astype(BF16) for f in fq]
            fq2 = [split_heads(f) for f in fq]
            yield
            part = [jnp.where(far_mask, nn(fq2[m], fk[m]), 0.0) for m in range(2)]
            lse = stats_ref[sub, p, 0]
            prob = jnp.exp(jnp.where(band, score - jnp.concatenate([lse, lse], 1), NEG))
            delta = jnp.sum(prob * d_prob, -1, keepdims=True)
            d_score = (prob * (d_prob - delta)).astype(BF16)
            yield
            dq = SCALE * pick(nt(d_score, kt_ext))
            dk_ext = tn(q2, d_score)
            dk = dk_ext[:, CHUNK:] + dkc_ref[lanes]
            dkc_ref[lanes] = dk_ext[:, :CHUNK]
            d_own = d_prob[:, CHUNK:]
            weight = prob[:, CHUNK:]
            yield
            scaled = []
            d_part = []
            entries = []
            right = jnp.zeros((CHUNK, CHUNK), F32)
            for m in range(2):
                part_lanes = slice(m * 128, (m + 1) * 128)
                fq_wide = fq[m].astype(F32)
                inv_z = stats_ref[sub, p, m + 1]
                weighted = part[m] * inv_z
                weight = weight + weighted
                entered = from_state[:, part_lanes]
                inv_wide = pick(inv_z)
                taken = fq_wide * inv_wide
                dot = jnp.sum(
                    weighted * d_own + split_heads(taken * entered), -1, keepdims=True
                )
                d_part.append(jnp.where(far_mask, (d_own - dot) * inv_z, 0.0).astype(BF16))
                entries.append(
                    inv_wide * (entered - over_lanes(dot) * (carry * sums[:1, part_lanes]))
                )
                scaled.append((taken * carry).astype(BF16))
                right = jnp.where(lane == 2 * m, -dot[:CHUNK], right)
                right = jnp.where(lane == 2 * m + 1, -dot[CHUNK:], right)
            both = jnp.concatenate([prob[:, :CHUNK].astype(BF16), weight.astype(BF16)], 1)
            yield
            dv_ext = tn(da2, both)
            dv = dv_ext[:, CHUNK:] + dvc_ref[lanes]
            dv = dv + tn(back_low[:, :CHUNK], jnp.concatenate(fk, 0) * tail)
            dvc_ref[lanes] = dv_ext[:, :CHUNK]
            update = tn(
                jnp.concatenate(scaled, 1), jnp.concatenate([da, right.astype(BF16)], 1)
            )
            r_ref[p] = keep * back + jnp.where(same_head, update, 0.0)
            dv_ref[lanes, rows] = dv.astype(BF16)
            yield
            for m in range(2):
                dq = dq + slope_q[m] * (pick(nt(d_part[m], fk[m])) + entries[m])
                dk = dk + slope_k[m] * (
                    tn(fq2[m], d_part[m]) + to_later[m * 128 : (m + 1) * 128]
                )
            dq_ref[rows, lanes] = dq.astype(BF16)
            dk_ref[lanes, rows] = dk.astype(BF16)

        for first in range(0, PAIRS, STEP_PAIRS):
            in_step(body(p) for p in range(first, first + STEP_PAIRS))
    for end_ref, ref in zip(end_refs, (r_ref, dkc_ref, dvc_ref)):
        end_ref[...] = ref[...]
    dim = x_ref.shape[1]
    tokens = pl.ds(pl.multiple_of(block * BLOCK, BLOCK), BLOCK)
    hidden_t = h_ref[...].T
    dq, dk, dv = dq_ref[...], dk_ref[...], dv_ref[...]
    dwq_acc[...] += nn(hidden_t, dq)
    dwk_acc[...] += nt(hidden_t, dk)
    dwv_acc[...] += nt(hidden_t, dv)
    d_hidden = nt(dq, wq_ref[...]) + tn(dk, wkt_ref[...]) + tn(dv, wvt_ref[...])
    d_norm, d_gain = norm_backward(x_ref[...].astype(F32), ga_ref[...], d_hidden)
    dg_acc[...] += jnp.broadcast_to(d_gain, dg_acc.shape)
    dx_ref[...] = (dx1_ref[tokens] + d_norm).astype(BF16)

    @pl.when(step == pl.num_programs(0) - 1)
    def _():
        core = place_ref[2]
        at = put_halves((dwq_acc, dwk_acc, dwv_acc), core, keep_ref, send_ref)
        keep_ref[at:] = jnp.zeros((GAIN_ROWS, keep_ref.shape[1]), BF16)
        send_ref[at:] = jnp.zeros((GAIN_ROWS, keep_ref.shape[1]), BF16)
        gains = jnp.concatenate([dg_acc[:1], dgf_ref[:1], jnp.zeros((14, dim), F32)], 0)
        keep_ref[at : at + 16] = jnp.where(core == 0, gains, 0.0).astype(BF16)
        send_ref[at : at + 16] = jnp.where(core == 0, 0.0, gains).astype(BF16)


HELD = pl.BlockSpec(memory_space=pltpu.VMEM)


def whole(shape):
    return pl.BlockSpec(shape, lambda i: (0,) * len(shape))


FFN_IN = HELD


def tokens_of(width, index=lambda i: i):
    return pl.BlockSpec((BLOCK, width), lambda i: (index(i), 0))


def of_chunks(shape, index=lambda i: i):
    return pl.BlockSpec((BLOCK // CHUNK,) + shape, lambda i: (index(i),) + (0,) * len(shape))


def work(micros):
    flops = int(micros * FLOPS_PER_US)
    return pl.CostEstimate(flops=flops, bytes_accessed=0, transcendentals=0)


def params(mib):
    return pltpu.CompilerParams(
        vmem_limit_bytes=mib * 1024 * 1024, dimension_semantics=("arbitrary",)
    )


def sds(shape, dtype):
    return jax.ShapeDtypeStruct(shape, dtype)


def run_forward(x, segments, place, gain_attn, gain_ffn, wq, wk, wv, wo, wu, wd, entry):
    length, dim = x.shape
    ff = wu.shape[1]
    chunks = length // CHUNK
    row = tokens_of(dim)
    column = pl.BlockSpec((dim, BLOCK), lambda i: (0, i))
    state_shape = (PAIRS, 4 * HEAD, 2 * HEAD)
    sum_shape = (PAIRS, 8, 4 * HEAD)
    stat_shape = (PAIRS, 3, 2 * CHUNK, CHUNK)
    ends = [(state_shape, F32), (sum_shape, F32)][: len(entry)]
    return pl.pallas_call(
        functools.partial(forward_kernel, len(entry)),
        grid=(length // BLOCK,),
        in_specs=[
            row, HELD, SMEM, HELD, HELD, HELD, HELD, HELD, HELD, HELD, HELD,
        ] + [whole(array.shape) for array in entry],
        out_specs=[
            row, HELD, HELD, row, row, column, column,
            of_chunks(stat_shape), of_chunks(state_shape), of_chunks(sum_shape),
        ] + [whole(shape) for shape, _ in ends],
        out_shape=[
            sds((length, dim), BF16), sds((length, dim), F32), sds((length, dim), BF16),
            sds((length, dim), BF16), sds((length, dim), BF16),
            sds((dim, length), BF16), sds((dim, length), BF16),
            sds((chunks,) + stat_shape, F32),
            sds((chunks,) + state_shape, BF16), sds((chunks,) + sum_shape, F32),
        ] + [sds(*end) for end in ends],
        scratch_shapes=[
            pltpu.VMEM(state_shape, F32), pltpu.VMEM(sum_shape, F32),
            pltpu.VMEM((dim, CHUNK), BF16), pltpu.VMEM((dim, CHUNK), BF16),
            pltpu.VMEM((dim, dim), BF16), pltpu.VMEM((dim, dim), BF16),
        ],
        compiler_params=params(FORWARD_MIB),
        cost_estimate=work(25),
        name="layer_forward",
    )(x, segments, place, gain_attn, gain_ffn, wq, wk, wv, wo, wu, wd, *entry)


SMEM = pl.BlockSpec(memory_space=pltpu.SMEM)
ANY = pl.BlockSpec(memory_space=pl.ANY)


def run_ffn_backward(dy, x1, a, gain_ffn, wo, wu, wd, core):
    length, dim = dy.shape
    ff = wu.shape[1]
    step_half = pl.BlockSpec((dim, dim), lambda i: (i, 0))
    return pl.pallas_call(
        ffn_backward_kernel,
        grid=(ff // dim,),
        in_specs=[
            FFN_IN, FFN_IN, FFN_IN, HELD, HELD,
            pl.BlockSpec((dim, dim), lambda i: (0, i)), step_half, SMEM,
        ],
        out_specs=[FFN_IN, FFN_IN, HELD, step_half, step_half, HELD, HELD],
        out_shape=[
            sds((length, dim), F32), sds((length, dim), BF16), sds((8, dim), F32),
            sds((ff, dim), BF16), sds((ff, dim), BF16),
            sds((dim // 2, dim), BF16), sds((dim // 2, dim), BF16),
        ],
        scratch_shapes=[
            pltpu.VMEM((length, dim), BF16), pltpu.VMEM((length, dim), F32),
            pltpu.VMEM((dim, dim), F32), pltpu.VMEM((dim, dim), F32),
        ],
        compiler_params=params(FFN_MIB),
        cost_estimate=work(20),
        name="ffn_backward",
    )(dy, x1, a, gain_ffn, wo, wu, wd, core)


def run_attention_backward(
    after, through, x, dx1, da, h, q, k, v, stats, states, sums, segments, place,
    gain_attn, dgf, wq, wk, wv, entry,
):
    length, dim = x.shape
    half = 3 * dim // 2 + GAIN_ROWS
    steps = length // BLOCK
    back = lambda i: steps - 1 - i
    row = tokens_of(dim, back)
    column = pl.BlockSpec((dim, BLOCK), lambda i: (0, back(i)))
    per = BLOCK // CHUNK
    prev = pl.BlockSpec((dim, CHUNK), lambda i: (0, jnp.maximum(back(i) * per - 1, 0)))
    streams = [of_chunks(array.shape[1:], back) for array in (stats, states, sums)]
    r_shape = (PAIRS, 4 * HEAD, 4 * HEAD)
    rim_shape = (dim, CHUNK)
    ends = [r_shape, rim_shape, rim_shape][: len(entry)]
    kernel = functools.partial(attention_backward_kernel, len(entry))
    skip = len(after) + len(through)
    streamed = [x, q, h, k, v, k, v, stats, states, sums]
    held = [da, segments, dx1, place, gain_attn, dgf, wq, wk, wv, *entry]
    inputs = skip + len(streamed) + len(held)

    def body(*refs):
        kernel(*refs[skip:inputs], *refs[inputs + len(through) :])

    return pl.pallas_call(
        body,
        grid=(steps,),
        input_output_aliases={len(after) + n: n for n in range(len(through))},
        in_specs=[ANY] * skip + [row, row, row, column, column, prev, prev] + streams
        + [SMEM if array is place else HELD for array in held],
        out_specs=[ANY] * len(through) + [row, HELD, HELD] + [whole(shape) for shape in ends],
        out_shape=[sds(array.shape, array.dtype) for array in through] + [
            sds((length, dim), BF16), sds((half, dim), BF16), sds((half, dim), BF16),
        ] + [sds(shape, F32) for shape in ends],
        scratch_shapes=[
            pltpu.VMEM(r_shape, F32), pltpu.VMEM(rim_shape, F32), pltpu.VMEM(rim_shape, F32),
            pltpu.VMEM((BLOCK, dim), BF16), pltpu.VMEM((dim, BLOCK), BF16),
            pltpu.VMEM((dim, BLOCK), BF16),
            pltpu.VMEM((dim, dim), F32), pltpu.VMEM((dim, dim), F32), pltpu.VMEM((dim, dim), F32),
            pltpu.VMEM((8, dim), F32),
            pltpu.VMEM((dim, dim), BF16), pltpu.VMEM((dim, dim), BF16),
        ],
        compiler_params=params(ATTENTION_MIB),
        cost_estimate=work(29),
        name="attention_backward",
    )(*after, *through, *streamed, *held)


def finish_ffn_kernel(core_ref, own_ref, other_ref, out_ref, done_ref):
    half = out_ref.shape[0] // 2
    for ref, which in ((own_ref, core_ref[0]), (other_ref, 1 - core_ref[0])):
        rows = pl.ds(pl.multiple_of(which * half, half), half)
        out_ref[rows] = ref[...].astype(F32)
    done_ref[...] = jnp.zeros_like(done_ref)


def run_finish_ffn(core_ref, own, other, across):
    dim = own.shape[1]
    ff = own.shape[0] * 2
    block = pl.BlockSpec((dim // 2, dim), lambda i: (i, 0))
    return pl.pallas_call(
        finish_ffn_kernel,
        grid=(ff // dim,),
        in_specs=[SMEM, block, block],
        out_specs=[
            pl.BlockSpec((dim, dim), (lambda i: (0, i)) if across else (lambda i: (i, 0))),
            whole((8, 128)),
        ],
        out_shape=[sds((dim, ff) if across else (ff, dim), F32), sds((8, 128), F32)],
        compiler_params=params(12),
        name="finish_ffn",
    )(core_ref, own, other)


def finish_kernel(starts, core_ref, own_ref, other_ref, *out_refs):
    for at, out_ref in zip(starts, out_refs):
        half = out_ref.shape[0] // 2
        for ref, which in ((own_ref, core_ref[0]), (other_ref, 1 - core_ref[0])):
            rows = pl.ds(pl.multiple_of(which * half, half), half)
            out_ref[rows] = ref[at : at + half].astype(F32)


def run_finish(core_ref, own, other, starts, shape):
    return pl.pallas_call(
        functools.partial(finish_kernel, starts),
        in_specs=[SMEM, HELD, HELD],
        out_specs=[HELD] * len(starts),
        out_shape=[sds(shape, F32)] * len(starts),
        compiler_params=pltpu.CompilerParams(vmem_limit_bytes=12 * 1024 * 1024),
        name="finish",
    )(core_ref, own, other)


def partner(array, seq_bits, row_bits):
    seq_count, row_groups = lax.axis_size("seq"), lax.axis_size("rows")
    pairs = [
        (s * row_groups + r, (s ^ seq_bits) * row_groups + (r ^ row_bits))
        for s in range(seq_count)
        for r in range(row_groups)
    ]
    return lax.ppermute(array, ("seq", "rows"), pairs)


def add(*parts):
    parts = [part.astype(F32) for part in parts]
    if len(parts) == 4:
        return ((parts[0] + parts[1]) + (parts[2] + parts[3])).astype(BF16)
    return (parts[0] + parts[1]).astype(BF16)


def take(array, index, size):
    return lax.dynamic_slice_in_dim(array, index * size, size, 0)


PLANE_BITS = ((1, 0), (0, 2), (1, 2))
DEPTH_BITS = (2, 4)


def cut(total, place):
    size = total.shape[0] // 4
    return [take(total, place ^ d, size) for d in range(4)]


def traded(parts, all_bits):
    return [parts[0]] + [partner(part, *bits) for part, bits in zip(parts[1:], all_bits)]


def cut_half(total, bit):
    size = total.shape[0] // 2
    return [take(total, bit, size), take(total, 1 - bit, size)]


def joined_half(own, other, bit):
    return jnp.where(bit == 0, jnp.concatenate([own, other], 0), jnp.concatenate([other, own], 0))


def joined(parts, place):
    blocks = jnp.stack(parts)
    blocks = [lax.dynamic_index_in_dim(blocks, place ^ d, 0, False) for d in range(4)]
    return jnp.concatenate(blocks, 0)


def sum_planes(places, halves):
    core, plane, depth = places
    others = [partner(send, 0, 1) for _, send in halves]
    keeps = yield [keep for keep, _ in halves]
    sums = [add(keep, other) for keep, other in zip(keeps, others)]
    parts = yield cut(jnp.concatenate(sums, 0) if len(sums) > 1 else sums[0], plane)
    parts = traded(parts, PLANE_BITS)
    parts = yield parts
    yield [add(*parts)]


def sum_depth_and_gather(places, total):
    core, plane, depth = places
    (total,) = yield [total]
    for n, (bits, bit) in enumerate(zip(DEPTH_BITS, depth)):
        keep, send = yield cut_half(total, bit)
        other = partner(send, bits, 0)
        keep, other = yield [keep, other]
        total = add(keep, other)
    for bits in further_bits():
        total = add(total, partner(total, *bits))
    for bits, bit in reversed(list(zip(DEPTH_BITS, depth))):
        (total,) = yield [total]
        other = partner(total, bits, 0)
        total, other = yield [total, other]
        total = joined_half(total, other, bit)
    (block,) = yield [total]
    parts = traded([block] * 4, PLANE_BITS)
    parts = yield parts
    (own,) = yield [joined(parts, plane)]
    yield [own, partner(own, 0, 1)]


def gate(array, *others, mib=None):
    return pl.pallas_call(
        lambda *refs: None,
        in_specs=[ANY] * (1 + len(others)),
        out_specs=ANY,
        out_shape=sds(array.shape, array.dtype),
        input_output_aliases={0: 0},
        compiler_params=pltpu.CompilerParams(vmem_limit_bytes=mib * 2**20 if mib else GATE_KIB * 1024),
        name="gate",
    )(array, *others)


def settled(array):
    def kernel(in_ref, out_ref, done_ref):
        out_ref[...] = in_ref[...]
        done_ref[...] = jnp.zeros_like(done_ref)

    block = pl.BlockSpec((1,) + array.shape[1:], lambda i: (i, 0, 0))
    return pl.pallas_call(
        kernel,
        grid=(array.shape[0],),
        in_specs=[block],
        out_specs=[block, whole((8, 128))],
        out_shape=[sds(array.shape, array.dtype), sds((8, 128), F32)],
        compiler_params=params(2),
        name="settled",
    )(array)


class Reduction:
    def __init__(self, steps):
        self.steps = steps
        self.arrays = next(steps)
        self.waits = False

    def step(self):
        self.arrays = self.steps.send(self.arrays)

    def turn(self, before):
        if self.waits:
            self.step()
        if before:
            self.arrays[0] = gate(self.arrays[0], *before)
        self.step()
        self.waits = True
        return self.arrays[1:] or self.arrays


def further_bits():
    bits = []
    bit = 8
    while bit < lax.axis_size("seq"):
        bits.append((bit, 0))
        bit *= 2
    bit = 4
    while bit < lax.axis_size("rows"):
        bits.append((0, bit))
        bit *= 2
    return bits


def all_reduce_small(small):
    small = small + partner(small, 0, 1)
    for bits in (((1, 0), (0, 2), (1, 2)), ((2, 0), (4, 0), (6, 0))):
        got = [small] + [partner(small, *b) for b in bits]
        small = (got[0] + got[1]) + (got[2] + got[3])
    for b in further_bits():
        small = small + partner(small, *b)
    return small


def local(
    tokens, segments, gain_attn, gain_ffn, w_query, w_key, w_value, w_out, w_up, w_down, cotangent
):
    row_count, shard_len, dim = tokens.shape
    seq_count = lax.axis_size("seq")
    parts = seq_count // row_count
    groups = [[g * row_count + r for r in range(row_count)] for g in range(parts)]
    length = row_count * shard_len
    index = lax.axis_index("seq")
    my_row = index % row_count
    my_part = index // row_count

    def trade(array):
        return lax.all_to_all(
            array.reshape(row_count, shard_len, dim), "seq", 0, 0, axis_index_groups=groups
        )

    def shifted(arrays, by):
        pairs = [
            (i, i + by * row_count)
            for i in range(seq_count)
            if 0 <= i + by * row_count < seq_count
        ]
        return lax.ppermute(arrays, "seq", pairs)

    ga, gf = gain_attn.reshape(1, dim), gain_ffn.reshape(1, dim)
    seq_index, row_index = lax.axis_index("seq"), lax.axis_index("rows")
    core, plane = row_index % 2, seq_index % 2 + 2 * (row_index // 2 % 2)
    places = core, plane, (seq_index // 2 % 2, seq_index // 4 % 2)
    place = jnp.stack([my_row, my_part * (length // CHUNK), core]).astype(jnp.int32)

    x = trade(tokens).reshape(length, dim)
    dy = trade(cotangent).reshape(length, dim)
    entry = ()
    if parts > 1:
        rim_zero = jnp.zeros((dim, CHUNK), BF16)
        entry = (
            jnp.zeros((PAIRS, 4 * HEAD, 2 * HEAD), F32), jnp.zeros((PAIRS, 8, 4 * HEAD), F32),
            rim_zero, rim_zero,
        )
    for turn in range(parts):
        out, x1, a, h, q, k, v, stats, states, sums, *ends = run_forward(
            x, segments, place, ga, gf, w_query, w_key, w_value, w_out, w_up, w_down, entry
        )
        if turn < parts - 1:
            entry = shifted((*ends, k[:, length - CHUNK :], v[:, length - CHUNK :]), 1)
    output = trade(out)
    core_ref = place[2:]
    dx1, da, dgf, keep, send, keep_out, send_out = run_ffn_backward(
        dy, x1, a, gf, w_out, w_up, w_down, core_ref
    )
    ffn = Reduction(sum_planes(places, [(keep, send)]))
    ffn.step()
    back = ()
    if parts > 1:
        rim = jnp.zeros((dim, CHUNK), F32)
        back = (jnp.zeros((PAIRS, 4 * HEAD, 4 * HEAD), F32), rim, rim)
    for turn in range(parts):
        through, after = [], []
        if turn == parts - 1:
            through, after = ffn.arrays[:1], ffn.arrays[1:]
        outs = run_attention_backward(
            after, through, x, dx1, da, h, q, k, v, stats, states, sums,
            segments, place, ga, dgf, w_query, w_key, w_value,
            back + entry[2:] if parts > 1 else (),
        )
        if turn < parts - 1:
            back = shifted(tuple(outs[3:]), -1)
    ffn.arrays[0], dx, keep, send = outs[:4]
    attention = Reduction(sum_planes(places, [(keep, send), (keep_out, send_out)]))
    ffn.step()
    ffn.arrays[0] = gate(ffn.arrays[0], output, mib=FFN_MIB)
    ffn.step()
    (total,) = ffn.arrays
    middle = total.shape[0] // 2
    sums = {
        "d": Reduction(sum_depth_and_gather(places, total[:middle])),
        "u": Reduction(sum_depth_and_gather(places, total[middle:])),
    }
    done = {}
    before = []
    for n, name in enumerate(TAIL):
        if name == "a" and "a" not in sums:
            sums["a"] = attention
            before = attention.turn(before)
        elif name == "A":
            attention.turn(before)
            sums["a"] = attention = Reduction(sum_depth_and_gather(places, attention.arrays[0]))
            before = attention.turn([])
        elif name in "DU":
            reduction = sums[name.lower()]
            reduction.step()
            done[name], finished = run_finish_ffn(core_ref, *reduction.arrays, name == "U")
            before = before + [finished]
        else:
            before = sums[name].turn(before)
        if n == SETTLE:
            output, arrived = settled(output)
            before = before + [arrived]
        if n == TRADE_AFTER:
            d_tokens = trade(gate(dx, *before))
        if n == TRADED:
            d_tokens, arrived = settled(d_tokens)
            before = before + [arrived]
    attention.step()
    dwd, dwu = done["D"], done["U"]
    own, other = attention.arrays
    half = dim // 2
    dwq, dwk, dwv, dwo = run_finish(
        core_ref, own, other, (0, half, 2 * half, 3 * half + GAIN_ROWS), (dim, dim)
    )
    at = 3 * dim // 2
    gains = jnp.where(core == 0, own[at : at + 2], other[at : at + 2]).astype(F32)
    return output, d_tokens, gains[0], gains[1], dwq, dwk, dwv, dwo, dwu, dwd


def solution(mesh):
    act = P("rows", "seq", None)
    return jax.shard_map(
        local,
        mesh=mesh,
        in_specs=(act, P("rows", None)) + (P(),) * 8 + (act,),
        out_specs=(act, act) + (P(),) * 8,
        check_vma=False,
    )
```
